32 devices in a mesh: rep: 4 (over x, core), shard: 8 (over z, y).
Axes of the slice: x: 2, y: 2, z: 4, core: 2. Of those that a mesh axis runs over, the one named last changes fastest.
Arguments:
- hidden_acts: bfloat16 [24576, 128], P(('rep', 'shard')), may hold values from -6 to 6
- out_cotangent: bfloat16 [24576, 4096], P(('rep', 'shard')), may hold values from -0.0390625 to 0.0390625
- weight: bfloat16 [128, 4096], P('shard'), may hold values from -6 to 6
- first_moment: float32 [128, 4096], P('shard'), may hold values from -6 to 6
- second_moment: float32 [128, 4096], P('shard'), may hold values from 0.05 to 2
Outputs:
- new_weight: bfloat16 [128, 4096], replicated
- new_first: float32 [128, 4096], P('shard')
- new_second: float32 [128, 4096], P('shard')
The draws below stay inside these ranges and needn't reach their ends.
All inputs are finite; a program needn't handle non-finite values.
Results may differ from the reference program's by a relative error of at most 0.0014.
Values may be sent and summed in bfloat16 or wider, within the bound.
No kernel may reach another device: no remote copies, remote signals or barrier semaphores. Data moves between devices by JAX's collectives and lax.ppermute only.
A program may use at most 128 MiB of HBM per device.

```python
import math
import jax
import jax.numpy as jnp
from jax import lax

D = 4096
TOK = 768
R = 128
TOKENS = 24576


def strengthened(drawn, stream_key, source, target, blocks, factor):
    owner, partner = [(jnp.arange(drawn.shape[axis_at]) // (drawn.shape[axis_at] // blocks)).reshape([-1 if axis == axis_at else 1 for axis in range(drawn.ndim)]) for axis_at in (source, target)]
    chosen = jax.random.permutation(stream_key, blocks)[partner]
    strong = (owner == chosen) | (owner == (partner + blocks // 2) % blocks)
    return jnp.where(strong, factor * drawn, drawn)


def steps_of(rng, shape, pieces, low, high):
    factor_of = 1.0
    for axis_at, blocks in pieces:
        heights = jax.random.uniform(jax.random.fold_in(jax.random.fold_in(rng, 6), axis_at), (blocks,), jnp.float32, low / len(pieces), high / len(pieces))
        factor_of = factor_of * jnp.repeat(jnp.exp(heights), shape[axis_at] // blocks).reshape((-1,) + (1,) * (len(shape) - 1 - axis_at))
    return factor_of


def gaussian(stream_key, dims, spread, limit, split=(), kind=jnp.bfloat16):
    level = steps_of(stream_key, dims, split, -0.22, 0.18) if split else 1.0
    result = jax.random.normal(stream_key, dims, jnp.float32) * spread * level
    return jnp.minimum(jnp.maximum(result, -limit), limit).astype(kind)


def heavy_noise(stream_key, shape, width, reach, pieces, heavy, kind=jnp.bfloat16):
    entries = width * jax.random.normal(stream_key, shape, jnp.float32)
    if pieces:
        entries = entries * steps_of(stream_key, shape, pieces, -0.22, 0.18)
    return jnp.clip(strengthened(entries, jax.random.fold_in(stream_key, 3), *heavy), -reach, reach).astype(kind)


def setup_inputs(seed: int = 0) -> dict:
    seeds = jax.random.split(jax.random.key(seed), 6)
    return {
        "hidden_acts": heavy_noise(seeds[0], (TOKENS, R), 1.0, 6.0, ((0, 32),), (0, 1, 32, 2.75)),
        "out_cotangent": gaussian(seeds[1], (TOKENS, D), TOKENS ** -0.5, 0.0390625, ((0, 32),)),
        "weight": gaussian(seeds[2], (R, D), 1.0, 6.0, ((0, 8),)),
        "first_moment": gaussian(seeds[3], (R, D), 1.0, 6.0, ((0, 8),), jnp.float32),
        "second_moment": jnp.clip(jnp.exp(math.log(2.0) - 3.6888794 * jax.random.uniform(seeds[4], (R, D), jnp.float32) ** steps_of(seeds[4], (R, D), ((0, 8),), -0.2, 0.2)), 0.05, 2.0),
    }


def adamw(weight, first_moment, second_moment, grad):
    corr_one = 0.9999734386011124
    corr_two = 0.0952078528
    new_first = 0.9 * first_moment + 0.1 * grad
    new_second = 0.999 * second_moment + 0.001 * grad * grad
    wfloat = weight.astype(jnp.float32)
    update = new_first / corr_one / (jnp.sqrt(new_second / corr_two) + 1e-08)
    new_weight = (wfloat - 0.05 * (update + 0.1 * wfloat)).astype(jnp.bfloat16)
    return (new_weight, new_first, new_second)

def reference(hidden_acts, out_cotangent, weight, first_moment, second_moment):
    blocks = TOKENS // TOK

    def step(index, total):
        acts = lax.dynamic_slice_in_dim(hidden_acts, index * TOK, TOK, 0).astype(jnp.float32)
        cots = lax.dynamic_slice_in_dim(out_cotangent, index * TOK, TOK, 0).astype(jnp.float32)
        return total + jnp.dot(acts.T, cots, preferred_element_type=jnp.float32)
    grad = lax.fori_loop(0, blocks, step, jnp.zeros((R, D), jnp.float32))
    return adamw(weight, first_moment, second_moment, grad)
```

```python
import functools

import jax
import jax.numpy as jnp
from jax import lax
from jax.experimental import pallas as pl
from jax.experimental.pallas import tpu as pltpu
from jax.sharding import PartitionSpec as P

F32 = jnp.float32
BF16 = jnp.bfloat16


def adamw_moments(first_moment, second_moment, grad):
    new_first = 0.9 * first_moment + 0.1 * grad
    new_second = 0.999 * second_moment + 0.001 * grad * grad
    return new_first, new_second


def adamw_weight(weight, new_first, new_second):
    corr_one = 0.9999734386011124
    corr_two = 0.0952078528
    wfloat = weight.astype(F32)
    update = new_first / corr_one / (jnp.sqrt(new_second / corr_two) + 1e-08)
    return (wfloat - 0.05 * (update + 0.1 * wfloat)).astype(BF16)


def contract(acts, cots):
    return lax.dot_general(acts, cots, (((0,), (0,)), ((), ())), preferred_element_type=F32)


def in_vmem(kernel, out_shapes, *args):
    spec = pl.BlockSpec(memory_space=pltpu.VMEM)
    return pl.pallas_call(
        kernel,
        out_shape=out_shapes,
        in_specs=[spec] * len(args),
        out_specs=jax.tree.map(lambda _: spec, out_shapes),
        compiler_params=pltpu.CompilerParams(vmem_limit_bytes=48 * 1024 * 1024),
    )(*args)


def shape(dims, kind):
    return jax.ShapeDtypeStruct(dims, kind)


def split_kernel(rows, kept_ref, came_ref, own_ref, *piece_refs):
    me = lax.axis_index("shard")
    for k in range(len(piece_refs) + 1):
        at = pl.ds(pl.multiple_of((me ^ k) * rows, rows), rows)
        total = kept_ref[at, :] + came_ref[at, :].astype(F32)
        if k == 0:
            own_ref[...] = total
        else:
            piece_refs[k - 1][...] = total.astype(BF16)


def place(index):
    bits = lax.axis_size("rep").bit_length() - 1
    return sum(((index >> bit) & 1) << (bits - 1 - bit) for bit in range(bits))


def update_kernel(w_ref, m_ref, v_ref, own_ref, *refs):
    piece_refs, (new_w_ref, grad_ref) = refs[:-2], refs[-2:]
    me = lax.axis_index("rep")
    total = own_ref[...]
    for ref in piece_refs:
        total += ref[...].astype(F32)
    cols = total.shape[1]
    at = pl.ds(pl.multiple_of(place(me) * cols, cols), cols)
    sent = total.astype(BF16)
    new_m, new_v = adamw_moments(m_ref[:, at], v_ref[:, at], sent.astype(F32))
    new_w_ref[...] = adamw_weight(w_ref[:, at], new_m, new_v)
    grad_ref[...] = sent


def moments_kernel(m_ref, v_ref, *refs):
    grad_refs, (new_m_ref, new_v_ref) = refs[:-2], refs[-2:]
    me = lax.axis_index("rep")
    for k, ref in enumerate(grad_refs):
        cols = ref.shape[1]
        at = pl.ds(pl.multiple_of(place(me ^ k) * cols, cols), cols)
        new_m_ref[:, at], new_v_ref[:, at] = adamw_moments(m_ref[:, at], v_ref[:, at], ref[...].astype(F32))


def rows_kernel(*refs):
    piece_refs, out_ref = refs[:-1], refs[-1]
    me = lax.axis_index("shard")
    for k, ref in enumerate(piece_refs):
        rows = ref.shape[0]
        out_ref[pl.ds(pl.multiple_of((me ^ k) * rows, rows), rows), :] = ref[...]


def columns_kernel(bit, low_ref, high_ref, out_ref):
    mine = (lax.axis_index("rep") >> bit) & 1
    cols = low_ref.shape[1]
    out_ref[:, pl.ds(pl.multiple_of(mine * cols, cols), cols)] = low_ref[...]
    out_ref[:, pl.ds(pl.multiple_of((1 - mine) * cols, cols), cols)] = high_ref[...]


def swap(value, axis, k):
    return lax.ppermute(value, axis, [(i, i ^ k) for i in range(lax.axis_size(axis))])


def body(hidden_acts, out_cotangent, weight, first_moment, second_moment):
    rows_dev, width = weight.shape
    rep_count = lax.axis_size("rep")
    shard_count = lax.axis_size("shard")
    all_rows = hidden_acts.shape[1]
    bits = rep_count.bit_length() - 1
    rep = lax.axis_index("rep")

    half = width // 2
    mine = rep & 1
    cut = lambda value, index, size: lax.dynamic_slice_in_dim(value, index * size, size, 1)
    away = contract(hidden_acts, cut(out_cotangent, 1 - mine, half)).astype(BF16)
    came = swap(away, "rep", 1)
    kept = contract(hidden_acts, cut(out_cotangent, mine, half))
    for bit in range(1, bits):
        total = kept + came.astype(F32)
        half //= 2
        mine = (rep >> bit) & 1
        came = swap(cut(total, 1 - mine, half).astype(BF16), "rep", 1 << bit)
        kept = cut(total, mine, half)

    cols = half
    own, *pieces = in_vmem(
        functools.partial(split_kernel, rows_dev),
        [shape((rows_dev, cols), F32)] + [shape((rows_dev, cols), BF16)] * (shard_count - 1),
        kept, came,
    )
    pieces = [swap(piece, "shard", k + 1) for k, piece in enumerate(pieces)]
    new_w, grad = in_vmem(
        update_kernel,
        [shape((rows_dev, cols), BF16)] * 2,
        weight, first_moment, second_moment, own, *pieces,
    )
    w_pieces = [new_w] + [swap(new_w, "shard", k) for k in range(1, shard_count)]
    grads = [grad] + [swap(grad, "rep", k) for k in range(1, rep_count)]
    part = in_vmem(rows_kernel, shape((all_rows, cols), BF16), *w_pieces)
    for bit in reversed(range(bits)):
        other = swap(part, "rep", 1 << bit)
        part = in_vmem(
            functools.partial(columns_kernel, bit),
            shape((all_rows, 2 * part.shape[1]), BF16), part, other,
        )
    new_m, new_v = in_vmem(
        moments_kernel,
        [shape((rows_dev, width), F32)] * 2,
        first_moment, second_moment, *grads,
    )
    return part, new_m, new_v


def solution(mesh):
    return jax.shard_map(
        body,
        mesh=mesh,
        in_specs=(
            P(("rep", "shard"), None),
            P(("rep", "shard"), None),
            P("shard", None),
            P("shard", None),
            P("shard", None),
        ),
        out_specs=(P(), P("shard", None), P("shard", None)),
        check_vma=False,
    )
```

```python
import functools

import jax
import jax.numpy as jnp
from jax import lax
from jax.experimental import pallas as pl
from jax.experimental.pallas import tpu as pltpu
from jax.sharding import PartitionSpec as P

F32 = jnp.float32
BF16 = jnp.bfloat16
CHUNK = 512


def adamw_moments(first_moment, second_moment, grad):
    new_first = 0.9 * first_moment + 0.1 * grad
    new_second = 0.999 * second_moment + 0.001 * grad * grad
    return new_first, new_second


def adamw_weight(weight, new_first, new_second):
    corr_one = 0.9999734386011124
    corr_two = 0.0952078528
    wfloat = weight.astype(F32)
    update = new_first / corr_one / (jnp.sqrt(new_second / corr_two) + 1e-08)
    return (wfloat - 0.05 * (update + 0.1 * wfloat)).astype(BF16)


def shape(dims, kind):
    return jax.ShapeDtypeStruct(dims, kind)


def call(kernel, outs, *args, far_in=(), far_out=False, scratch=(), aliases=None):
    near, far = pl.BlockSpec(memory_space=pltpu.VMEM), pl.BlockSpec(memory_space=pltpu.HBM)
    return pl.pallas_call(
        kernel,
        out_shape=outs,
        in_specs=[far if i in far_in else near for i in range(len(args))],
        out_specs=[far if far_out else near for _ in outs],
        scratch_shapes=scratch,
        input_output_aliases=aliases or {},
        compiler_params=pltpu.CompilerParams(vmem_limit_bytes=48 * 1024 * 1024),
    )(*args)


def swap(value, axis, k):
    return lax.ppermute(value, axis, [(i, i ^ k) for i in range(lax.axis_size(axis))])


def place():
    rep, shard = lax.axis_index("rep"), lax.axis_index("shard")
    return rep & 1, rep >> 1, shard & 1, shard >> 1


def block(index, size):
    return pl.ds(pl.multiple_of(index * size, size), size)


def contract_kernel(away, acts_ref, cots_ref, out_ref, acts, cots, sems):
    core = place()[0]
    half = 1 - core if away else core
    count = cots.shape[0]
    copies = [pltpu.make_async_copy(acts_ref, acts, sems.at[count])]
    for i in range(count):
        source = cots_ref.at[:, block(half * count + i, CHUNK)]
        copies.append(pltpu.make_async_copy(source, cots.at[i], sems.at[i]))
    for copy in copies:
        copy.start()
    copies[0].wait()
    turned = acts[...].T
    for i in range(count):
        copies[i + 1].wait()
        term = jnp.dot(turned, cots[i], preferred_element_type=F32)
        out_ref[:, i * CHUNK:(i + 1) * CHUNK] = term.astype(out_ref.dtype)


def contract(away, acts, cots, kind):
    tokens, rows = acts.shape
    half = cots.shape[1] // 2
    count = half // CHUNK
    return call(
        functools.partial(contract_kernel, away),
        [shape((rows, half), kind)], acts, cots, far_in=(0, 1),
        scratch=[
            pltpu.VMEM((tokens, rows), BF16),
            pltpu.VMEM((count, tokens, CHUNK), BF16),
            pltpu.SemaphoreType.DMA((count + 1,)),
        ],
    )[0]


def first_kernel(rows, kept, came, a_keep, a_send, b_keep, b_send):
    _, x, y, _ = place()
    quarter = a_keep.shape[1]
    for out, side in ((a_keep, x), (a_send, 1 - x)):
        at = block(side, quarter)
        out[...] = (kept[:, at] + came[:, at].astype(F32)).astype(out.dtype)
    for out, side in ((b_keep, y), (b_send, 1 - y)):
        for z in range(out.shape[0] // rows):
            at = block(2 * z + side, rows)
            total = kept[at, 2 * quarter:] + came[at, 2 * quarter:].astype(F32)
            out[z * rows:(z + 1) * rows, :] = total.astype(out.dtype)


def second_a_kernel(rows, kept, came, keep, send):
    _, _, y, _ = place()
    for out, side in ((keep, y), (send, 1 - y)):
        for z in range(out.shape[0] // rows):
            at = block(2 * z + side, rows)
            out[z * rows:(z + 1) * rows, :] = (kept[at, :] + came[at, :].astype(F32)).astype(out.dtype)


def second_b_kernel(kept, came, keep, send):
    _, x, _, _ = place()
    for out, side in ((keep, x), (send, 1 - x)):
        at = block(side, out.shape[1])
        out[...] = (kept[:, at] + came[:, at].astype(F32)).astype(out.dtype)


def third_kernel(a_kept, a_came, b_kept, b_came, *pieces):
    z = place()[3]
    rows, quarter = pieces[0].shape[0], a_kept.shape[1]
    for k, out in enumerate(pieces):
        at = block(z ^ k, rows)
        out[:, :quarter] = (a_kept[at, :] + a_came[at, :].astype(F32)).astype(out.dtype)
        out[:, quarter:] = (b_kept[at, :] + b_came[at, :].astype(F32)).astype(out.dtype)


def update_kernel(w, m, v, own, *refs):
    pieces, (new_w, grad) = refs[:-2], refs[-2:]
    core, x, _, _ = place()
    total = own[...]
    for ref in pieces:
        total += ref[...].astype(F32)
    grad[...] = total.astype(BF16)
    quarter = total.shape[1] // 2
    for part in range(2):
        mine = slice(part * quarter, (part + 1) * quarter)
        at = block(core * 4 + part * 2 + x, quarter)
        new_m, new_v = adamw_moments(m[:, at], v[:, at], total[:, mine])
        new_w[:, mine] = adamw_weight(w[:, at], new_m, new_v)


def pack_kernel(grad, *refs):
    pieces, (a_out, b_out) = refs[:-2], refs[-2:]
    z = place()[3]
    rows, quarter = grad.shape[0], a_out.shape[1]
    for k, ref in enumerate(pieces):
        at = block(z ^ k, rows)
        a_out[at, :] = ref[:, :quarter]
        b_out[at, :] = ref[:, quarter:]
    tail = a_out.shape[0]
    b_out[tail:tail + rows, :] = grad[:, :quarter]
    b_out[tail + rows:tail + 2 * rows, :] = grad[:, quarter:]


def join_a_kernel(rows, mine, other, out):
    y = place()[2]
    for ref, side in ((mine, y), (other, 1 - y)):
        for z in range(ref.shape[0] // rows):
            out[block(2 * z + side, rows), :] = ref[z * rows:(z + 1) * rows, :]


def join_b_kernel(mine, other, out):
    x = place()[1]
    for ref, side in ((mine, x), (other, 1 - x)):
        out[:, block(side, ref.shape[1])] = ref[:out.shape[0], :]


def half_kernel(rows, a_mine, a_other, b_mine, b_other, g_mine, g_other, out):
    _, x, y, _ = place()
    all_rows, quarter = a_mine.shape
    tail = b_mine.shape[0]
    for ref, grad, side in ((a_mine, g_mine, x), (a_other, g_other, 1 - x)):
        out[:all_rows, block(side, quarter)] = ref[...]
        out[all_rows:, block(side, quarter)] = grad[tail:tail + rows, :]
        out[all_rows:, block(2 + side, quarter)] = grad[tail + rows:, :]
    for ref, side in ((b_mine, y), (b_other, 1 - y)):
        for z in range(tail // rows):
            out[block(2 * z + side, rows), 2 * quarter:] = ref[z * rows:(z + 1) * rows, :]


def write_kernel(away, part, m, v, *refs):
    w_out, m_out, v_out, new_m, new_v, sems = refs[-6:]
    core = place()[0]
    all_rows, half = w_out.shape[0], part.shape[1]
    at = block(1 - core if away else core, half)
    copies = [pltpu.make_async_copy(part.at[pl.ds(0, all_rows), :], w_out.at[:, at], sems.at[0])]
    copies[0].start()
    new_m[...], new_v[...] = adamw_moments(m[:, at], v[:, at], part[all_rows:, :].astype(F32))
    for i, (source, out) in enumerate(((new_m, m_out), (new_v, v_out))):
        copies.append(pltpu.make_async_copy(source, out.at[:, at], sems.at[i + 1]))
        copies[-1].start()
    for copy in copies:
        copy.wait()


def body(hidden_acts, out_cotangent, weight, first_moment, second_moment):
    rows, width = weight.shape
    shard_count = lax.axis_size("shard")
    all_rows = hidden_acts.shape[1]
    some_rows, levels = all_rows // 2, shard_count // 2
    half, quarter = width // 2, width // 8

    came = swap(contract(True, hidden_acts, out_cotangent, BF16), "rep", 1)
    kept = contract(False, hidden_acts, out_cotangent, F32)

    a_keep, a_send, b_keep, b_send = call(
        functools.partial(first_kernel, rows),
        [shape((all_rows, quarter), F32), shape((all_rows, quarter), BF16),
         shape((some_rows, 2 * quarter), F32), shape((some_rows, 2 * quarter), BF16)],
        kept, came,
    )
    a_came, b_came = swap(a_send, "rep", 2), swap(b_send, "shard", 1)
    sizes = [shape((some_rows, quarter), F32), shape((some_rows, quarter), BF16)]
    a_keep, a_send = call(functools.partial(second_a_kernel, rows), sizes, a_keep, a_came)
    b_keep, b_send = call(second_b_kernel, sizes, b_keep, b_came)
    a_came, b_came = swap(a_send, "shard", 1), swap(b_send, "rep", 2)
    own, *pieces = call(
        third_kernel,
        [shape((rows, 2 * quarter), F32)] + [shape((rows, 2 * quarter), BF16)] * (levels - 1),
        a_keep, a_came, b_keep, b_came,
    )
    pieces = [swap(piece, "shard", 2 * (k + 1)) for k, piece in enumerate(pieces)]
    new_w, grad = call(
        update_kernel, [shape((rows, 2 * quarter), BF16)] * 2,
        weight, first_moment, second_moment, own, *pieces,
    )

    pieces = [new_w] + [swap(new_w, "shard", 2 * k) for k in range(1, levels)]
    a_part, b_part = call(
        pack_kernel,
        [shape((some_rows, quarter), BF16), shape((some_rows + 2 * rows, quarter), BF16)],
        grad, *pieces,
    )
    a_other, g_other = swap(a_part, "shard", 1), swap(b_part, "rep", 2)
    a_mine = call(functools.partial(join_a_kernel, rows), [shape((all_rows, quarter), BF16)], a_part, a_other)[0]
    b_mine = call(join_b_kernel, [shape((some_rows, 2 * quarter), BF16)], b_part, g_other)[0]
    a_other, b_other = swap(a_mine, "rep", 2), swap(b_mine, "shard", 1)
    part = call(
        functools.partial(half_kernel, rows), [shape((all_rows + rows, half), BF16)],
        a_mine, a_other, b_mine, b_other, b_part, g_other,
    )[0]
    other = swap(part, "rep", 1)
    results = [shape((all_rows, width), BF16), shape((rows, width), F32), shape((rows, width), F32)]
    scratch = [pltpu.VMEM((rows, half), F32), pltpu.VMEM((rows, half), F32), pltpu.SemaphoreType.DMA((3,))]
    written = call(
        functools.partial(write_kernel, False), results,
        part, first_moment, second_moment, far_out=True, scratch=scratch,
    )
    return tuple(call(
        functools.partial(write_kernel, True), results,
        other, first_moment, second_moment, *written,
        far_in=(3, 4, 5), far_out=True, scratch=scratch, aliases={3: 0, 4: 1, 5: 2},
    ))


def solution(mesh):
    return jax.shard_map(
        body,
        mesh=mesh,
        in_specs=(
            P(("rep", "shard"), None),
            P(("rep", "shard"), None),
            P("shard", None),
            P("shard", None),
            P("shard", None),
        ),
        out_specs=(P(), P("shard", None), P("shard", None)),
        check_vma=False,
    )
```

```python
import functools

import jax
import jax.numpy as jnp
from jax import lax
from jax.experimental import pallas as pl
from jax.experimental.pallas import tpu as pltpu
from jax.sharding import PartitionSpec as P

F32 = jnp.float32
BF16 = jnp.bfloat16
CHUNK = 512


def adamw_moments(first_moment, second_moment, grad):
    new_first = 0.9 * first_moment + 0.1 * grad
    new_second = 0.999 * second_moment + 0.001 * grad * grad
    return new_first, new_second


def adamw_weight(weight, new_first, new_second):
    corr_one = 0.9999734386011124
    corr_two = 0.0952078528
    wfloat = weight.astype(F32)
    update = new_first / corr_one / (jnp.sqrt(new_second / corr_two) + 1e-08)
    return (wfloat - 0.05 * (update + 0.1 * wfloat)).astype(BF16)


def shape(dims, kind):
    return jax.ShapeDtypeStruct(dims, kind)


def call(kernel, outs, *args, far_in=(), far_out=False, scratch=(), aliases=None):
    near, far = pl.BlockSpec(memory_space=pltpu.VMEM), pl.BlockSpec(memory_space=pltpu.HBM)
    return pl.pallas_call(
        kernel,
        out_shape=outs,
        in_specs=[far if i in far_in else near for i in range(len(args))],
        out_specs=[far if far_out else near for _ in outs],
        scratch_shapes=scratch,
        input_output_aliases=aliases or {},
        compiler_params=pltpu.CompilerParams(vmem_limit_bytes=48 * 1024 * 1024),
    )(*args)


def swap(value, axis, k):
    return lax.ppermute(value, axis, [(i, i ^ k) for i in range(lax.axis_size(axis))])


def place():
    rep, shard = lax.axis_index("rep"), lax.axis_index("shard")
    return rep & 1, rep >> 1, shard & 1, shard >> 1


def block(index, size):
    return pl.ds(pl.multiple_of(index * size, size), size)


def contract_kernel(away, acts_ref, cots_ref, out_ref, acts, cots, sems):
    core = place()[0]
    half = 1 - core if away else core
    count = cots.shape[0]
    copies = [pltpu.make_async_copy(acts_ref, acts, sems.at[count])]
    for i in range(count):
        source = cots_ref.at[:, block(half * count + i, CHUNK)]
        copies.append(pltpu.make_async_copy(source, cots.at[i], sems.at[i]))
    for copy in copies:
        copy.start()
    copies[0].wait()
    turned = acts[...].T
    for i in range(count):
        copies[i + 1].wait()
        term = jnp.dot(turned, cots[i], preferred_element_type=F32)
        out_ref[:, i * CHUNK:(i + 1) * CHUNK] = term.astype(out_ref.dtype)


def contract(away, acts, cots, kind):
    tokens, rows = acts.shape
    half = cots.shape[1] // 2
    count = half // CHUNK
    return call(
        functools.partial(contract_kernel, away),
        [shape((rows, half), kind)], acts, cots, far_in=(0, 1),
        scratch=[
            pltpu.VMEM((tokens, rows), BF16),
            pltpu.VMEM((count, tokens, CHUNK), BF16),
            pltpu.SemaphoreType.DMA((count + 1,)),
        ],
    )[0]


def split_kernel(kept, came, keep, send):
    x = place()[1]
    for out, side in ((keep, x), (send, 1 - x)):
        at = block(side, out.shape[1])
        out[...] = (kept[:, at] + came[:, at].astype(F32)).astype(out.dtype)


def sum_kernel(kept, came, send):
    send[...] = (kept[...] + came[...].astype(F32)).astype(BF16)


def update_kernel(w, m, v, kept, came, pieces, new_w, grad):
    core, x, _, _ = place()
    rows, quarter = grad.shape
    mine = block(lax.axis_index("shard"), rows)
    total = kept[mine, :] + came[mine, :].astype(F32)
    total -= (total.astype(BF16)).astype(F32)
    for k in range(pieces.shape[0] // rows):
        total += pieces[k * rows:(k + 1) * rows, :].astype(F32)
    grad[...] = total.astype(BF16)
    at = block(core * 2 + x, quarter)
    new_m, new_v = adamw_moments(m[:, at], v[:, at], total)
    fresh = adamw_weight(w[:, at], new_m, new_v)
    for k in range(new_w.shape[0] // rows):
        new_w[k * rows:(k + 1) * rows, :] = fresh


def pack_kernel(weights, grad, out):
    all_rows = weights.shape[0]
    out[:all_rows, :] = weights[...]
    out[all_rows:, :] = grad[...]


def join_kernel(mine, other, out):
    x = place()[1]
    for ref, side in ((mine, x), (other, 1 - x)):
        out[:, block(side, ref.shape[1])] = ref[...]


def write_kernel(away, part, m, v, *refs):
    w_out, m_out, v_out, new_m, new_v, sems = refs[-6:]
    core = place()[0]
    all_rows, half = w_out.shape[0], part.shape[1]
    at = block(1 - core if away else core, half)
    copies = [pltpu.make_async_copy(part.at[pl.ds(0, all_rows), :], w_out.at[:, at], sems.at[0])]
    copies[0].start()
    new_m[...], new_v[...] = adamw_moments(m[:, at], v[:, at], part[all_rows:, :].astype(F32))
    for i, (source, out) in enumerate(((new_m, m_out), (new_v, v_out))):
        copies.append(pltpu.make_async_copy(source, out.at[:, at], sems.at[i + 1]))
        copies[-1].start()
    for copy in copies:
        copy.wait()


def body(hidden_acts, out_cotangent, weight, first_moment, second_moment):
    rows, width = weight.shape
    all_rows = hidden_acts.shape[1]
    half, quarter = width // 2, width // 4

    came = swap(contract(True, hidden_acts, out_cotangent, BF16), "rep", 1)
    kept = contract(False, hidden_acts, out_cotangent, F32)

    keep, send = call(
        split_kernel, [shape((all_rows, quarter), F32), shape((all_rows, quarter), BF16)], kept, came,
    )
    came = swap(send, "rep", 2)
    send = call(sum_kernel, [shape((all_rows, quarter), BF16)], keep, came)[0]
    pieces = lax.all_to_all(send, "shard", 0, 0, tiled=True)
    new_w, grad = call(
        update_kernel, [shape((all_rows, quarter), BF16), shape((rows, quarter), BF16)],
        weight, first_moment, second_moment, keep, came, pieces,
    )
    gathered = lax.all_to_all(new_w, "shard", 0, 0, tiled=True)
    part = call(pack_kernel, [shape((all_rows + rows, quarter), BF16)], gathered, grad)[0]
    part = call(join_kernel, [shape((all_rows + rows, half), BF16)], part, swap(part, "rep", 2))[0]
    other = swap(part, "rep", 1)
    results = [shape((all_rows, width), BF16), shape((rows, width), F32), shape((rows, width), F32)]
    scratch = [pltpu.VMEM((rows, half), F32), pltpu.VMEM((rows, half), F32), pltpu.SemaphoreType.DMA((3,))]
    written = call(
        functools.partial(write_kernel, False), results,
        part, first_moment, second_moment, far_out=True, scratch=scratch,
    )
    return tuple(call(
        functools.partial(write_kernel, True), results,
        other, first_moment, second_moment, *written,
        far_in=(3, 4, 5), far_out=True, scratch=scratch, aliases={3: 0, 4: 1, 5: 2},
    ))


def solution(mesh):
    return jax.shard_map(
        body,
        mesh=mesh,
        in_specs=(
            P(("rep", "shard"), None),
            P(("rep", "shard"), None),
            P("shard", None),
            P("shard", None),
            P("shard", None),
        ),
        out_specs=(P(), P("shard", None), P("shard", None)),
        check_vma=False,
    )
```

```python
import functools

import jax
import jax.numpy as jnp
from jax import lax
from jax.experimental import pallas as pl
from jax.experimental.pallas import tpu as pltpu
from jax.sharding import PartitionSpec as P

F32 = jnp.float32
BF16 = jnp.bfloat16
CHUNK = 512
LOAD_LIMIT = 48 * 1024 * 1024


def adamw_moments(first_moment, second_moment, grad):
    new_first = 0.9 * first_moment + 0.1 * grad
    new_second = 0.999 * second_moment + 0.001 * grad * grad
    return new_first, new_second


def adamw_weight(weight, new_first, new_second):
    corr_one = 0.9999734386011124
    corr_two = 0.0952078528
    wfloat = weight.astype(F32)
    update = new_first / corr_one / (jnp.sqrt(new_second / corr_two) + 1e-08)
    return (wfloat - 0.05 * (update + 0.1 * wfloat)).astype(BF16)


def shape(dims, kind):
    return jax.ShapeDtypeStruct(dims, kind)


def call(kernel, outs, *args, far_in=(), far_out=0, scratch=(), aliases=None, limit=48 * 1024 * 1024):
    near, far = pl.BlockSpec(memory_space=pltpu.VMEM), pl.BlockSpec(memory_space=pltpu.HBM)
    return pl.pallas_call(
        kernel,
        out_shape=outs,
        in_specs=[far if i in far_in else near for i in range(len(args))],
        out_specs=[far if i < far_out else near for i in range(len(outs))],
        scratch_shapes=scratch,
        input_output_aliases=aliases or {},
        compiler_params=pltpu.CompilerParams(vmem_limit_bytes=limit),
    )(*args)


def exchange(value, other):
    reps, shards = lax.axis_size("rep"), lax.axis_size("shard")
    pairs = []
    for rep in range(reps):
        for shard in range(shards):
            to_rep, to_shard = other(rep, shard)
            pairs.append((rep * shards + shard, to_rep * shards + to_shard))
    return lax.ppermute(value, ("rep", "shard"), pairs)


def to_sibling(value):
    return exchange(value, lambda rep, shard: (rep ^ 1, shard))


def first_way(value):
    return exchange(value, lambda rep, shard: (rep, shard ^ 1) if rep & 1 else (rep ^ 2, shard))


def second_way(value):
    return exchange(value, lambda rep, shard: (rep ^ 2, shard) if rep & 1 else (rep, shard ^ 1))


def along_z(value, k):
    return exchange(value, lambda rep, shard: (rep, shard ^ (2 * k)))


def far_first(levels):
    return [k for k in range(levels - 1, 0, -1)]


def place():
    rep, shard = lax.axis_index("rep"), lax.axis_index("shard")
    return rep & 1, rep >> 1, shard & 1, shard >> 1


def block(index, size):
    return pl.ds(pl.multiple_of(index * size, size), size)


def pair(kept):
    core, x, y, _ = place()
    x, y = (x, y) if kept else (1 - x, 1 - y)
    return [(jnp.where(core == 0, j, y), jnp.where(core == 0, x, j)) for j in range(2)]


def chosen():
    core, x, y, _ = place()
    return jnp.where(core == 0, y, x)


def load_kernel(acts_ref, cots_ref, out, turned, kept_cots, acts, cots, sems):
    core = place()[0]
    count = cots.shape[0]
    copies = [pltpu.make_async_copy(acts_ref, acts, sems.at[count])]
    for i in range(count):
        source = cots_ref.at[:, block((1 - core) * count + i, CHUNK)]
        copies.append(pltpu.make_async_copy(source, cots.at[i], sems.at[i]))
    own = cots_ref.at[:, block(core, kept_cots.shape[1])]
    copies.append(pltpu.make_async_copy(own, kept_cots, sems.at[count + 1]))
    for copy in copies:
        copy.start()
    copies[0].wait()
    turned[...] = acts[...].T
    for i in range(count):
        copies[i + 1].wait()
        term = jnp.dot(turned[...], cots[i], preferred_element_type=F32)
        out[:, i * CHUNK:(i + 1) * CHUNK] = term.astype(out.dtype)
    copies[-1].wait()


def product_kernel(turned, cots, out):
    for i in range(out.shape[1] // CHUNK):
        at = slice(i * CHUNK, (i + 1) * CHUNK)
        out[:, at] = jnp.dot(turned[...], cots[:, at], preferred_element_type=F32)


def first_kernel(rows, kept, came, keep, send):
    some_rows, quarter = keep.shape[0] // 2, keep.shape[1]
    for out, sides in ((keep, pair(True)), (send, pair(False))):
        for j, (y, x) in enumerate(sides):
            cols = block(x, quarter)
            for z in range(some_rows // rows):
                at = block(2 * z + y, rows)
                total = kept[at, cols] + came[at, cols].astype(F32)
                out[j * some_rows + z * rows:j * some_rows + (z + 1) * rows, :] = total.astype(out.dtype)


def second_kernel(kept, came, keep, send):
    mine = chosen()
    for out, side in ((keep, mine), (send, 1 - mine)):
        at = block(side, out.shape[0])
        out[...] = (kept[at, :] + came[at, :].astype(F32)).astype(out.dtype)


def third_kernel(steps, kept, came, own, *pieces):
    z = place()[3]
    for k, out in zip([0] + steps, (own,) + pieces):
        at = block(z ^ k, out.shape[0])
        out[...] = (kept[at, :] + came[at, :].astype(F32)).astype(out.dtype)


def update_kernel(w, m, v, own, *refs):
    pieces, (new_w, grad) = refs[:-2], refs[-2:]
    core, x, _, _ = place()
    total = own[...]
    for ref in pieces:
        total += ref[...].astype(F32)
    grad[...] = total.astype(BF16)
    at = block(core * 2 + x, total.shape[1])
    new_m, new_v = adamw_moments(m[:, at], v[:, at], total)
    new_w[...] = adamw_weight(w[:, at], new_m, new_v)


def pack_kernel(steps, grad, *refs):
    pieces, out = refs[:-1], refs[-1]
    z = place()[3]
    rows = grad.shape[0]
    for k, ref in zip([0] + steps, pieces):
        out[block(z ^ k, rows), :] = ref[...]
    out[out.shape[0] - rows:, :] = grad[...]


def join_kernel(rows, mine, other, out):
    some_rows = mine.shape[0] - rows
    out[block(chosen(), some_rows), :] = mine[:some_rows, :]
    out[block(1 - chosen(), some_rows), :] = other[:some_rows, :]
    out[2 * some_rows:, :] = mine[some_rows:, :]


def rest_kernel(rows, late, early, _, out):
    core = place()[0]
    tail = out.shape[0] - rows
    out[:tail, :] = late[:tail, :]

    @pl.when(core == 0)
    def _():
        out[tail:, :] = late[tail:, :]

    @pl.when(core != 0)
    def _():
        out[tail:, :] = early[early.shape[0] - rows:, :]


def write_kernel(pieces, m, v, *refs):
    parts = refs[:len(pieces)]
    w_out, m_out, v_out, after, new_m, new_v, sems = refs[-7:]
    core, near_x, near_y, _ = place()
    rows, quarter = new_m.shape[1:]
    copies, targets = [], []

    def send(source, out):
        copies.append(pltpu.make_async_copy(source, out, sems.at[len(copies)]))
        copies[-1].start()

    for part, (sibling, kept) in zip(parts, pieces):
        side = 1 - core if sibling else core
        x, y = (near_x, near_y) if kept else (1 - near_x, 1 - near_y)
        targets.append(block(2 * side + x, quarter))
        some_rows = (part.shape[0] - rows) // 2
        for j in range(2):
            to_y, to_x = jnp.where(side == 0, j, y), jnp.where(side == 0, x, j)
            for z in range(some_rows // rows):
                source = part.at[pl.ds(j * some_rows + z * rows, rows), :]
                send(source, w_out.at[block(2 * z + to_y, rows), block(2 * side + to_x, quarter)])
    for i, (part, at) in enumerate(zip(parts, targets)):
        grad = part[part.shape[0] - rows:, :].astype(F32)
        new_m[i], new_v[i] = adamw_moments(m[:, at], v[:, at], grad)
        send(new_m.at[i], m_out.at[:, at])
        send(new_v.at[i], v_out.at[:, at])
    after[...] = jnp.zeros_like(after)
    for copy in copies:
        copy.wait()


def write(pieces, parts, m, v, outs, written=()):
    rows, quarter = m.shape[0], m.shape[1] // 4
    count = len(parts)
    copies = count * ((parts[0].shape[0] - rows) // rows + 2)
    first = 2 + count
    return call(
        functools.partial(write_kernel, pieces), outs + [shape((8, 128), F32)], m, v, *parts, *written,
        far_in=range(first, first + len(written)), far_out=len(outs),
        scratch=[
            pltpu.VMEM((count, rows, quarter), F32),
            pltpu.VMEM((count, rows, quarter), F32),
            pltpu.SemaphoreType.DMA((copies,)),
        ],
        aliases={first + i: i for i in range(len(written))},
    )


def body(hidden_acts, out_cotangent, weight, first_moment, second_moment):
    rows, width = weight.shape
    tokens, all_rows = hidden_acts.shape
    some_rows, levels = all_rows // 2, lax.axis_size("shard") // 2
    half, quarter = width // 2, width // 4
    count = half // CHUNK
    steps = far_first(levels)

    away, turned, cots = call(
        load_kernel,
        [shape((all_rows, half), BF16), shape((all_rows, tokens), BF16), shape((tokens, half), BF16)],
        hidden_acts, out_cotangent, far_in=(0, 1),
        scratch=[
            pltpu.VMEM((tokens, all_rows), BF16),
            pltpu.VMEM((count, tokens, CHUNK), BF16),
            pltpu.SemaphoreType.DMA((count + 2,)),
        ],
        limit=LOAD_LIMIT,
    )
    came = to_sibling(away)
    kept = call(product_kernel, [shape((all_rows, half), F32)], turned, cots)[0]

    keep, send = call(
        functools.partial(first_kernel, rows),
        [shape((all_rows, quarter), F32), shape((all_rows, quarter), BF16)], kept, came,
    )
    keep, send = call(
        second_kernel,
        [shape((some_rows, quarter), F32), shape((some_rows, quarter), BF16)], keep, first_way(send),
    )
    own, *pieces = call(
        functools.partial(third_kernel, steps),
        [shape((rows, quarter), F32)] + [shape((rows, quarter), BF16)] * (levels - 1), keep, second_way(send),
    )
    pieces = [along_z(piece, k) for k, piece in zip(steps, pieces)]
    new_w, grad = call(
        update_kernel, [shape((rows, quarter), BF16)] * 2,
        weight, first_moment, second_moment, own, *pieces,
    )

    pieces = [new_w] + [along_z(new_w, k) for k in steps]
    mine = call(
        functools.partial(pack_kernel, steps), [shape((some_rows + rows, quarter), BF16)], grad, *pieces,
    )[0]
    early = second_way(mine)
    mine = call(functools.partial(join_kernel, rows), [shape((all_rows + rows, quarter), BF16)], mine, early)[0]
    late = first_way(mine)
    results = [shape((all_rows, width), BF16), shape((rows, width), F32), shape((rows, width), F32)]
    *outs, after = write([(False, True)], [mine], first_moment, second_moment, results)
    other = to_sibling(mine)
    rest = call(
        functools.partial(rest_kernel, rows), [shape((all_rows + rows, quarter), BF16)], late, early, after,
    )[0]
    last = to_sibling(rest)
    *outs, _ = write([(False, False), (True, True)], [rest, other], first_moment, second_moment, results, outs)
    return tuple(write([(True, False)], [last], first_moment, second_moment, results, outs)[:3])


def solution(mesh):
    return jax.shard_map(
        body,
        mesh=mesh,
        in_specs=(
            P(("rep", "shard"), None),
            P(("rep", "shard"), None),
            P("shard", None),
            P("shard", None),
            P("shard", None),
        ),
        out_specs=(P(), P("shard", None), P("shard", None)),
        check_vma=False,
    )
```

```python
import functools

import jax
import jax.numpy as jnp
from jax import lax
from jax.experimental import pallas as pl
from jax.experimental.pallas import tpu as pltpu
from jax.sharding import PartitionSpec as P

F32 = jnp.float32
BF16 = jnp.bfloat16
CHUNK = 512
LOAD_LIMIT = 48 * 1024 * 1024


def adamw_moments(first_moment, second_moment, grad):
    new_first = 0.9 * first_moment + 0.1 * grad
    new_second = 0.999 * second_moment + 0.001 * grad * grad
    return new_first, new_second


def adamw_weight(weight, new_first, new_second):
    corr_one = 0.9999734386011124
    corr_two = 0.0952078528
    wfloat = weight.astype(F32)
    update = new_first / corr_one / (jnp.sqrt(new_second / corr_two) + 1e-08)
    return (wfloat - 0.05 * (update + 0.1 * wfloat)).astype(BF16)


def shape(dims, kind):
    return jax.ShapeDtypeStruct(dims, kind)


def call(kernel, outs, *args, far_in=(), far_out=0, scratch=(), aliases=None, limit=48 * 1024 * 1024):
    near, far = pl.BlockSpec(memory_space=pltpu.VMEM), pl.BlockSpec(memory_space=pltpu.HBM)
    return pl.pallas_call(
        kernel,
        out_shape=outs,
        in_specs=[far if i in far_in else near for i in range(len(args))],
        out_specs=[far if i < far_out else near for i in range(len(outs))],
        scratch_shapes=scratch,
        input_output_aliases=aliases or {},
        compiler_params=pltpu.CompilerParams(vmem_limit_bytes=limit),
    )(*args)


def between(value, step):
    reps, shards = lax.axis_size("rep"), lax.axis_size("shard")
    pairs = []
    for rep in range(1, reps, 2):
        for shard in range(shards):
            to_rep, to_shard = step(rep, shard)
            pairs.append((rep * shards + shard, to_rep * shards + to_shard))
    return lax.ppermute(value, ("rep", "shard"), pairs)


def along_x(value):
    return between(value, lambda rep, shard: (rep ^ 2, shard))


def along_y(value):
    return between(value, lambda rep, shard: (rep, shard ^ 1))


def along_z(value, k):
    return between(value, lambda rep, shard: (rep, shard ^ (2 * k)))


def to_core(core, value):
    return lax.ppermute(value, "rep", [(rep ^ 1, rep) for rep in range(core, lax.axis_size("rep"), 2)])


def far_first(levels):
    return [k for k in range(levels - 1, 0, -1)]


def place():
    rep, shard = lax.axis_index("rep"), lax.axis_index("shard")
    return rep & 1, rep >> 1, shard & 1, shard >> 1


def block(index, size):
    return pl.ds(pl.multiple_of(index * size, size), size)


def load_kernel(acts_ref, cots_ref, sent, kept, turned, cots_b, acts, cots, sems):
    count = cots.shape[0]
    copies = [pltpu.make_async_copy(acts_ref, acts, sems.at[count])]
    for i in range(count):
        source = cots_ref.at[:, pl.ds(i * CHUNK, CHUNK)]
        copies.append(pltpu.make_async_copy(source, cots.at[i], sems.at[i]))
    rest = cots_ref.at[:, pl.ds(count * CHUNK, cots_b.shape[1])]
    copies.append(pltpu.make_async_copy(rest, cots_b, sems.at[count + 1]))
    for copy in copies:
        copy.start()
    copies[0].wait()
    turned[...] = acts[...].T
    for i in range(count):
        copies[i + 1].wait()
        at = slice(i * CHUNK, (i + 1) * CHUNK)
        term = jnp.dot(turned[...], cots[i], preferred_element_type=F32)
        kept[:, at] = term
        sent[:, at] = term.astype(BF16)
    copies[-1].wait()


def product_kernel(turned, cots, sent, kept):
    for i in range(kept.shape[1] // CHUNK):
        at = slice(i * CHUNK, (i + 1) * CHUNK)
        term = jnp.dot(turned[...], cots[:, at], preferred_element_type=F32)
        kept[:, at] = term
        sent[:, at] = term.astype(BF16)


def by_x_kernel(kept, came, keep, send):
    x = place()[1]
    for out, side in ((keep, x), (send, 1 - x)):
        at = block(side, out.shape[1])
        out[...] = (kept[:, at] + came[:, at].astype(F32)).astype(out.dtype)


def by_y_kernel(rows, kept, came, keep, send):
    y = place()[2]
    for out, side in ((keep, y), (send, 1 - y)):
        for z in range(out.shape[0] // rows):
            at = block(2 * z + side, rows)
            out[z * rows:(z + 1) * rows, :] = (kept[at, :] + came[at, :].astype(F32)).astype(out.dtype)


def by_z_kernel(steps, a_kept, a_came, b_kept, b_came, own, *pieces):
    z = place()[3]
    rows, quarter = own.shape[0], a_kept.shape[1]
    for k, out in zip([0] + steps, (own,) + pieces):
        at = block(z ^ k, rows)
        out[:, :quarter] = (a_kept[at, :] + a_came[at, :].astype(F32)).astype(out.dtype)
        out[:, quarter:] = (b_kept[at, :] + b_came[at, :].astype(F32)).astype(out.dtype)


def update_kernel(w, m, v, own, *refs):
    pieces, (new_w, grad) = refs[:-2], refs[-2:]
    x = place()[1]
    total = own[...]
    for ref in pieces:
        total += ref[...].astype(F32)
    grad[...] = total.astype(BF16)
    quarter = total.shape[1] // 2
    for part in range(2):
        mine = slice(part * quarter, (part + 1) * quarter)
        at = block(2 * part + x, quarter)
        new_m, new_v = adamw_moments(m[:, at], v[:, at], total[:, mine])
        new_w[:, mine] = adamw_weight(w[:, at], new_m, new_v)


def pack_kernel(steps, grad, *refs):
    pieces, (a_out, b_out) = refs[:-2], refs[-2:]
    z = place()[3]
    rows, quarter = grad.shape[0], a_out.shape[1]
    for k, ref in zip([0] + steps, pieces):
        at = block(z ^ k, rows)
        a_out[at, :] = ref[:, :quarter]
        b_out[at, :] = ref[:, quarter:]
    tail = a_out.shape[0]
    b_out[tail:tail + rows, :] = grad[:, :quarter]
    b_out[tail + rows:tail + 2 * rows, :] = grad[:, quarter:]


def join_y_kernel(rows, mine, other, out):
    y = place()[2]
    for ref, side in ((mine, y), (other, 1 - y)):
        for z in range(ref.shape[0] // rows):
            out[block(2 * z + side, rows), :] = ref[z * rows:(z + 1) * rows, :]


def join_x_kernel(mine, other, out, grads):
    x = place()[1]
    some_rows, rows = out.shape[0], grads.shape[0]
    for ref, side in ((mine, x), (other, 1 - x)):
        out[:, block(side, ref.shape[1])] = ref[:some_rows, :]
        for part in range(2):
            at = pl.ds(some_rows + part * rows, rows)
            grads[:, block(2 * part + side, ref.shape[1])] = ref[at, :]


def either(core, own, got, action):
    @pl.when(core == 1)
    def _():
        action(own)

    @pl.when(core != 1)
    def _():
        action(got)


def write_a(kept, sems, copies, own, got, w_out):
    core, x, _, _ = place()
    at = block(x if kept else 1 - x, own.shape[1])
    either(core, own, got, lambda ref: pltpu.make_async_copy(ref, w_out.at[:, at], sems.at[len(copies)]).start())
    copies.append(pltpu.make_async_copy(own, w_out.at[:, at], sems.at[len(copies)]))


def write_b(kept, rows, sems, copies, own, got, w_out):
    core, _, y, _ = place()
    width = own.shape[1]
    for z in range(own.shape[0] // rows):
        target = w_out.at[block(2 * z + (y if kept else 1 - y), rows), pl.ds(width, width)]
        sem = sems.at[len(copies)]
        at = pl.ds(z * rows, rows)
        either(core, own, got, lambda ref: pltpu.make_async_copy(ref.at[at, :], target, sem).start())
        copies.append(pltpu.make_async_copy(own.at[at, :], target, sem))


def write_first_kernel(m, v, a, a_got, b, b_got, g, g_got, w_out, m_out, v_out, after, new_m, new_v, sems):
    copies = []
    write_a(True, sems, copies, a, a_got, w_out)
    write_b(True, m.shape[0], sems, copies, b, b_got, w_out)

    def moments(ref):
        new_m[...], new_v[...] = adamw_moments(m[...], v[...], ref[...].astype(F32))

    either(place()[0], g, g_got, moments)
    for source, out in ((new_m, m_out), (new_v, v_out)):
        copies.append(pltpu.make_async_copy(source, out, sems.at[len(copies)]))
        copies[-1].start()
    after[...] = jnp.zeros_like(after)
    for copy in copies:
        copy.wait()


def write_a_kernel(a, a_got, _after, _w, w_out, after, sems):
    copies = []
    write_a(False, sems, copies, a, a_got, w_out)
    after[...] = jnp.zeros_like(after)
    copies[0].wait()


def write_b_kernel(rows, b, b_got, _after, _w, w_out, sems):
    copies = []
    write_b(False, rows, sems, copies, b, b_got, w_out)
    for copy in copies:
        copy.wait()


def body(hidden_acts, out_cotangent, weight, first_moment, second_moment):
    rows, width = weight.shape
    tokens, all_rows = hidden_acts.shape
    some_rows, levels = all_rows // 2, lax.axis_size("shard") // 2
    half, quarter = width // 2, width // 4
    count = half // CHUNK
    steps = far_first(levels)
    halves = [shape((all_rows, half), BF16), shape((all_rows, half), F32)]

    a_sent, a_kept, turned, cots = call(
        load_kernel,
        halves + [shape((all_rows, tokens), BF16), shape((tokens, half), BF16)],
        hidden_acts, out_cotangent, far_in=(0, 1),
        scratch=[
            pltpu.VMEM((tokens, all_rows), BF16),
            pltpu.VMEM((count, tokens, CHUNK), BF16),
            pltpu.SemaphoreType.DMA((count + 2,)),
        ],
        limit=LOAD_LIMIT,
    )
    a_came = to_core(1, a_sent)
    b_sent, b_kept = call(product_kernel, halves, turned, cots)
    b_came = to_core(1, b_sent)

    def split(kernel, dims, *args):
        return call(kernel, [shape(dims, F32), shape(dims, BF16)], *args)

    by_y = functools.partial(by_y_kernel, rows)
    a_keep, a_send = split(by_x_kernel, (all_rows, quarter), a_kept, a_came)
    a_came = along_x(a_send)
    b_keep, b_send = split(by_y, (some_rows, half), b_kept, b_came)
    b_came = along_y(b_send)
    a_keep, a_send = split(by_y, (some_rows, quarter), a_keep, a_came)
    a_came = along_y(a_send)
    b_keep, b_send = split(by_x_kernel, (some_rows, quarter), b_keep, b_came)
    b_came = along_x(b_send)
    own, *pieces = call(
        functools.partial(by_z_kernel, steps),
        [shape((rows, half), F32)] + [shape((rows, half), BF16)] * (levels - 1), a_keep, a_came, b_keep, b_came,
    )
    pieces = [along_z(piece, k) for k, piece in zip(steps, pieces)]
    new_w, grad = call(
        update_kernel, [shape((rows, half), BF16)] * 2, weight, first_moment, second_moment, own, *pieces,
    )

    pieces = [new_w] + [along_z(new_w, k) for k in steps]
    a_part, b_part = call(
        functools.partial(pack_kernel, steps),
        [shape((some_rows, quarter), BF16), shape((some_rows + 2 * rows, quarter), BF16)], grad, *pieces,
    )
    a_other, b_other = along_y(a_part), along_x(b_part)
    a_mine = call(functools.partial(join_y_kernel, rows), [shape((all_rows, quarter), BF16)], a_part, a_other)[0]
    a_other = along_x(a_mine)
    b_mine, grads = call(
        join_x_kernel, [shape((some_rows, half), BF16), shape((rows, width), BF16)], b_part, b_other,
    )
    b_other = along_y(b_mine)
    a_mine, b_mine, grads = lax.optimization_barrier((a_mine, b_mine, grads))

    w_out = shape((all_rows, width), BF16)
    token = shape((8, 128), F32)
    new_w, new_m, new_v, after = call(
        write_first_kernel, [w_out] + [shape((rows, width), F32)] * 2 + [token],
        first_moment, second_moment,
        a_mine, to_core(0, a_mine), b_mine, to_core(0, b_mine), grads, to_core(0, grads),
        far_out=3,
        scratch=[pltpu.VMEM((rows, width), F32)] * 2 + [pltpu.SemaphoreType.DMA((levels + 3,))],
    )
    a_other, b_other, after = lax.optimization_barrier((a_other, b_other, after))
    a_got, b_got = to_core(0, a_other), to_core(0, b_other)
    new_w, after = call(
        write_a_kernel, [w_out, token], a_other, a_got, after, new_w,
        far_in=(3,), far_out=1, scratch=[pltpu.SemaphoreType.DMA((1,))], aliases={3: 0},
    )
    new_w = call(
        functools.partial(write_b_kernel, rows), [w_out], b_other, b_got, after, new_w,
        far_in=(3,), far_out=1, scratch=[pltpu.SemaphoreType.DMA((levels,))], aliases={3: 0},
    )[0]
    return new_w, new_m, new_v


def solution(mesh):
    return jax.shard_map(
        body,
        mesh=mesh,
        in_specs=(
            P(("rep", "shard"), None),
            P(("rep", "shard"), None),
            P("shard", None),
            P("shard", None),
            P("shard", None),
        ),
        out_specs=(P(), P("shard", None), P("shard", None)),
        check_vma=False,
    )
```

```python
import functools

import jax
import jax.numpy as jnp
from jax import lax
from jax.experimental import pallas as pl
from jax.experimental.pallas import tpu as pltpu
from jax.sharding import PartitionSpec as P

F32 = jnp.float32
BF16 = jnp.bfloat16
CHUNK = 512
LOAD_LIMIT = 48 * 1024 * 1024


def adamw_moments(first_moment, second_moment, grad):
    new_first = 0.9 * first_moment + 0.1 * grad
    new_second = 0.999 * second_moment + 0.001 * grad * grad
    return new_first, new_second


def adamw_weight(weight, new_first, new_second):
    corr_one = 0.9999734386011124
    corr_two = 0.0952078528
    wfloat = weight.astype(F32)
    update = new_first / corr_one / (jnp.sqrt(new_second / corr_two) + 1e-08)
    return (wfloat - 0.05 * (update + 0.1 * wfloat)).astype(BF16)


def shape(dims, kind):
    return jax.ShapeDtypeStruct(dims, kind)


def call(kernel, outs, *args, far_in=(), far_out=0, scratch=(), aliases=None, limit=48 * 1024 * 1024):
    near, far = pl.BlockSpec(memory_space=pltpu.VMEM), pl.BlockSpec(memory_space=pltpu.HBM)
    return pl.pallas_call(
        kernel,
        out_shape=outs,
        in_specs=[far if i in far_in else near for i in range(len(args))],
        out_specs=[far if i < far_out else near for i in range(len(outs))],
        scratch_shapes=scratch,
        input_output_aliases=aliases or {},
        compiler_params=pltpu.CompilerParams(vmem_limit_bytes=limit),
    )(*args)


def between(value, step):
    reps, shards = lax.axis_size("rep"), lax.axis_size("shard")
    pairs = []
    for rep in range(reps):
        for shard in range(shards):
            to_rep, to_shard = step(rep, shard) if rep & 1 else (rep, shard)
            pairs.append((rep * shards + shard, to_rep * shards + to_shard))
    return lax.ppermute(value, ("rep", "shard"), pairs)


def along_x(value):
    return between(value, lambda rep, shard: (rep ^ 2, shard))


def along_y(value):
    return between(value, lambda rep, shard: (rep, shard ^ 1))


def along_z(value, k):
    return between(value, lambda rep, shard: (rep, shard ^ (2 * k)))


def to_sibling(value):
    return lax.ppermute(value, "rep", [(rep, rep ^ 1) for rep in range(lax.axis_size("rep"))])


def far_first(levels):
    return [k for k in range(levels - 1, 0, -1)]


def place():
    rep, shard = lax.axis_index("rep"), lax.axis_index("shard")
    return rep & 1, rep >> 1, shard & 1, shard >> 1


def block(index, size):
    return pl.ds(pl.multiple_of(index * size, size), size)


def load_kernel(acts_ref, cots_ref, sent, kept, turned, cots_b, acts, cots, sems):
    count = cots.shape[0]
    copies = [pltpu.make_async_copy(acts_ref, acts, sems.at[count])]
    for i in range(count):
        source = cots_ref.at[:, pl.ds(i * CHUNK, CHUNK)]
        copies.append(pltpu.make_async_copy(source, cots.at[i], sems.at[i]))
    rest = cots_ref.at[:, pl.ds(count * CHUNK, cots_b.shape[1])]
    copies.append(pltpu.make_async_copy(rest, cots_b, sems.at[count + 1]))
    for copy in copies:
        copy.start()
    copies[0].wait()
    turned[...] = acts[...].T
    for i in range(count):
        copies[i + 1].wait()
        at = slice(i * CHUNK, (i + 1) * CHUNK)
        term = jnp.dot(turned[...], cots[i], preferred_element_type=F32)
        kept[:, at] = term
        sent[:, at] = term.astype(BF16)
    copies[-1].wait()


def product_kernel(turned, cots, sent, kept):
    for i in range(kept.shape[1] // CHUNK):
        at = slice(i * CHUNK, (i + 1) * CHUNK)
        term = jnp.dot(turned[...], cots[:, at], preferred_element_type=F32)
        kept[:, at] = term
        sent[:, at] = term.astype(BF16)


def by_x_kernel(kept, came, keep, send):
    x = place()[1]
    for out, side in ((keep, x), (send, 1 - x)):
        at = block(side, out.shape[1])
        out[...] = (kept[:, at] + came[:, at].astype(F32)).astype(out.dtype)


def by_y_kernel(rows, kept, came, keep, send):
    y = place()[2]
    for out, side in ((keep, y), (send, 1 - y)):
        for z in range(out.shape[0] // rows):
            at = block(2 * z + side, rows)
            out[z * rows:(z + 1) * rows, :] = (kept[at, :] + came[at, :].astype(F32)).astype(out.dtype)


def by_z_kernel(steps, a_kept, a_came, b_kept, b_came, own, *pieces):
    z = place()[3]
    rows, quarter = own.shape[0], a_kept.shape[1]
    for k, out in zip([0] + steps, (own,) + pieces):
        at = block(z ^ k, rows)
        out[:, :quarter] = (a_kept[at, :] + a_came[at, :].astype(F32)).astype(out.dtype)
        out[:, quarter:] = (b_kept[at, :] + b_came[at, :].astype(F32)).astype(out.dtype)


def update_kernel(w, m, v, own, *refs):
    pieces, (new_w, grad) = refs[:-2], refs[-2:]
    x = place()[1]
    total = own[...]
    for ref in pieces:
        total += ref[...].astype(F32)
    grad[...] = total.astype(BF16)
    quarter = total.shape[1] // 2
    for part in range(2):
        mine = slice(part * quarter, (part + 1) * quarter)
        at = block(2 * part + x, quarter)
        new_m, new_v = adamw_moments(m[:, at], v[:, at], total[:, mine])
        new_w[:, mine] = adamw_weight(w[:, at], new_m, new_v)


def pack_kernel(steps, grad, *refs):
    pieces, (a_out, b_out) = refs[:-2], refs[-2:]
    z = place()[3]
    rows, quarter = grad.shape[0], a_out.shape[1]
    for k, ref in zip([0] + steps, pieces):
        at = block(z ^ k, rows)
        a_out[at, :] = ref[:, :quarter]
        b_out[at, :] = ref[:, quarter:]
    tail = a_out.shape[0]
    b_out[tail:tail + rows, :] = grad[:, :quarter]
    b_out[tail + rows:tail + 2 * rows, :] = grad[:, quarter:]


def join_y_kernel(rows, mine, other, out):
    y = place()[2]
    for ref, side in ((mine, y), (other, 1 - y)):
        for z in range(ref.shape[0] // rows):
            out[block(2 * z + side, rows), :] = ref[z * rows:(z + 1) * rows, :]


def join_x_kernel(mine, other, out, grads):
    x = place()[1]
    some_rows, rows = out.shape[0], grads.shape[0]
    for ref, side in ((mine, x), (other, 1 - x)):
        out[:, block(side, ref.shape[1])] = ref[:some_rows, :]
        for part in range(2):
            at = pl.ds(some_rows + part * rows, rows)
            grads[:, block(2 * part + side, ref.shape[1])] = ref[at, :]


def either(core, own, got, action):
    @pl.when(core == 1)
    def _():
        action(own)

    @pl.when(core != 1)
    def _():
        action(got)


def write_a(kept, sems, copies, own, got, w_out):
    core, x, _, _ = place()
    at = block(x if kept else 1 - x, own.shape[1])
    either(core, own, got, lambda ref: pltpu.make_async_copy(ref, w_out.at[:, at], sems.at[len(copies)]).start())
    copies.append(pltpu.make_async_copy(own, w_out.at[:, at], sems.at[len(copies)]))


def write_b(kept, rows, sems, copies, own, got, w_out):
    core, _, y, _ = place()
    width = own.shape[1]
    for z in range(own.shape[0] // rows):
        target = w_out.at[block(2 * z + (y if kept else 1 - y), rows), pl.ds(width, width)]
        sem = sems.at[len(copies)]
        at = pl.ds(z * rows, rows)
        either(core, own, got, lambda ref: pltpu.make_async_copy(ref.at[at, :], target, sem).start())
        copies.append(pltpu.make_async_copy(own.at[at, :], target, sem))


def write_first_kernel(m, v, a, a_got, b, b_got, g, g_got, w_out, m_out, v_out, after, new_m, new_v, sems):
    copies = []
    write_a(True, sems, copies, a, a_got, w_out)
    write_b(True, m.shape[0], sems, copies, b, b_got, w_out)

    def moments(ref):
        new_m[...], new_v[...] = adamw_moments(m[...], v[...], ref[...].astype(F32))

    either(place()[0], g, g_got, moments)
    for source, out in ((new_m, m_out), (new_v, v_out)):
        copies.append(pltpu.make_async_copy(source, out, sems.at[len(copies)]))
        copies[-1].start()
    after[...] = jnp.zeros_like(after)
    for copy in copies:
        copy.wait()


def write_a_kernel(a, a_got, _after, _w, w_out, after, sems):
    copies = []
    write_a(False, sems, copies, a, a_got, w_out)
    after[...] = jnp.zeros_like(after)
    copies[0].wait()


def write_b_kernel(rows, b, b_got, _after, _w, w_out, sems):
    copies = []
    write_b(False, rows, sems, copies, b, b_got, w_out)
    for copy in copies:
        copy.wait()


def body(hidden_acts, out_cotangent, weight, first_moment, second_moment):
    rows, width = weight.shape
    tokens, all_rows = hidden_acts.shape
    some_rows, levels = all_rows // 2, lax.axis_size("shard") // 2
    half, quarter = width // 2, width // 4
    count = half // CHUNK
    steps = far_first(levels)
    halves = [shape((all_rows, half), BF16), shape((all_rows, half), F32)]

    a_sent, a_kept, turned, cots = call(
        load_kernel,
        halves + [shape((all_rows, tokens), BF16), shape((tokens, half), BF16)],
        hidden_acts, out_cotangent, far_in=(0, 1),
        scratch=[
            pltpu.VMEM((tokens, all_rows), BF16),
            pltpu.VMEM((count, tokens, CHUNK), BF16),
            pltpu.SemaphoreType.DMA((count + 2,)),
        ],
        limit=LOAD_LIMIT,
    )
    a_came = to_sibling(a_sent)
    b_sent, b_kept = call(product_kernel, halves, turned, cots)
    b_came = to_sibling(b_sent)

    def split(kernel, dims, *args):
        return call(kernel, [shape(dims, F32), shape(dims, BF16)], *args)

    by_y = functools.partial(by_y_kernel, rows)
    a_keep, a_send = split(by_x_kernel, (all_rows, quarter), a_kept, a_came)
    a_came = along_x(a_send)
    b_keep, b_send = split(by_y, (some_rows, half), b_kept, b_came)
    b_came = along_y(b_send)
    a_keep, a_send = split(by_y, (some_rows, quarter), a_keep, a_came)
    a_came = along_y(a_send)
    b_keep, b_send = split(by_x_kernel, (some_rows, quarter), b_keep, b_came)
    b_came = along_x(b_send)
    own, *pieces = call(
        functools.partial(by_z_kernel, steps),
        [shape((rows, half), F32)] + [shape((rows, half), BF16)] * (levels - 1), a_keep, a_came, b_keep, b_came,
    )
    pieces = [along_z(piece, k) for k, piece in zip(steps, pieces)]
    new_w, grad = call(
        update_kernel, [shape((rows, half), BF16)] * 2, weight, first_moment, second_moment, own, *pieces,
    )

    pieces = [new_w] + [along_z(new_w, k) for k in steps]
    a_part, b_part = call(
        functools.partial(pack_kernel, steps),
        [shape((some_rows, quarter), BF16), shape((some_rows + 2 * rows, quarter), BF16)], grad, *pieces,
    )
    a_other, b_other = along_y(a_part), along_x(b_part)
    a_mine = call(functools.partial(join_y_kernel, rows), [shape((all_rows, quarter), BF16)], a_part, a_other)[0]
    a_other = along_x(a_mine)
    b_mine, grads = call(
        join_x_kernel, [shape((some_rows, half), BF16), shape((rows, width), BF16)], b_part, b_other,
    )
    b_other = along_y(b_mine)
    a_mine, b_mine, grads = lax.optimization_barrier((a_mine, b_mine, grads))

    w_out = shape((all_rows, width), BF16)
    token = shape((8, 128), F32)
    new_w, new_m, new_v, after = call(
        write_first_kernel, [w_out] + [shape((rows, width), F32)] * 2 + [token],
        first_moment, second_moment,
        a_mine, to_sibling(a_mine), b_mine, to_sibling(b_mine), grads, to_sibling(grads),
        far_out=3,
        scratch=[pltpu.VMEM((rows, width), F32)] * 2 + [pltpu.SemaphoreType.DMA((levels + 3,))],
    )
    a_other, b_other, after = lax.optimization_barrier((a_other, b_other, after))
    a_got, b_got = to_sibling(a_other), to_sibling(b_other)
    new_w, after = call(
        write_a_kernel, [w_out, token], a_other, a_got, after, new_w,
        far_in=(3,), far_out=1, scratch=[pltpu.SemaphoreType.DMA((1,))], aliases={3: 0},
    )
    new_w = call(
        functools.partial(write_b_kernel, rows), [w_out], b_other, b_got, after, new_w,
        far_in=(3,), far_out=1, scratch=[pltpu.SemaphoreType.DMA((levels,))], aliases={3: 0},
    )[0]
    return new_w, new_m, new_v


def solution(mesh):
    return jax.shard_map(
        body,
        mesh=mesh,
        in_specs=(
            P(("rep", "shard"), None),
            P(("rep", "shard"), None),
            P("shard", None),
            P("shard", None),
            P("shard", None),
        ),
        out_specs=(P(), P("shard", None), P("shard", None)),
        check_vma=False,
    )
```

```python
import functools

import jax
import jax.numpy as jnp
from jax import lax
from jax.experimental import pallas as pl
from jax.experimental.pallas import tpu as pltpu
from jax.sharding import PartitionSpec as P

F32 = jnp.float32
BF16 = jnp.bfloat16
CHUNK = 512
LOAD_LIMIT = 48 * 1024 * 1024


def adamw_moments(first_moment, second_moment, grad):
    new_first = 0.9 * first_moment + 0.1 * grad
    new_second = 0.999 * second_moment + 0.001 * grad * grad
    return new_first, new_second


def adamw_weight(weight, new_first, new_second):
    corr_one = 0.9999734386011124
    corr_two = 0.0952078528
    wfloat = weight.astype(F32)
    update = new_first / corr_one / (jnp.sqrt(new_second / corr_two) + 1e-08)
    return (wfloat - 0.05 * (update + 0.1 * wfloat)).astype(BF16)


def shape(dims, kind):
    return jax.ShapeDtypeStruct(dims, kind)


def call(kernel, outs, *args, far_in=(), far_out=0, scratch=(), aliases=None, limit=48 * 1024 * 1024):
    near, far = pl.BlockSpec(memory_space=pltpu.VMEM), pl.BlockSpec(memory_space=pltpu.HBM)
    return pl.pallas_call(
        kernel,
        out_shape=outs,
        in_specs=[far if i in far_in else near for i in range(len(args))],
        out_specs=[far if i < far_out else near for i in range(len(outs))],
        scratch_shapes=scratch,
        input_output_aliases=aliases or {},
        compiler_params=pltpu.CompilerParams(vmem_limit_bytes=limit),
    )(*args)


def exchange(value, other):
    reps, shards = lax.axis_size("rep"), lax.axis_size("shard")
    pairs = []
    for rep in range(reps):
        for shard in range(shards):
            to_rep, to_shard = other(rep, shard)
            pairs.append((rep * shards + shard, to_rep * shards + to_shard))
    return lax.ppermute(value, ("rep", "shard"), pairs)


def to_sibling(value):
    return exchange(value, lambda rep, shard: (rep ^ 1, shard))


def across(value, dy, dx):
    return exchange(value, lambda rep, shard: (rep ^ (2 * dx), shard ^ dy))


def along_z(value, k):
    return exchange(value, lambda rep, shard: (rep, shard ^ (2 * k)))


SQUARE = ((1, 1), (0, 1), (1, 0))


def far_first(levels):
    return [k for k in range(levels - 1, 0, -1)]


def place():
    rep, shard = lax.axis_index("rep"), lax.axis_index("shard")
    return rep & 1, rep >> 1, shard & 1, shard >> 1


def block(index, size):
    return pl.ds(pl.multiple_of(index * size, size), size)


def load_kernel(acts_ref, cots_ref, out, turned, kept_cots, acts, cots, sems):
    core = place()[0]
    count = cots.shape[0]
    copies = [pltpu.make_async_copy(acts_ref, acts, sems.at[count])]
    for i in range(count):
        source = cots_ref.at[:, block((1 - core) * count + i, CHUNK)]
        copies.append(pltpu.make_async_copy(source, cots.at[i], sems.at[i]))
    own = cots_ref.at[:, block(core, kept_cots.shape[1])]
    copies.append(pltpu.make_async_copy(own, kept_cots, sems.at[count + 1]))
    for copy in copies:
        copy.start()
    copies[0].wait()
    turned[...] = acts[...].T
    for i in range(count):
        copies[i + 1].wait()
        term = jnp.dot(turned[...], cots[i], preferred_element_type=F32)
        out[:, i * CHUNK:(i + 1) * CHUNK] = term.astype(out.dtype)
    copies[-1].wait()


def product_kernel(turned, cots, out):
    for i in range(out.shape[1] // CHUNK):
        at = slice(i * CHUNK, (i + 1) * CHUNK)
        out[:, at] = jnp.dot(turned[...], cots[:, at], preferred_element_type=F32)


def square_kernel(kept, came, own, *pieces):
    _, x, y, _ = place()
    some_rows, quarter = own.shape
    rows = kept.shape[0] // lax.axis_size("shard")
    for (dy, dx), out in zip(((0, 0),) + SQUARE, (own,) + pieces):
        cols = block(x ^ dx, quarter)
        for z in range(some_rows // rows):
            at = block(2 * z + (y ^ dy), rows)
            out[z * rows:(z + 1) * rows, :] = (kept[at, cols] + came[at, cols].astype(F32)).astype(out.dtype)


def line_kernel(steps, kept, *refs):
    came, (own, *pieces) = refs[:len(SQUARE)], refs[len(SQUARE):]
    z = place()[3]
    rows = own.shape[0]
    for k, out in zip([0] + steps, [own] + pieces):
        at = block(z ^ k, rows)
        total = kept[at, :]
        for ref in came:
            total += ref[at, :].astype(F32)
        out[...] = total.astype(out.dtype)


def update_kernel(w, m, v, own, *refs):
    pieces, (new_w, grad) = refs[:-2], refs[-2:]
    core, x, _, _ = place()
    total = own[...]
    for ref in pieces:
        total += ref[...].astype(F32)
    grad[...] = total.astype(BF16)
    at = block(core * 2 + x, total.shape[1])
    new_m, new_v = adamw_moments(m[:, at], v[:, at], total)
    new_w[...] = adamw_weight(w[:, at], new_m, new_v)


def pack_kernel(steps, grad, *refs):
    pieces, (out, with_grad) = refs[:-2], refs[-2:]
    z = place()[3]
    rows, some_rows = grad.shape[0], out.shape[0]
    for k, ref in zip([0] + steps, pieces):
        at = block(z ^ k, rows)
        out[at, :] = ref[...]
        with_grad[at, :] = ref[...]
    with_grad[some_rows:, :] = grad[...]


def half_kernel(own, *refs):
    parts, out = (own,) + refs[:-1], refs[-1]
    _, x, y, _ = place()
    rows = out.shape[0] // (lax.axis_size("shard") + 1)
    some_rows, quarter = parts[-1].shape
    for (dy, dx), ref in zip(((0, 0),) + SQUARE[::-1], parts):
        cols = block(x ^ dx, quarter)
        for z in range(some_rows // rows):
            out[block(2 * z + (y ^ dy), rows), cols] = ref[z * rows:(z + 1) * rows, :]
        if dy == 0:
            out[2 * some_rows:, cols] = ref[some_rows:, :]


def write_kernel(away, part, m, v, *refs):
    w_out, m_out, v_out, new_m, new_v, sems = refs[-6:]
    core = place()[0]
    all_rows, half = w_out.shape[0], part.shape[1]
    at = block(1 - core if away else core, half)
    copies = [pltpu.make_async_copy(part.at[pl.ds(0, all_rows), :], w_out.at[:, at], sems.at[0])]
    copies[0].start()
    new_m[...], new_v[...] = adamw_moments(m[:, at], v[:, at], part[all_rows:, :].astype(F32))
    for i, (source, out) in enumerate(((new_m, m_out), (new_v, v_out))):
        copies.append(pltpu.make_async_copy(source, out.at[:, at], sems.at[i + 1]))
        copies[-1].start()
    for copy in copies:
        copy.wait()


def body(hidden_acts, out_cotangent, weight, first_moment, second_moment):
    rows, width = weight.shape
    tokens, all_rows = hidden_acts.shape
    some_rows, levels = all_rows // 2, lax.axis_size("shard") // 2
    half, quarter = width // 2, width // 4
    count = half // CHUNK
    steps = far_first(levels)

    away, turned, cots = call(
        load_kernel,
        [shape((all_rows, half), BF16), shape((all_rows, tokens), BF16), shape((tokens, half), BF16)],
        hidden_acts, out_cotangent, far_in=(0, 1),
        scratch=[
            pltpu.VMEM((tokens, all_rows), BF16),
            pltpu.VMEM((count, tokens, CHUNK), BF16),
            pltpu.SemaphoreType.DMA((count + 2,)),
        ],
        limit=LOAD_LIMIT,
    )
    came = to_sibling(away)
    kept = call(product_kernel, [shape((all_rows, half), F32)], turned, cots)[0]

    own, *pieces = call(
        square_kernel,
        [shape((some_rows, quarter), F32)] + [shape((some_rows, quarter), BF16)] * len(SQUARE), kept, came,
    )
    came = [across(piece, *step) for step, piece in zip(SQUARE, pieces)]
    own, *pieces = call(
        functools.partial(line_kernel, steps),
        [shape((rows, quarter), F32)] + [shape((rows, quarter), BF16)] * (levels - 1), own, *came,
    )
    pieces = [along_z(piece, k) for k, piece in zip(steps, pieces)]
    new_w, grad = call(
        update_kernel, [shape((rows, quarter), BF16)] * 2,
        weight, first_moment, second_moment, own, *pieces,
    )

    back = steps[::-1]
    pieces = [new_w] + [along_z(new_w, k) for k in back]
    mine, with_grad = call(
        functools.partial(pack_kernel, back),
        [shape((some_rows, quarter), BF16), shape((some_rows + rows, quarter), BF16)], grad, *pieces,
    )
    parts = [across(mine if dy else with_grad, dy, dx) for dy, dx in SQUARE[::-1]]
    part = call(half_kernel, [shape((all_rows + rows, half), BF16)], with_grad, *parts)[0]
    other = to_sibling(part)
    results = [shape((all_rows, width), BF16), shape((rows, width), F32), shape((rows, width), F32)]
    scratch = [pltpu.VMEM((rows, half), F32), pltpu.VMEM((rows, half), F32), pltpu.SemaphoreType.DMA((3,))]
    written = call(
        functools.partial(write_kernel, False), results,
        part, first_moment, second_moment, far_out=3, scratch=scratch,
    )
    return tuple(call(
        functools.partial(write_kernel, True), results,
        other, first_moment, second_moment, *written,
        far_in=(3, 4, 5), far_out=3, scratch=scratch, aliases={3: 0, 4: 1, 5: 2},
    ))


def solution(mesh):
    return jax.shard_map(
        body,
        mesh=mesh,
        in_specs=(
            P(("rep", "shard"), None),
            P(("rep", "shard"), None),
            P("shard", None),
            P("shard", None),
            P("shard", None),
        ),
        out_specs=(P(), P("shard", None), P("shard", None)),
        check_vma=False,
    )
```

```python
import functools

import jax
import jax.numpy as jnp
from jax import lax
from jax.experimental import pallas as pl
from jax.experimental.pallas import tpu as pltpu
from jax.sharding import PartitionSpec as P

F32 = jnp.float32
BF16 = jnp.bfloat16
CHUNK = 512
LOAD_LIMIT = 48 * 1024 * 1024


def adamw_moments(first_moment, second_moment, grad):
    new_first = 0.9 * first_moment + 0.1 * grad
    new_second = 0.999 * second_moment + 0.001 * grad * grad
    return new_first, new_second


def adamw_weight(weight, new_first, new_second):
    corr_one = 0.9999734386011124
    corr_two = 0.0952078528
    wfloat = weight.astype(F32)
    update = new_first / corr_one / (jnp.sqrt(new_second / corr_two) + 1e-08)
    return (wfloat - 0.05 * (update + 0.1 * wfloat)).astype(BF16)


def shape(dims, kind):
    return jax.ShapeDtypeStruct(dims, kind)


def call(kernel, outs, *args, far_in=(), far_out=0, scratch=(), aliases=None, limit=48 * 1024 * 1024):
    near, far = pl.BlockSpec(memory_space=pltpu.VMEM), pl.BlockSpec(memory_space=pltpu.HBM)
    return pl.pallas_call(
        kernel,
        out_shape=outs,
        in_specs=[far if i in far_in else near for i in range(len(args))],
        out_specs=[far if i < far_out else near for i in range(len(outs))],
        scratch_shapes=scratch,
        input_output_aliases=aliases or {},
        compiler_params=pltpu.CompilerParams(vmem_limit_bytes=limit),
    )(*args)


def exchange(value, other):
    reps, shards = lax.axis_size("rep"), lax.axis_size("shard")
    pairs = []
    for rep in range(reps):
        for shard in range(shards):
            to_rep, to_shard = other(rep, shard)
            pairs.append((rep * shards + shard, to_rep * shards + to_shard))
    return lax.ppermute(value, ("rep", "shard"), pairs)


def to_sibling(value):
    return exchange(value, lambda rep, shard: (rep ^ 1, shard))


SQUARE = ((1, 1), (1, 0), (0, 1))
LINE = (3, 2, 1)
STEPS = tuple(zip(SQUARE, LINE))
X_STEP = SQUARE.index((0, 1))
STAY = ((0, 0), 0)


def stage(value, step, square_core):
    (dy, dx), k = step
    return exchange(
        value,
        lambda rep, shard: (rep ^ (2 * dx), shard ^ dy) if rep & 1 == square_core else (rep, shard ^ (2 * k)),
    )


def wide_stage(value, step):
    return stage(value, step, 0)


def narrow_stage(value, step):
    return stage(value, step, 1)


def along_rest(value, k):
    return exchange(value, lambda rep, shard: (rep, shard ^ (8 * k)))


def place():
    rep, shard = lax.axis_index("rep"), lax.axis_index("shard")
    return rep & 1, rep >> 1, shard & 1, (shard >> 1) & 3, shard >> 3


def in_half(step, group):
    core, x, y, z, _ = place()
    (dy, dx), k = step
    first = core == 0
    return (
        jnp.where(first, y ^ dy, group >> 1), jnp.where(first, x ^ dx, group & 1), jnp.where(first, group, z ^ k),
    )


def group_of(step):
    core, x, y, z, _ = place()
    (dy, dx), k = step
    return jnp.where(core == 0, z ^ k, 2 * (y ^ dy) + (x ^ dx))


def block(index, size):
    return pl.ds(pl.multiple_of(index * size, size), size)


def load_kernel(acts_ref, cots_ref, out, turned, kept_cots, acts, cots, sems):
    core = place()[0]
    count = cots.shape[0]
    copies = [pltpu.make_async_copy(acts_ref, acts, sems.at[count])]
    for i in range(count):
        source = cots_ref.at[:, block((1 - core) * count + i, CHUNK)]
        copies.append(pltpu.make_async_copy(source, cots.at[i], sems.at[i]))
    own = cots_ref.at[:, block(core, kept_cots.shape[1])]
    copies.append(pltpu.make_async_copy(own, kept_cots, sems.at[count + 1]))
    for copy in copies:
        copy.start()
    copies[0].wait()
    turned[...] = acts[...].T
    for i in range(count):
        copies[i + 1].wait()
        term = jnp.dot(turned[...], cots[i], preferred_element_type=F32)
        out[:, i * CHUNK:(i + 1) * CHUNK] = term.astype(out.dtype)
    copies[-1].wait()


def product_kernel(turned, cots, out):
    for i in range(out.shape[1] // CHUNK):
        at = slice(i * CHUNK, (i + 1) * CHUNK)
        out[:, at] = jnp.dot(turned[...], cots[:, at], preferred_element_type=F32)


def wide_kernel(rows, kept, came, own, *pieces):
    quarter = own.shape[1]
    count = own.shape[0] // (4 * rows)
    for step, out in zip((STAY,) + STEPS, (own,) + pieces):
        for group in range(4):
            y, x, z = in_half(step, group)
            cols = block(x, quarter)
            for w in range(count):
                at = block(8 * w + 2 * z + y, rows)
                total = kept[at, cols] + came[at, cols].astype(F32)
                to = (group * count + w) * rows
                out[to:to + rows, :] = total.astype(out.dtype)


def narrow_kernel(kept, *refs):
    came, (own, *pieces) = refs[:len(STEPS)], refs[len(STEPS):]
    for step, out in zip((STAY,) + STEPS, [own] + pieces):
        at = block(group_of(step), out.shape[0])
        total = kept[at, :]
        for ref in came:
            total += ref[at, :].astype(F32)
        out[...] = total.astype(out.dtype)


def rest_kernel(kept, *refs):
    came, outs = refs[:len(STEPS)], refs[len(STEPS):]
    w = place()[4]
    for k, out in enumerate(outs):
        at = block(w ^ k, out.shape[0])
        total = kept[at, :]
        for ref in came:
            total += ref[at, :].astype(F32)
        out[...] = total.astype(out.dtype)


def update_kernel(w, m, v, own, *refs):
    pieces, (new_w, grad) = refs[:-2], refs[-2:]
    core, x, _, _, _ = place()
    total = own[...]
    for ref in pieces:
        total += ref[...].astype(F32)
    grad[...] = total.astype(BF16)
    at = block(core * 2 + x, total.shape[1])
    new_m, new_v = adamw_moments(m[:, at], v[:, at], total)
    new_w[...] = adamw_weight(w[:, at], new_m, new_v)


def rest_back_kernel(grad, *refs):
    pieces, (out, with_grad) = refs[:-2], refs[-2:]
    w = place()[4]
    rows, tail = grad.shape[0], out.shape[0]
    for k, ref in enumerate(pieces):
        at = block(w ^ k, rows)
        out[at, :] = ref[...]
        with_grad[at, :] = ref[...]
    with_grad[tail:, :] = grad[...]


def narrow_back_kernel(own, *refs):
    parts, (out, with_grad) = (own,) + refs[:-2], refs[-2:]
    size = out.shape[0] // 4
    for step, ref in zip((STAY,) + STEPS[::-1], parts):
        at = block(group_of(step), size)
        out[at, :] = ref[:size, :]
        with_grad[at, :] = ref[:size, :]
    with_grad[4 * size:, :] = own[size:, :]


def wide_back_kernel(early, own, *refs):
    parts, out = (own,) + refs[:-1], refs[-1]
    core, near, _, _, _ = place()
    rows = out.shape[0] // (lax.axis_size("shard") + 1)
    all_rows, quarter = out.shape[0] - rows, own.shape[1]
    size = all_rows // 2
    count = size // (4 * rows)
    for step, ref in zip((STAY,) + STEPS[::-1], parts):
        for group in range(4):
            y, x, z = in_half(step, group)
            for w in range(count):
                at = (group * count + w) * rows
                out[block(8 * w + 2 * z + y, rows), block(x, quarter)] = ref[at:at + rows, :]
    out[all_rows:, block(near, quarter)] = own[size:, :]
    late = parts[len(STEPS) - X_STEP]
    far = block(1 - near, quarter)
    narrow = early.shape[0] - rows

    @pl.when(core == 0)
    def _():
        out[all_rows:, far] = late[size:, :]

    @pl.when(core != 0)
    def _():
        out[all_rows:, far] = early[narrow:, :]


def write_kernel(away, part, m, v, *refs):
    w_out, m_out, v_out, new_m, new_v, sems = refs[-6:]
    core = place()[0]
    all_rows, half = w_out.shape[0], part.shape[1]
    at = block(1 - core if away else core, half)
    copies = [pltpu.make_async_copy(part.at[pl.ds(0, all_rows), :], w_out.at[:, at], sems.at[0])]
    copies[0].start()
    new_m[...], new_v[...] = adamw_moments(m[:, at], v[:, at], part[all_rows:, :].astype(F32))
    for i, (source, out) in enumerate(((new_m, m_out), (new_v, v_out))):
        copies.append(pltpu.make_async_copy(source, out.at[:, at], sems.at[i + 1]))
        copies[-1].start()
    for copy in copies:
        copy.wait()


def body(hidden_acts, out_cotangent, weight, first_moment, second_moment):
    rows, width = weight.shape
    tokens, all_rows = hidden_acts.shape
    half, quarter = width // 2, width // 4
    count = half // CHUNK
    rest = lax.axis_size("shard") // 8
    wide_rows, narrow_rows = all_rows // 2, all_rows // 8

    away, turned, cots = call(
        load_kernel,
        [shape((all_rows, half), BF16), shape((all_rows, tokens), BF16), shape((tokens, half), BF16)],
        hidden_acts, out_cotangent, far_in=(0, 1),
        scratch=[
            pltpu.VMEM((tokens, all_rows), BF16),
            pltpu.VMEM((count, tokens, CHUNK), BF16),
            pltpu.SemaphoreType.DMA((count + 2,)),
        ],
        limit=LOAD_LIMIT,
    )
    came = to_sibling(away)
    kept = call(product_kernel, [shape((all_rows, half), F32)], turned, cots)[0]

    def split(kernel, size, parts, *args):
        kept, sent = shape((size, quarter), F32), shape((size, quarter), BF16)
        return call(kernel, [kept] + [sent] * (parts - 1), *args)

    own, *pieces = split(functools.partial(wide_kernel, rows), wide_rows, 4, kept, came)
    came = [wide_stage(piece, step) for step, piece in zip(STEPS, pieces)]
    own, *pieces = split(narrow_kernel, narrow_rows, 4, own, *came)
    came = [narrow_stage(piece, step) for step, piece in zip(STEPS, pieces)]
    if rest > 1:
        own, *pieces = split(rest_kernel, rows, rest, own, *came)
        came = [along_rest(piece, k + 1) for k, piece in enumerate(pieces)]
    new_w, grad = call(
        update_kernel, [shape((rows, quarter), BF16)] * 2, weight, first_moment, second_moment, own, *came,
    )

    def gathered(kernel, size, *args):
        return call(kernel, [shape((size, quarter), BF16), shape((size + rows, quarter), BF16)], *args)

    def back(send, part, with_grad):
        return [send(with_grad if i == X_STEP else part, STEPS[i]) for i in reversed(range(len(STEPS)))]

    pieces = [along_rest(new_w, k) for k in range(1, rest)]
    part, with_grad = gathered(rest_back_kernel, narrow_rows, grad, new_w, *pieces)
    came = back(narrow_stage, part, with_grad)
    early = came[len(STEPS) - 1 - X_STEP]
    part, with_grad = gathered(narrow_back_kernel, wide_rows, with_grad, *came)
    came = back(wide_stage, part, with_grad)
    part = call(wide_back_kernel, [shape((all_rows + rows, half), BF16)], early, with_grad, *came)[0]
    other = to_sibling(part)
    results = [shape((all_rows, width), BF16), shape((rows, width), F32), shape((rows, width), F32)]
    scratch = [pltpu.VMEM((rows, half), F32), pltpu.VMEM((rows, half), F32), pltpu.SemaphoreType.DMA((3,))]
    written = call(
        functools.partial(write_kernel, False), results,
        part, first_moment, second_moment, far_out=3, scratch=scratch,
    )
    return tuple(call(
        functools.partial(write_kernel, True), results,
        other, first_moment, second_moment, *written,
        far_in=(3, 4, 5), far_out=3, scratch=scratch, aliases={3: 0, 4: 1, 5: 2},
    ))


def solution(mesh):
    return jax.shard_map(
        body,
        mesh=mesh,
        in_specs=(
            P(("rep", "shard"), None),
            P(("rep", "shard"), None),
            P("shard", None),
            P("shard", None),
            P("shard", None),
        ),
        out_specs=(P(), P("shard", None), P("shard", None)),
        check_vma=False,
    )
```

```python
import functools

import jax
import jax.numpy as jnp
from jax import lax
from jax.experimental import pallas as pl
from jax.experimental.pallas import tpu as pltpu
from jax.sharding import PartitionSpec as P

F32 = jnp.float32
BF16 = jnp.bfloat16
CHUNK = 512
LOAD_LIMIT = 45 * 1024 * 1024


def adamw_moments(first_moment, second_moment, grad):
    new_first = 0.9 * first_moment + 0.1 * grad
    new_second = 0.999 * second_moment + 0.001 * grad * grad
    return new_first, new_second


def adamw_weight(weight, new_first, new_second):
    corr_one = 0.9999734386011124
    corr_two = 0.0952078528
    wfloat = weight.astype(F32)
    update = new_first / corr_one / (jnp.sqrt(new_second / corr_two) + 1e-08)
    return (wfloat - 0.05 * (update + 0.1 * wfloat)).astype(BF16)


def shape(dims, kind):
    return jax.ShapeDtypeStruct(dims, kind)


def call(kernel, outs, *args, far_in=(), far_out=0, scratch=(), aliases=None, limit=48 * 1024 * 1024):
    near, far = pl.BlockSpec(memory_space=pltpu.VMEM), pl.BlockSpec(memory_space=pltpu.HBM)
    return pl.pallas_call(
        kernel,
        out_shape=outs,
        in_specs=[far if i in far_in else near for i in range(len(args))],
        out_specs=[far if i < far_out else near for i in range(len(outs))],
        scratch_shapes=scratch,
        input_output_aliases=aliases or {},
        compiler_params=pltpu.CompilerParams(vmem_limit_bytes=limit),
    )(*args)


def exchange(value, other):
    reps, shards = lax.axis_size("rep"), lax.axis_size("shard")
    pairs = []
    for rep in range(reps):
        for shard in range(shards):
            to_rep, to_shard = other(rep, shard)
            pairs.append((rep * shards + shard, to_rep * shards + to_shard))
    return lax.ppermute(value, ("rep", "shard"), pairs)


def to_sibling(value):
    return exchange(value, lambda rep, shard: (rep ^ 1, shard))


SQUARE = ((1, 1), (1, 0), (0, 1))
LINE = (3, 2, 1)
STEPS = tuple(zip(SQUARE, LINE))
X_STEP = SQUARE.index((0, 1))
STAY = ((0, 0), 0)


def stage(value, step, square_core):
    (dy, dx), k = step
    return exchange(
        value,
        lambda rep, shard: (rep ^ (2 * dx), shard ^ dy) if rep & 1 == square_core else (rep, shard ^ (2 * k)),
    )


def wide_stage(value, step):
    return stage(value, step, 0)


def narrow_stage(value, step):
    return stage(value, step, 1)


def along_rest(value, k):
    return exchange(value, lambda rep, shard: (rep, shard ^ (8 * k)))


def place():
    rep, shard = lax.axis_index("rep"), lax.axis_index("shard")
    return rep & 1, rep >> 1, shard & 1, (shard >> 1) & 3, shard >> 3


def in_half(step, group):
    core, x, y, z, _ = place()
    (dy, dx), k = step
    first = core == 0
    return (
        jnp.where(first, y ^ dy, group >> 1), jnp.where(first, x ^ dx, group & 1), jnp.where(first, group, z ^ k),
    )


def group_of(step):
    core, x, y, z, _ = place()
    (dy, dx), k = step
    return jnp.where(core == 0, z ^ k, 2 * (y ^ dy) + (x ^ dx))


def block(index, size):
    return pl.ds(pl.multiple_of(index * size, size), size)


def load_kernel(cots_ref, away, kept, sems):
    core = place()[0]
    copies = []
    for out, side in ((away, 1 - core), (kept, core)):
        source = cots_ref.at[:, block(side, out.shape[1])]
        copies.append(pltpu.make_async_copy(source, out, sems.at[len(copies)]))
        copies[-1].start()
    for copy in copies:
        copy.wait()


def away_kernel(acts, cots, out, turned):
    turned[...] = acts[...].T
    for i in range(out.shape[1] // CHUNK):
        at = slice(i * CHUNK, (i + 1) * CHUNK)
        out[:, at] = jnp.dot(turned[...], cots[:, at], preferred_element_type=F32).astype(BF16)


def product_kernel(turned, cots, out):
    for i in range(out.shape[1] // CHUNK):
        at = slice(i * CHUNK, (i + 1) * CHUNK)
        out[:, at] = jnp.dot(turned[...], cots[:, at], preferred_element_type=F32)


def wide_kernel(rows, kept, came, own, *pieces):
    quarter = own.shape[1]
    count = own.shape[0] // (4 * rows)
    for step, out in zip((STAY,) + STEPS, (own,) + pieces):
        for group in range(4):
            y, x, z = in_half(step, group)
            cols = block(x, quarter)
            for w in range(count):
                at = block(8 * w + 2 * z + y, rows)
                total = kept[at, cols] + came[at, cols].astype(F32)
                to = (group * count + w) * rows
                out[to:to + rows, :] = total.astype(out.dtype)


def narrow_kernel(kept, *refs):
    came, (own, *pieces) = refs[:len(STEPS)], refs[len(STEPS):]
    for step, out in zip((STAY,) + STEPS, [own] + pieces):
        at = block(group_of(step), out.shape[0])
        total = kept[at, :]
        for ref in came:
            total += ref[at, :].astype(F32)
        out[...] = total.astype(out.dtype)


def rest_kernel(kept, *refs):
    came, outs = refs[:len(STEPS)], refs[len(STEPS):]
    w = place()[4]
    for k, out in enumerate(outs):
        at = block(w ^ k, out.shape[0])
        total = kept[at, :]
        for ref in came:
            total += ref[at, :].astype(F32)
        out[...] = total.astype(out.dtype)


def update_kernel(w, m, v, own, *refs):
    pieces, (new_w, grad) = refs[:-2], refs[-2:]
    core, x, _, _, _ = place()
    total = own[...]
    for ref in pieces:
        total += ref[...].astype(F32)
    grad[...] = total.astype(BF16)
    at = block(core * 2 + x, total.shape[1])
    new_m, new_v = adamw_moments(m[:, at], v[:, at], total)
    new_w[...] = adamw_weight(w[:, at], new_m, new_v)


def put(outs, at, value):
    for out in outs:
        out[at, :] = value


def rest_back_kernel(grad, *refs):
    pieces, outs = refs[:-len(STEPS)], refs[-len(STEPS):]
    w = place()[4]
    rows, tail = grad.shape[0], outs[0].shape[0]
    for k, ref in enumerate(pieces):
        put(outs, block(w ^ k, rows), ref[...])
    outs[X_STEP][tail:, :] = grad[...]


def narrow_back_kernel(_, own, *refs):
    parts, outs = (own,) + refs[:-len(STEPS)], refs[-len(STEPS):]
    size = outs[0].shape[0] // 4
    for step, ref in zip((STAY,) + STEPS, parts):
        put(outs, block(group_of(step), size), ref[:size, :])
    outs[X_STEP][4 * size:, :] = own[size:, :]


def wide_back_kernel(early, own, *refs):
    parts, out = (own,) + refs[:-1], refs[-1]
    core, near, _, _, _ = place()
    rows = out.shape[0] // (lax.axis_size("shard") + 1)
    all_rows, quarter = out.shape[0] - rows, own.shape[1]
    size = all_rows // 2
    count = size // (4 * rows)
    for step, ref in zip((STAY,) + STEPS, parts):
        for group in range(4):
            y, x, z = in_half(step, group)
            for w in range(count):
                at = (group * count + w) * rows
                out[block(8 * w + 2 * z + y, rows), block(x, quarter)] = ref[at:at + rows, :]
    out[all_rows:, block(near, quarter)] = own[size:, :]
    late = parts[1 + X_STEP]
    far = block(1 - near, quarter)
    narrow = early.shape[0] - rows

    @pl.when(core == 0)
    def _():
        out[all_rows:, far] = late[size:, :]

    @pl.when(core != 0)
    def _():
        out[all_rows:, far] = early[narrow:, :]


def write_kernel(away, part, m, v, *refs):
    w_out, m_out, v_out, new_m, new_v, sems = refs[-6:]
    core = place()[0]
    all_rows, half = w_out.shape[0], part.shape[1]
    at = block(1 - core if away else core, half)
    copies = [pltpu.make_async_copy(part.at[pl.ds(0, all_rows), :], w_out.at[:, at], sems.at[0])]
    copies[0].start()
    new_m[...], new_v[...] = adamw_moments(m[:, at], v[:, at], part[all_rows:, :].astype(F32))
    for i, (source, out) in enumerate(((new_m, m_out), (new_v, v_out))):
        copies.append(pltpu.make_async_copy(source, out.at[:, at], sems.at[i + 1]))
        copies[-1].start()
    for copy in copies:
        copy.wait()


def body(hidden_acts, out_cotangent, weight, first_moment, second_moment):
    rows, width = weight.shape
    tokens, all_rows = hidden_acts.shape
    half, quarter = width // 2, width // 4
    rest = lax.axis_size("shard") // 8
    wide_rows, narrow_rows = all_rows // 2, all_rows // 8

    loaded = [shape((tokens, half), BF16)] * 2
    away_cots, cots = call(
        load_kernel, loaded, out_cotangent, far_in=(0,), scratch=[pltpu.SemaphoreType.DMA((2,))], limit=LOAD_LIMIT,
    )
    away, turned = call(
        away_kernel, [shape((all_rows, half), BF16), shape((all_rows, tokens), BF16)], hidden_acts, away_cots,
    )
    came = to_sibling(away)
    kept = call(product_kernel, [shape((all_rows, half), F32)], turned, cots)[0]

    def split(kernel, size, parts, *args):
        kept, sent = shape((size, quarter), F32), shape((size, quarter), BF16)
        return call(kernel, [kept] + [sent] * (parts - 1), *args)

    own, *pieces = split(functools.partial(wide_kernel, rows), wide_rows, 4, kept, came)
    came = [wide_stage(piece, step) for step, piece in zip(STEPS, pieces)]
    own, *pieces = split(narrow_kernel, narrow_rows, 4, own, *came)
    came = [narrow_stage(piece, step) for step, piece in zip(STEPS, pieces)]
    if rest > 1:
        own, *pieces = split(rest_kernel, rows, rest, own, *came)
        came = [along_rest(piece, k + 1) for k, piece in enumerate(pieces)]
    new_w, grad = call(
        update_kernel, [shape((rows, quarter), BF16)] * 2, weight, first_moment, second_moment, own, *came,
    )

    def gathered(kernel, size, *args):
        sizes = [size + rows if i == X_STEP else size for i in range(len(STEPS))]
        return call(kernel, [shape((size, quarter), BF16) for size in sizes], *args)

    level = to_sibling(grad)
    pieces = [along_rest(new_w, k) for k in range(1, rest)]
    parts = gathered(rest_back_kernel, narrow_rows, grad, new_w, *pieces)
    early = [narrow_stage(part, step) for step, part in zip(STEPS, parts)]
    parts = gathered(narrow_back_kernel, wide_rows, level, parts[X_STEP], *early)
    came = [wide_stage(part, step) for step, part in zip(STEPS, parts)]
    part = call(
        wide_back_kernel, [shape((all_rows + rows, half), BF16)], early[X_STEP], parts[X_STEP], *came,
    )[0]
    other = to_sibling(part)
    results = [shape((all_rows, width), BF16), shape((rows, width), F32), shape((rows, width), F32)]
    scratch = [pltpu.VMEM((rows, half), F32), pltpu.VMEM((rows, half), F32), pltpu.SemaphoreType.DMA((3,))]
    written = call(
        functools.partial(write_kernel, False), results,
        part, first_moment, second_moment, far_out=3, scratch=scratch,
    )
    return tuple(call(
        functools.partial(write_kernel, True), results,
        other, first_moment, second_moment, *written,
        far_in=(3, 4, 5), far_out=3, scratch=scratch, aliases={3: 0, 4: 1, 5: 2},
    ))


def solution(mesh):
    return jax.shard_map(
        body,
        mesh=mesh,
        in_specs=(
            P(("rep", "shard"), None),
            P(("rep", "shard"), None),
            P("shard", None),
            P("shard", None),
            P("shard", None),
        ),
        out_specs=(P(), P("shard", None), P("shard", None)),
        check_vma=False,
    )
```

```python
import functools

import jax
import jax.numpy as jnp
from jax import lax
from jax.experimental import pallas as pl
from jax.experimental.pallas import tpu as pltpu
from jax.sharding import PartitionSpec as P

F32 = jnp.float32
BF16 = jnp.bfloat16
CHUNK = 512
LOAD_LIMIT = 48 * 1024 * 1024
KEPT_LIMIT = 52 * 1024 * 1024


def adamw_moments(first_moment, second_moment, grad):
    new_first = 0.9 * first_moment + 0.1 * grad
    new_second = 0.999 * second_moment + 0.001 * grad * grad
    return new_first, new_second


def adamw_weight(weight, new_first, new_second):
    corr_one = 0.9999734386011124
    corr_two = 0.0952078528
    wfloat = weight.astype(F32)
    update = new_first / corr_one / (jnp.sqrt(new_second / corr_two) + 1e-08)
    return (wfloat - 0.05 * (update + 0.1 * wfloat)).astype(BF16)


def shape(dims, kind):
    return jax.ShapeDtypeStruct(dims, kind)


def call(kernel, outs, *args, far_in=(), far_out=0, scratch=(), aliases=None, limit=48 * 1024 * 1024):
    near, far = pl.BlockSpec(memory_space=pltpu.VMEM), pl.BlockSpec(memory_space=pltpu.HBM)
    return pl.pallas_call(
        kernel,
        out_shape=outs,
        in_specs=[far if i in far_in else near for i in range(len(args))],
        out_specs=[far if i < far_out else near for i in range(len(outs))],
        scratch_shapes=scratch,
        input_output_aliases=aliases or {},
        compiler_params=pltpu.CompilerParams(vmem_limit_bytes=limit),
    )(*args)


def exchange(value, other):
    reps, shards = lax.axis_size("rep"), lax.axis_size("shard")
    pairs = []
    for rep in range(reps):
        for shard in range(shards):
            to_rep, to_shard = other(rep, shard)
            pairs.append((rep * shards + shard, to_rep * shards + to_shard))
    return lax.ppermute(value, ("rep", "shard"), pairs)


def to_sibling(value):
    return exchange(value, lambda rep, shard: (rep ^ 1, shard))


SQUARE = ((1, 1), (1, 0), (0, 1))
LINE = (3, 2, 1)
STEPS = tuple(zip(SQUARE, LINE))
STAY = ((0, 0), 0)


def stage(value, step, square_core):
    (dy, dx), k = step
    return exchange(
        value,
        lambda rep, shard: (rep ^ (2 * dx), shard ^ dy) if rep & 1 == square_core else (rep, shard ^ (2 * k)),
    )


def wide_stage(value, step):
    return stage(value, step, 0)


def narrow_stage(value, step):
    return stage(value, step, 1)


def along_x(value):
    return exchange(value, lambda rep, shard: (rep ^ 2, shard))


def along_rest(value, k):
    return exchange(value, lambda rep, shard: (rep, shard ^ (8 * k)))


def place():
    rep, shard = lax.axis_index("rep"), lax.axis_index("shard")
    return rep & 1, rep >> 1, shard & 1, (shard >> 1) & 3, shard >> 3


def in_half(step, group):
    core, x, y, z, _ = place()
    (dy, dx), k = step
    first = core == 0
    return (
        jnp.where(first, y ^ dy, group >> 1), jnp.where(first, x ^ dx, group & 1), jnp.where(first, group, z ^ k),
    )


def group_of(step):
    core, x, y, z, _ = place()
    (dy, dx), k = step
    return jnp.where(core == 0, z ^ k, 2 * (y ^ dy) + (x ^ dx))


def block(index, size):
    return pl.ds(pl.multiple_of(index * size, size), size)


def load_kernel(cots_ref, away, first, sems):
    core = place()[0]
    starts = ((away, 1 - core), (first, core))
    copies = []
    for out, side in starts:
        at = pl.ds(pl.multiple_of(side * away.shape[1], CHUNK), out.shape[1])
        copies.append(pltpu.make_async_copy(cots_ref.at[:, at], out, sems.at[len(copies)]))
        copies[-1].start()
    for copy in copies:
        copy.wait()


def turn_kernel(acts, cots, out, turned):
    turned[...] = acts[...].T
    for i in range(out.shape[1] // CHUNK):
        at = slice(i * CHUNK, (i + 1) * CHUNK)
        out[:, at] = jnp.dot(turned[...], cots[:, at], preferred_element_type=F32).astype(BF16)


def away_kernel(turned, cots, out):
    skip = cots.shape[1] - out.shape[1]
    for i in range(out.shape[1] // CHUNK):
        at = slice(i * CHUNK, (i + 1) * CHUNK)
        term = jnp.dot(turned[...], cots[:, skip + i * CHUNK:skip + (i + 1) * CHUNK], preferred_element_type=F32)
        out[:, at] = term.astype(BF16)


def kept_kernel(turned, first, cots_ref, out, cots, sems):
    core = place()[0]
    count = cots.shape[0]
    copies = []
    for i in range(count):
        source = cots_ref.at[:, block(core * (count + 1) + i + 1, CHUNK)]
        copies.append(pltpu.make_async_copy(source, cots.at[i], sems.at[i]))
        copies[i].start()
    out[:, :CHUNK] = jnp.dot(turned[...], first[...], preferred_element_type=F32)
    for i in range(count):
        copies[i].wait()
        at = slice((i + 1) * CHUNK, (i + 2) * CHUNK)
        out[:, at] = jnp.dot(turned[...], cots[i], preferred_element_type=F32)


def wide_kernel(rows, kept, came_low, came_high, own, *pieces):
    quarter = own.shape[1]
    count = own.shape[0] // (4 * rows)
    for step, out in zip((STAY,) + STEPS, (own,) + pieces):
        for group in range(4):
            y, x, z = in_half(step, group)
            cols = block(x, quarter)
            for w in range(count):
                at = block(8 * w + 2 * z + y, rows)
                came = jnp.where(x == 0, came_low[at, :], came_high[at, :])
                total = kept[at, cols] + came.astype(F32)
                to = (group * count + w) * rows
                out[to:to + rows, :] = total.astype(out.dtype)


def narrow_kernel(kept, *refs):
    came, (own, *pieces) = refs[:len(STEPS)], refs[len(STEPS):]
    for step, out in zip((STAY,) + STEPS, [own] + pieces):
        at = block(group_of(step), out.shape[0])
        total = kept[at, :]
        for ref in came:
            total += ref[at, :].astype(F32)
        out[...] = total.astype(out.dtype)


def rest_kernel(kept, *refs):
    came, outs = refs[:len(STEPS)], refs[len(STEPS):]
    w = place()[4]
    for k, out in enumerate(outs):
        at = block(w ^ k, out.shape[0])
        total = kept[at, :]
        for ref in came:
            total += ref[at, :].astype(F32)
        out[...] = total.astype(out.dtype)


def update_kernel(w, m, v, own, *refs):
    pieces, (new_w, grad) = refs[:-2], refs[-2:]
    core, x, _, _, _ = place()
    total = own[...]
    for ref in pieces:
        total += ref[...].astype(F32)
    grad[...] = total.astype(BF16)
    at = block(core * 2 + x, total.shape[1])
    new_m, new_v = adamw_moments(m[:, at], v[:, at], total)
    new_w[...] = adamw_weight(w[:, at], new_m, new_v)


def put(outs, at, value):
    for out in outs:
        out[at, :] = value


def put(outs, at, value):
    for out in outs:
        out[at, :] = value


def rest_back_kernel(*refs):
    pieces, outs = refs[:-len(STEPS)], refs[-len(STEPS):]
    w = place()[4]
    rows = pieces[0].shape[0]
    for k, ref in enumerate(pieces):
        put(outs, block(w ^ k, rows), ref[...])


def narrow_back_kernel(_, own, *refs):
    parts, outs = (own,) + refs[:-len(STEPS)], refs[-len(STEPS):]
    size = own.shape[0]
    for step, ref in zip((STAY,) + STEPS, parts):
        put(outs, block(group_of(step), size), ref[...])


def wide_back_kernel(rows, own, *refs):
    parts, out = (own,) + refs[:-1], refs[-1]
    count = own.shape[0] // (4 * rows)
    for step, ref in zip((STAY,) + STEPS, parts):
        for group in range(4):
            y, x, z = in_half(step, group)
            for w in range(count):
                at = (group * count + w) * rows
                out[block(8 * w + 2 * z + y, rows), block(x, own.shape[1])] = ref[at:at + rows, :]


def moments_kernel(m, v, *refs):
    grads, (new_m, new_v) = refs[:4], refs[4:]
    core, x, _, _, _ = place()
    for i, grad in enumerate(grads):
        at = block(2 * (core ^ (i >> 1)) + (x ^ (i & 1)), grad.shape[1])
        new_m[:, at], new_v[:, at] = adamw_moments(m[:, at], v[:, at], grad[...].astype(F32))


def write_kernel(away, part, *refs):
    out, sem = refs[-2:]
    core = place()[0]
    copy = pltpu.make_async_copy(part, out.at[:, block(1 - core if away else core, part.shape[1])], sem)
    copy.start()
    copy.wait()


def body(hidden_acts, out_cotangent, weight, first_moment, second_moment):
    rows, width = weight.shape
    tokens, all_rows = hidden_acts.shape
    half, quarter = width // 2, width // 4
    rest = lax.axis_size("shard") // 8
    wide_rows, narrow_rows = all_rows // 2, all_rows // 8

    chunks = half // CHUNK
    away_cots, first = call(
        load_kernel, [shape((tokens, half), BF16), shape((tokens, CHUNK), BF16)], out_cotangent,
        far_in=(0,), scratch=[pltpu.SemaphoreType.DMA((2,))], limit=LOAD_LIMIT,
    )
    low, turned = call(
        turn_kernel, [shape((all_rows, quarter), BF16), shape((all_rows, tokens), BF16)], hidden_acts, away_cots,
    )
    came_low = to_sibling(low)
    came_high = to_sibling(call(away_kernel, [shape((all_rows, quarter), BF16)], turned, away_cots)[0])
    kept = call(
        kept_kernel, [shape((all_rows, half), F32)], turned, first, out_cotangent,
        far_in=(2,), limit=KEPT_LIMIT,
        scratch=[pltpu.VMEM((chunks - 1, tokens, CHUNK), BF16), pltpu.SemaphoreType.DMA((chunks - 1,))],
    )[0]

    def split(kernel, size, parts, *args):
        kept, sent = shape((size, quarter), F32), shape((size, quarter), BF16)
        return call(kernel, [kept] + [sent] * (parts - 1), *args)

    own, *pieces = split(functools.partial(wide_kernel, rows), wide_rows, 4, kept, came_low, came_high)
    came = [wide_stage(piece, step) for step, piece in zip(STEPS, pieces)]
    own, *pieces = split(narrow_kernel, narrow_rows, 4, own, *came)
    came = [narrow_stage(piece, step) for step, piece in zip(STEPS, pieces)]
    if rest > 1:
        own, *pieces = split(rest_kernel, rows, rest, own, *came)
        came = [along_rest(piece, k + 1) for k, piece in enumerate(pieces)]
    new_w, grad = call(
        update_kernel, [shape((rows, quarter), BF16)] * 2, weight, first_moment, second_moment, own, *came,
    )

    def gathered(kernel, size, *args):
        return call(kernel, [shape((size, quarter), BF16)] * len(STEPS), *args)

    sibling_grad = to_sibling(grad)
    pieces = [along_rest(new_w, k) for k in range(1, rest)]
    parts = gathered(rest_back_kernel, narrow_rows, new_w, *pieces)
    came = [narrow_stage(part, step) for step, part in zip(STEPS, parts)]
    parts = gathered(narrow_back_kernel, wide_rows, sibling_grad, parts[-1], *came)
    came = [wide_stage(part, step) for step, part in zip(STEPS, parts)]
    *came, x_grad = lax.optimization_barrier((*came, along_x(grad)))
    new_m, new_v = call(
        moments_kernel, [shape((rows, width), F32)] * 2,
        first_moment, second_moment, grad, x_grad, sibling_grad, to_sibling(x_grad),
    )
    part = call(functools.partial(wide_back_kernel, rows), [shape((all_rows, half), BF16)], parts[-1], *came)[0]
    other, new_m, new_v = lax.optimization_barrier((to_sibling(part), new_m, new_v))
    out, sem = [shape((all_rows, width), BF16)], [pltpu.SemaphoreType.DMA]
    new_w = call(functools.partial(write_kernel, False), out, part, far_out=1, scratch=sem)[0]
    new_w = call(
        functools.partial(write_kernel, True), out, other, new_w,
        far_in=(1,), far_out=1, scratch=sem, aliases={1: 0},
    )[0]
    return new_w, new_m, new_v


def solution(mesh):
    return jax.shard_map(
        body,
        mesh=mesh,
        in_specs=(
            P(("rep", "shard"), None),
            P(("rep", "shard"), None),
            P("shard", None),
            P("shard", None),
            P("shard", None),
        ),
        out_specs=(P(), P("shard", None), P("shard", None)),
        check_vma=False,
    )
```

```python
import functools

import jax
import jax.numpy as jnp
from jax import lax
from jax.experimental import pallas as pl
from jax.experimental.pallas import tpu as pltpu
from jax.sharding import PartitionSpec as P

F32 = jnp.float32
BF16 = jnp.bfloat16
CHUNK = 512
LOAD_LIMIT = 45 * 1024 * 1024


def adamw_moments(first_moment, second_moment, grad):
    new_first = 0.9 * first_moment + 0.1 * grad
    new_second = 0.999 * second_moment + 0.001 * grad * grad
    return new_first, new_second


def adamw_weight(weight, new_first, new_second):
    corr_one = 0.9999734386011124
    corr_two = 0.0952078528
    wfloat = weight.astype(F32)
    update = new_first / corr_one / (jnp.sqrt(new_second / corr_two) + 1e-08)
    return (wfloat - 0.05 * (update + 0.1 * wfloat)).astype(BF16)


def shape(dims, kind):
    return jax.ShapeDtypeStruct(dims, kind)


def call(kernel, outs, *args, far_in=(), far_out=0, scratch=(), aliases=None, limit=48 * 1024 * 1024):
    near, far = pl.BlockSpec(memory_space=pltpu.VMEM), pl.BlockSpec(memory_space=pltpu.HBM)
    return pl.pallas_call(
        kernel,
        out_shape=outs,
        in_specs=[far if i in tuple(far_in) else near for i in range(len(args))],
        out_specs=[far if i < far_out else near for i in range(len(outs))],
        scratch_shapes=scratch,
        input_output_aliases=aliases or {},
        compiler_params=pltpu.CompilerParams(vmem_limit_bytes=limit),
    )(*args)


def exchange(value, other):
    reps, shards = lax.axis_size("rep"), lax.axis_size("shard")
    pairs = []
    for rep in range(reps):
        for shard in range(shards):
            to_rep, to_shard = other(rep, shard)
            pairs.append((rep * shards + shard, to_rep * shards + to_shard))
    return lax.ppermute(value, ("rep", "shard"), pairs)


def to_sibling(value):
    return exchange(value, lambda rep, shard: (rep ^ 1, shard))


SQUARE = ((1, 1), (1, 0), (0, 1))
LINE = (3, 2, 1)
STEPS = tuple(zip(SQUARE, LINE))
STAY = ((0, 0), 0)


def stage(value, step, square_core):
    (dy, dx), k = step
    return exchange(
        value,
        lambda rep, shard: (rep ^ (2 * dx), shard ^ dy) if rep & 1 == square_core else (rep, shard ^ (2 * k)),
    )


def wide_stage(value, step):
    return stage(value, step, 0)


def narrow_stage(value, step):
    return stage(value, step, 1)


def along_rest(value, k):
    return exchange(value, lambda rep, shard: (rep, shard ^ (8 * k)))


def place():
    rep, shard = lax.axis_index("rep"), lax.axis_index("shard")
    return rep & 1, rep >> 1, shard & 1, (shard >> 1) & 3, shard >> 3


def in_half(step, group):
    core, x, y, z, _ = place()
    (dy, dx), k = step
    first = core == 0
    return (
        jnp.where(first, y ^ dy, group >> 1), jnp.where(first, x ^ dx, group & 1), jnp.where(first, group, z ^ k),
    )


def group_of(step):
    core, x, y, z, _ = place()
    (dy, dx), k = step
    return jnp.where(core == 0, z ^ k, 2 * (y ^ dy) + (x ^ dx))


def block(index, size):
    return pl.ds(pl.multiple_of(index * size, size), size)


def load_kernel(cots_ref, away, kept, sems):
    core = place()[0]
    copies = []
    for out, side in ((away, 1 - core), (kept, core)):
        source = cots_ref.at[:, block(side, out.shape[1])]
        copies.append(pltpu.make_async_copy(source, out, sems.at[len(copies)]))
        copies[-1].start()
    for copy in copies:
        copy.wait()


def turn_kernel(acts, cots, out, turned):
    turned[...] = acts[...].T
    for i in range(out.shape[1] // CHUNK):
        at = slice(i * CHUNK, (i + 1) * CHUNK)
        out[:, at] = jnp.dot(turned[...], cots[:, at], preferred_element_type=F32).astype(BF16)


def product_kernel(turned, cots, out):
    skip = cots.shape[1] - out.shape[1]
    for i in range(out.shape[1] // CHUNK):
        at = slice(i * CHUNK, (i + 1) * CHUNK)
        term = jnp.dot(turned[...], cots[:, skip + i * CHUNK:skip + (i + 1) * CHUNK], preferred_element_type=F32)
        out[:, at] = term.astype(out.dtype)


def wide_kernel(rows, kept, came_low, came_high, own, *pieces):
    quarter = own.shape[1]
    count = own.shape[0] // (4 * rows)
    for step, out in zip((STAY,) + STEPS, (own,) + pieces):
        for group in range(4):
            y, x, z = in_half(step, group)
            cols = block(x, quarter)
            for w in range(count):
                at = block(8 * w + 2 * z + y, rows)
                came = jnp.where(x == 0, came_low[at, :], came_high[at, :])
                total = kept[at, cols] + came.astype(F32)
                to = (group * count + w) * rows
                out[to:to + rows, :] = total.astype(out.dtype)


def narrow_kernel(kept, *refs):
    came, (own, *pieces) = refs[:len(STEPS)], refs[len(STEPS):]
    for step, out in zip((STAY,) + STEPS, [own] + pieces):
        at = block(group_of(step), out.shape[0])
        total = kept[at, :]
        for ref in came:
            total += ref[at, :].astype(F32)
        out[...] = total.astype(out.dtype)


def rest_kernel(kept, *refs):
    came, outs = refs[:len(STEPS)], refs[len(STEPS):]
    w = place()[4]
    for k, out in enumerate(outs):
        at = block(w ^ k, out.shape[0])
        total = kept[at, :]
        for ref in came:
            total += ref[at, :].astype(F32)
        out[...] = total.astype(out.dtype)


def update_kernel(w, m, v, own, *refs):
    pieces, (new_w, grad) = refs[:-2], refs[-2:]
    core, x, _, _, _ = place()
    total = own[...]
    for ref in pieces:
        total += ref[...].astype(F32)
    grad[...] = total.astype(BF16)
    at = block(core * 2 + x, total.shape[1])
    new_m, new_v = adamw_moments(m[:, at], v[:, at], total)
    new_w[...] = adamw_weight(w[:, at], new_m, new_v)


def put(outs, at, value):
    for out in outs:
        out[at, :] = value


def put(outs, at, value):
    for out in outs:
        out[at, :] = value


def rest_back_kernel(*refs):
    pieces, outs = refs[:1 - len(STEPS)], refs[1 - len(STEPS):]
    w = place()[4]
    rows = pieces[0].shape[0]
    for k, ref in enumerate(pieces):
        put(outs, block(w ^ k, rows), ref[...])


def with_gradients_kernel(part, grad, sibling_grad, out):
    core = place()[0]
    size, rows = part.shape[0], grad.shape[0]
    out[:size, :] = part[...]
    out[block(size // rows + core, rows), :] = grad[...]
    out[block(size // rows + 1 - core, rows), :] = sibling_grad[...]


def narrow_back_kernel(own, *refs):
    parts, (*outs, far) = (own,) + refs[:-1 - len(STEPS)], refs[-1 - len(STEPS):]
    size = own.shape[0]
    for step, ref in zip((STAY,) + STEPS, parts):
        put(outs, block(group_of(step), size), ref[:size, :])
    far[...] = parts[-1][size:, :]


def half_blocks(rows, sibling, parts, out):
    core, x, y, z, _ = place()
    first = (core == 0) != sibling
    size, quarter = parts[0].shape
    count = size // (4 * rows)
    for ((dy, dx), k), ref in zip((STAY,) + STEPS, parts):
        for group in range(4):
            to_y = jnp.where(first, y ^ dy, group >> 1)
            to_x = jnp.where(first, x ^ dx, group & 1)
            to_z = jnp.where(first, group, z ^ k)
            for w in range(count):
                at = (group * count + w) * rows
                out[block(8 * w + 2 * to_z + to_y, rows), block(to_x, quarter)] = ref[at:at + rows, :]


def moments_kernel(m, v, grad, sibling_grad, far, sibling_far, new_m, new_v):
    core, x, _, _, _ = place()
    rows, quarter = grad.shape

    def fill(side, to_x, ref, at):
        cols = block(2 * side + to_x, quarter)
        new_m[:, cols], new_v[:, cols] = adamw_moments(m[:, cols], v[:, cols], ref[at, :].astype(F32))

    def fill_far(ref):
        for side in range(2):
            fill(side, 1 - x, ref, pl.ds(side * rows, rows))

    fill(core, x, grad, slice(None))
    fill(1 - core, x, sibling_grad, slice(None))

    @pl.when(core == 1)
    def _():
        fill_far(far)

    @pl.when(core != 1)
    def _():
        fill_far(sibling_far)


def write_kernel(sibling, *refs):
    parts, (out, half, sem) = refs[:1 + len(STEPS)], refs[-3:]
    rows = out.shape[0] // lax.axis_size("shard")
    half_blocks(rows, sibling, parts, half)
    copy = pltpu.make_async_copy(half, out.at[:, block(place()[0] ^ sibling, half.shape[1])], sem)
    copy.start()
    copy.wait()


def body(hidden_acts, out_cotangent, weight, first_moment, second_moment):
    rows, width = weight.shape
    tokens, all_rows = hidden_acts.shape
    half, quarter = width // 2, width // 4
    rest = lax.axis_size("shard") // 8
    wide_rows, narrow_rows = all_rows // 2, all_rows // 8

    away_cots, kept_cots = call(
        load_kernel, [shape((tokens, half), BF16)] * 2, out_cotangent,
        far_in=(0,), scratch=[pltpu.SemaphoreType.DMA((2,))], limit=LOAD_LIMIT,
    )
    low, turned = call(
        turn_kernel, [shape((all_rows, quarter), BF16), shape((all_rows, tokens), BF16)], hidden_acts, away_cots,
    )
    came_low = to_sibling(low)
    came_high = to_sibling(call(product_kernel, [shape((all_rows, quarter), BF16)], turned, away_cots)[0])
    kept = call(product_kernel, [shape((all_rows, half), F32)], turned, kept_cots)[0]

    def split(kernel, size, parts, *args):
        kept, sent = shape((size, quarter), F32), shape((size, quarter), BF16)
        return call(kernel, [kept] + [sent] * (parts - 1), *args)

    own, *pieces = split(functools.partial(wide_kernel, rows), wide_rows, 4, kept, came_low, came_high)
    came = [wide_stage(piece, step) for step, piece in zip(STEPS, pieces)]
    own, *pieces = split(narrow_kernel, narrow_rows, 4, own, *came)
    came = [narrow_stage(piece, step) for step, piece in zip(STEPS, pieces)]
    if rest > 1:
        own, *pieces = split(rest_kernel, rows, rest, own, *came)
        came = [along_rest(piece, k + 1) for k, piece in enumerate(pieces)]
    new_w, grad = call(
        update_kernel, [shape((rows, quarter), BF16)] * 2, weight, first_moment, second_moment, own, *came,
    )

    sibling_grad = to_sibling(grad)
    pieces = [along_rest(new_w, k) for k in range(1, rest)]
    parts = call(rest_back_kernel, [shape((narrow_rows, quarter), BF16)] * (len(STEPS) - 1), new_w, *pieces)
    parts += call(
        with_gradients_kernel, [shape((narrow_rows + 2 * rows, quarter), BF16)], parts[-1], grad, sibling_grad,
    )
    came = [narrow_stage(part, step) for step, part in zip(STEPS, parts)]
    *parts, far = call(
        narrow_back_kernel,
        [shape((wide_rows, quarter), BF16)] * len(STEPS) + [shape((2 * rows, quarter), BF16)], parts[-2], *came,
    )
    came = [wide_stage(part, step) for step, part in zip(STEPS, parts)]
    new_m, new_v = call(
        moments_kernel, [shape((rows, width), F32)] * 2,
        first_moment, second_moment, grad, sibling_grad, far, to_sibling(far),
    )
    came[0], new_m, new_v = lax.optimization_barrier((came[0], new_m, new_v))

    mine = [parts[-1]] + came
    others = [to_sibling(part) for part in mine]
    out = [shape((all_rows, width), BF16)]
    scratch = [pltpu.VMEM((all_rows, half), BF16), pltpu.SemaphoreType.DMA]
    new_w = call(functools.partial(write_kernel, 0), out, *mine, far_out=1, scratch=scratch)[0]
    new_w = call(
        functools.partial(write_kernel, 1), out, *others, new_w,
        far_in=(len(others),), far_out=1, scratch=scratch, aliases={len(others): 0},
    )[0]
    return new_w, new_m, new_v


def solution(mesh):
    return jax.shard_map(
        body,
        mesh=mesh,
        in_specs=(
            P(("rep", "shard"), None),
            P(("rep", "shard"), None),
            P("shard", None),
            P("shard", None),
            P("shard", None),
        ),
        out_specs=(P(), P("shard", None), P("shard", None)),
        check_vma=False,
    )
```

```python
import functools

import jax
import jax.numpy as jnp
from jax import lax
from jax.experimental import pallas as pl
from jax.experimental.pallas import tpu as pltpu
from jax.sharding import PartitionSpec as P

F32 = jnp.float32
BF16 = jnp.bfloat16
CHUNK = 512
LOAD_LIMIT = 48 * 1024 * 1024
KEPT_LIMIT = 50 * 1024 * 1024


def adamw_moments(first_moment, second_moment, grad):
    new_first = 0.9 * first_moment + 0.1 * grad
    new_second = 0.999 * second_moment + 0.001 * grad * grad
    return new_first, new_second


def adamw_weight(weight, new_first, new_second):
    corr_one = 0.9999734386011124
    corr_two = 0.0952078528
    wfloat = weight.astype(F32)
    update = new_first / corr_one / (jnp.sqrt(new_second / corr_two) + 1e-08)
    return (wfloat - 0.05 * (update + 0.1 * wfloat)).astype(BF16)


def shape(dims, kind):
    return jax.ShapeDtypeStruct(dims, kind)


def call(kernel, outs, *args, far_in=(), far_out=0, scratch=(), aliases=None, limit=48 * 1024 * 1024):
    near, far = pl.BlockSpec(memory_space=pltpu.VMEM), pl.BlockSpec(memory_space=pltpu.HBM)
    return pl.pallas_call(
        kernel,
        out_shape=outs,
        in_specs=[far if i in tuple(far_in) else near for i in range(len(args))],
        out_specs=[far if i < far_out else near for i in range(len(outs))],
        scratch_shapes=scratch,
        input_output_aliases=aliases or {},
        compiler_params=pltpu.CompilerParams(vmem_limit_bytes=limit),
    )(*args)


def exchange(value, other):
    reps, shards = lax.axis_size("rep"), lax.axis_size("shard")
    pairs = []
    for rep in range(reps):
        for shard in range(shards):
            to_rep, to_shard = other(rep, shard)
            pairs.append((rep * shards + shard, to_rep * shards + to_shard))
    return lax.ppermute(value, ("rep", "shard"), pairs)


def to_sibling(value):
    return exchange(value, lambda rep, shard: (rep ^ 1, shard))


SQUARE = ((1, 1), (1, 0), (0, 1))
LINE = (3, 2, 1)
STEPS = tuple(zip(SQUARE, LINE))
STAY = ((0, 0), 0)


def stage(value, step, square_core):
    (dy, dx), k = step
    return exchange(
        value,
        lambda rep, shard: (rep ^ (2 * dx), shard ^ dy) if rep & 1 == square_core else (rep, shard ^ (2 * k)),
    )


def wide_stage(value, step):
    return stage(value, step, 0)


def narrow_stage(value, step):
    return stage(value, step, 1)


def along_x(value):
    return exchange(value, lambda rep, shard: (rep ^ 2, shard))


def along_rest(value, k):
    return exchange(value, lambda rep, shard: (rep, shard ^ (8 * k)))


def place():
    rep, shard = lax.axis_index("rep"), lax.axis_index("shard")
    return rep & 1, rep >> 1, shard & 1, (shard >> 1) & 3, shard >> 3


def in_half(step, group):
    core, x, y, z, _ = place()
    (dy, dx), k = step
    first = core == 0
    return (
        jnp.where(first, y ^ dy, group >> 1), jnp.where(first, x ^ dx, group & 1), jnp.where(first, group, z ^ k),
    )


def group_of(step):
    core, x, y, z, _ = place()
    (dy, dx), k = step
    return jnp.where(core == 0, z ^ k, 2 * (y ^ dy) + (x ^ dx))


def block(index, size):
    return pl.ds(pl.multiple_of(index * size, size), size)


def load_kernel(cots_ref, away, first, sems):
    core = place()[0]
    copies = []
    for out, side in ((away, 1 - core), (first, core)):
        at = pl.ds(pl.multiple_of(side * away.shape[1], CHUNK), out.shape[1])
        copies.append(pltpu.make_async_copy(cots_ref.at[:, at], out, sems.at[len(copies)]))
        copies[-1].start()
    for copy in copies:
        copy.wait()


def away_kernel(acts, cots, out, turned):
    turned[...] = acts[...].T
    for i in range(out.shape[1] // CHUNK):
        at = slice(i * CHUNK, (i + 1) * CHUNK)
        out[:, at] = jnp.dot(turned[...], cots[:, at], preferred_element_type=F32).astype(BF16)


def kept_kernel(turned, first, cots_ref, out, cots, sems):
    core = place()[0]
    ready, count = first.shape[1] // CHUNK, out.shape[1] // CHUNK
    copies = []
    for i in range(ready, count):
        source = cots_ref.at[:, block(core * count + i, CHUNK)]
        copies.append(pltpu.make_async_copy(source, cots.at[i - ready], sems.at[i - ready]))
        copies[-1].start()
    for i in range(count):
        at = slice(i * CHUNK, (i + 1) * CHUNK)
        if i >= ready:
            copies[i - ready].wait()
        chunk = cots[i - ready] if i >= ready else first[:, at]
        out[:, at] = jnp.dot(turned[...], chunk, preferred_element_type=F32)


def wide_kernel(rows, kept, came, own, *pieces):
    quarter = own.shape[1]
    count = own.shape[0] // (4 * rows)
    for step, out in zip((STAY,) + STEPS, (own,) + pieces):
        for group in range(4):
            y, x, z = in_half(step, group)
            cols = block(x, quarter)
            for w in range(count):
                at = block(8 * w + 2 * z + y, rows)
                total = kept[at, cols] + came[at, cols].astype(F32)
                to = (group * count + w) * rows
                out[to:to + rows, :] = total.astype(out.dtype)


def narrow_kernel(kept, *refs):
    came, (own, *pieces) = refs[:len(STEPS)], refs[len(STEPS):]
    for step, out in zip((STAY,) + STEPS, [own] + pieces):
        at = block(group_of(step), out.shape[0])
        total = kept[at, :]
        for ref in came:
            total += ref[at, :].astype(F32)
        out[...] = total.astype(out.dtype)


def rest_kernel(kept, *refs):
    came, outs = refs[:len(STEPS)], refs[len(STEPS):]
    w = place()[4]
    for k, out in enumerate(outs):
        at = block(w ^ k, out.shape[0])
        total = kept[at, :]
        for ref in came:
            total += ref[at, :].astype(F32)
        out[...] = total.astype(out.dtype)


def update_kernel(w, m, v, own, *refs):
    pieces, (new_w, grad) = refs[:-2], refs[-2:]
    core, x, _, _, _ = place()
    total = own[...]
    for ref in pieces:
        total += ref[...].astype(F32)
    grad[...] = total.astype(BF16)
    at = block(core * 2 + x, total.shape[1])
    new_m, new_v = adamw_moments(m[:, at], v[:, at], total)
    new_w[...] = adamw_weight(w[:, at], new_m, new_v)


def put(outs, at, value):
    for out in outs:
        out[at, :] = value


def put(outs, at, value):
    for out in outs:
        out[at, :] = value


def rest_back_kernel(*refs):
    pieces, outs = refs[:-len(STEPS)], refs[-len(STEPS):]
    w = place()[4]
    rows = pieces[0].shape[0]
    for k, ref in enumerate(pieces):
        put(outs, block(w ^ k, rows), ref[...])


def narrow_back_kernel(grad, sibling_grad, own, *refs):
    parts, (*outs, grads) = (own,) + refs[:-1 - len(STEPS)], refs[-1 - len(STEPS):]
    size, rows = own.shape[0], grad.shape[0]
    for step, ref in zip((STAY,) + STEPS, parts):
        put(outs, block(group_of(step), size), ref[...])
    core = place()[0]
    grads[block(core, rows), :] = grad[...]
    grads[block(1 - core, rows), :] = sibling_grad[...]


def half_blocks(rows, sibling, parts, out):
    core, x, y, z, _ = place()
    first = (core == 0) != sibling
    size, quarter = parts[0].shape
    count = size // (4 * rows)
    for ((dy, dx), k), ref in zip((STAY,) + STEPS, parts):
        for group in range(4):
            to_y = jnp.where(first, y ^ dy, group >> 1)
            to_x = jnp.where(first, x ^ dx, group & 1)
            to_z = jnp.where(first, group, z ^ k)
            for w in range(count):
                at = (group * count + w) * rows
                out[block(8 * w + 2 * to_z + to_y, rows), block(to_x, quarter)] = ref[at:at + rows, :]


def write_moments(far, grads, m, v, m_out, v_out, new_m, new_v, sems):
    x = place()[1]
    rows, quarter = new_m.shape[1:]
    copies = []
    for side in range(2):
        at = block(2 * side + (x ^ far), quarter)
        grad = grads[side * rows:(side + 1) * rows, :].astype(F32)
        new_m[side], new_v[side] = adamw_moments(m[:, at], v[:, at], grad)
        for source, out in ((new_m, m_out), (new_v, v_out)):
            copies.append(pltpu.make_async_copy(source.at[side], out.at[:, at], sems.at[len(copies)]))
            copies[-1].start()
    return copies


def moments_kernel(m, v, grads, m_out, v_out, *scratch):
    for copy in write_moments(0, grads, m, v, m_out, v_out, *scratch):
        copy.wait()


def write_half(sibling, parts, out, half, sem):
    half_blocks(out.shape[0] // lax.axis_size("shard"), sibling, parts, half)
    copy = pltpu.make_async_copy(half, out.at[:, block(place()[0] ^ sibling, half.shape[1])], sem)
    copy.start()
    return copy


def write_own_kernel(m, v, grads, _m, _v, *refs):
    parts, (m_out, v_out, out, half, sem, *scratch) = refs[:1 + len(STEPS)], refs[1 + len(STEPS):]
    rows = write_half(0, parts, out, half, sem)
    for copy in write_moments(1, grads, m, v, m_out, v_out, *scratch):
        copy.wait()
    rows.wait()


def write_other_kernel(_, *refs):
    parts, (out, half, sem) = refs[:1 + len(STEPS)], refs[1 + len(STEPS):]
    write_half(1, parts, out, half, sem).wait()


def body(hidden_acts, out_cotangent, weight, first_moment, second_moment):
    rows, width = weight.shape
    tokens, all_rows = hidden_acts.shape
    half, quarter = width // 2, width // 4
    rest = lax.axis_size("shard") // 8
    wide_rows, narrow_rows = all_rows // 2, all_rows // 8

    away_cots, first = call(
        load_kernel, [shape((tokens, half), BF16), shape((tokens, quarter), BF16)], out_cotangent,
        far_in=(0,), scratch=[pltpu.SemaphoreType.DMA((2,))], limit=LOAD_LIMIT,
    )
    away, turned = call(
        away_kernel, [shape((all_rows, half), BF16), shape((all_rows, tokens), BF16)], hidden_acts, away_cots,
    )
    came = to_sibling(away)
    later = (half - quarter) // CHUNK
    kept = call(
        kept_kernel, [shape((all_rows, half), F32)], turned, first, out_cotangent,
        far_in=(2,), limit=KEPT_LIMIT,
        scratch=[pltpu.VMEM((later, tokens, CHUNK), BF16), pltpu.SemaphoreType.DMA((later,))],
    )[0]

    def split(kernel, size, parts, *args):
        kept, sent = shape((size, quarter), F32), shape((size, quarter), BF16)
        return call(kernel, [kept] + [sent] * (parts - 1), *args)

    own, *pieces = split(functools.partial(wide_kernel, rows), wide_rows, 4, kept, came)
    came = [wide_stage(piece, step) for step, piece in zip(STEPS, pieces)]
    own, *pieces = split(narrow_kernel, narrow_rows, 4, own, *came)
    came = [narrow_stage(piece, step) for step, piece in zip(STEPS, pieces)]
    if rest > 1:
        own, *pieces = split(rest_kernel, rows, rest, own, *came)
        came = [along_rest(piece, k + 1) for k, piece in enumerate(pieces)]
    new_w, grad = call(
        update_kernel, [shape((rows, quarter), BF16)] * 2, weight, first_moment, second_moment, own, *came,
    )

    sibling_grad = to_sibling(grad)
    pieces = [along_rest(new_w, k) for k in range(1, rest)]
    parts = call(rest_back_kernel, [shape((narrow_rows, quarter), BF16)] * len(STEPS), new_w, *pieces)
    came = [narrow_stage(part, step) for step, part in zip(STEPS, parts)]
    *parts, grads = call(
        narrow_back_kernel,
        [shape((wide_rows, quarter), BF16)] * len(STEPS) + [shape((2 * rows, quarter), BF16)],
        grad, sibling_grad, parts[-1], *came,
    )
    came = [wide_stage(part, step) for step, part in zip(STEPS, parts)]
    far_grads = along_x(grads)
    moments = [shape((rows, width), F32)] * 2
    moments_scratch = [pltpu.VMEM((2, rows, quarter), F32)] * 2 + [pltpu.SemaphoreType.DMA((4,))]
    new_m, new_v = call(
        moments_kernel, moments, first_moment, second_moment, grads, far_out=2, scratch=moments_scratch,
    )
    came[0], far_grads, new_m, new_v = lax.optimization_barrier((came[0], far_grads, new_m, new_v))

    mine = [parts[-1]] + came
    others = [to_sibling(part) for part in mine]
    out = [shape((all_rows, width), BF16)]
    scratch = [pltpu.VMEM((all_rows, half), BF16), pltpu.SemaphoreType.DMA]
    new_m, new_v, new_w = call(
        write_own_kernel, moments + out, first_moment, second_moment, far_grads, new_m, new_v, *mine,
        far_in=(3, 4), far_out=3, scratch=scratch + moments_scratch, aliases={3: 0, 4: 1},
    )
    new_w = call(
        write_other_kernel, out, new_w, *others, far_in=(0,), far_out=1, scratch=scratch, aliases={0: 0},
    )[0]
    return new_w, new_m, new_v


def solution(mesh):
    return jax.shard_map(
        body,
        mesh=mesh,
        in_specs=(
            P(("rep", "shard"), None),
            P(("rep", "shard"), None),
            P("shard", None),
            P("shard", None),
            P("shard", None),
        ),
        out_specs=(P(), P("shard", None), P("shard", None)),
        check_vma=False,
    )
```

```python
import functools

import jax
import jax.numpy as jnp
from jax import lax
from jax.experimental import pallas as pl
from jax.experimental.pallas import tpu as pltpu
from jax.sharding import PartitionSpec as P

F32 = jnp.float32
BF16 = jnp.bfloat16
CHUNK = 512
LOAD_LIMIT = 48 * 1024 * 1024
KEPT_LIMIT = 50 * 1024 * 1024


def adamw_moments(first_moment, second_moment, grad):
    new_first = 0.9 * first_moment + 0.1 * grad
    new_second = 0.999 * second_moment + 0.001 * grad * grad
    return new_first, new_second


def adamw_weight(weight, new_first, new_second):
    corr_one = 0.9999734386011124
    corr_two = 0.0952078528
    wfloat = weight.astype(F32)
    update = new_first / corr_one / (jnp.sqrt(new_second / corr_two) + 1e-08)
    return (wfloat - 0.05 * (update + 0.1 * wfloat)).astype(BF16)


def shape(dims, kind):
    return jax.ShapeDtypeStruct(dims, kind)


def call(kernel, outs, *args, far_in=(), far_out=0, scratch=(), aliases=None, limit=48 * 1024 * 1024):
    near, far = pl.BlockSpec(memory_space=pltpu.VMEM), pl.BlockSpec(memory_space=pltpu.HBM)
    return pl.pallas_call(
        kernel,
        out_shape=outs,
        in_specs=[far if i in tuple(far_in) else near for i in range(len(args))],
        out_specs=[far if i < far_out else near for i in range(len(outs))],
        scratch_shapes=scratch,
        input_output_aliases=aliases or {},
        compiler_params=pltpu.CompilerParams(vmem_limit_bytes=limit),
    )(*args)


def exchange(value, other):
    reps, shards = lax.axis_size("rep"), lax.axis_size("shard")
    pairs = []
    for rep in range(reps):
        for shard in range(shards):
            to_rep, to_shard = other(rep, shard)
            pairs.append((rep * shards + shard, to_rep * shards + to_shard))
    return lax.ppermute(value, ("rep", "shard"), pairs)


def to_sibling(value):
    return exchange(value, lambda rep, shard: (rep ^ 1, shard))


SQUARE = ((1, 1), (1, 0), (0, 1))
LINE = (3, 2, 1)
STEPS = tuple(zip(SQUARE, LINE))
STAY = ((0, 0), 0)


def stage(value, step, square_core):
    (dy, dx), k = step
    return exchange(
        value,
        lambda rep, shard: (rep ^ (2 * dx), shard ^ dy) if rep & 1 == square_core else (rep, shard ^ (2 * k)),
    )


def wide_stage(value, step):
    return stage(value, step, 0)


def narrow_stage(value):
    reps, shards = lax.axis_size("rep"), lax.axis_size("shard")
    groups = []
    for rep in range(0, reps, 2):
        for first in range(0, shards, 8):
            for y in range(2):
                groups.append([rep * shards + first + 2 * z + y for z in range(4)])
    for shard in range(0, shards, 2):
        groups.append([(2 * x + 1) * shards + shard + y for y in range(2) for x in range(2)])
    return lax.all_to_all(value, ("rep", "shard"), 0, 0, axis_index_groups=groups, tiled=True)


def along_x(value):
    return exchange(value, lambda rep, shard: (rep ^ 2, shard))


def along_rest(value, k):
    return exchange(value, lambda rep, shard: (rep, shard ^ (8 * k)))


def place():
    rep, shard = lax.axis_index("rep"), lax.axis_index("shard")
    return rep & 1, rep >> 1, shard & 1, (shard >> 1) & 3, shard >> 3


def in_half(step, group):
    core, x, y, z, _ = place()
    (dy, dx), k = step
    first = core == 0
    return (
        jnp.where(first, y ^ dy, group >> 1), jnp.where(first, x ^ dx, group & 1), jnp.where(first, group, z ^ k),
    )


def own_group():
    core, x, y, z, _ = place()
    return jnp.where(core == 0, z, 2 * y + x)


def block(index, size):
    return pl.ds(pl.multiple_of(index * size, size), size)


def load_kernel(cots_ref, away, first, sems):
    core = place()[0]
    copies = []
    for out, side in ((away, 1 - core), (first, core)):
        at = pl.ds(pl.multiple_of(side * away.shape[1], CHUNK), out.shape[1])
        copies.append(pltpu.make_async_copy(cots_ref.at[:, at], out, sems.at[len(copies)]))
        copies[-1].start()
    for copy in copies:
        copy.wait()


def away_kernel(acts, cots, out, turned):
    turned[...] = acts[...].T
    for i in range(out.shape[1] // CHUNK):
        at = slice(i * CHUNK, (i + 1) * CHUNK)
        out[:, at] = jnp.dot(turned[...], cots[:, at], preferred_element_type=F32).astype(BF16)


def kept_kernel(turned, first, cots_ref, out, cots, sems):
    core = place()[0]
    ready, count = first.shape[1] // CHUNK, out.shape[1] // CHUNK
    copies = []
    for i in range(ready, count):
        source = cots_ref.at[:, block(core * count + i, CHUNK)]
        copies.append(pltpu.make_async_copy(source, cots.at[i - ready], sems.at[i - ready]))
        copies[-1].start()
    for i in range(count):
        at = slice(i * CHUNK, (i + 1) * CHUNK)
        if i >= ready:
            copies[i - ready].wait()
        chunk = cots[i - ready] if i >= ready else first[:, at]
        out[:, at] = jnp.dot(turned[...], chunk, preferred_element_type=F32)


def wide_kernel(rows, kept, came, own, *pieces):
    quarter = own.shape[1]
    count = own.shape[0] // (4 * rows)
    for step, out in zip((STAY,) + STEPS, (own,) + pieces):
        for group in range(4):
            y, x, z = in_half(step, group)
            cols = block(x, quarter)
            for w in range(count):
                at = block(8 * w + 2 * z + y, rows)
                total = kept[at, cols] + came[at, cols].astype(F32)
                to = (group * count + w) * rows
                out[to:to + rows, :] = total.astype(out.dtype)


def narrow_kernel(kept, *refs):
    came, (own, sent) = refs[:len(STEPS)], refs[len(STEPS):]
    total = kept[...]
    for ref in came:
        total += ref[...].astype(F32)
    sent[...] = total.astype(BF16)
    mine = block(own_group(), own.shape[0])
    total = kept[mine, :]
    for ref in came:
        total += ref[mine, :].astype(F32)
    own[...] = total


def narrow_sum(own, came, at):
    size = own.shape[0]
    total = own[at, :]
    for group in range(4):
        term = came[group * size:(group + 1) * size, :] if size == total.shape[0] else came[pl.ds(
            pl.multiple_of(group * size + at.start, total.shape[0]), total.shape[0]), :]
        total += jnp.where(group == own_group(), 0.0, term.astype(F32))
    return total


def rest_kernel(own, came, *outs):
    w = place()[4]
    for k, out in enumerate(outs):
        out[...] = narrow_sum(own, came, block(w ^ k, out.shape[0])).astype(out.dtype)


def update_kernel(summed, w, m, v, own, *refs):
    pieces, (new_w, grad) = refs[:-2], refs[-2:]
    core, x, _, _, _ = place()
    if summed:
        total = own[...]
        for ref in pieces:
            total += ref[...].astype(F32)
    else:
        total = narrow_sum(own, pieces[0], slice(None))
    grad[...] = total.astype(BF16)
    at = block(core * 2 + x, total.shape[1])
    new_m, new_v = adamw_moments(m[:, at], v[:, at], total)
    new_w[...] = adamw_weight(w[:, at], new_m, new_v)


def put(outs, at, value):
    for out in outs:
        out[at, :] = value


def put(outs, at, value):
    for out in outs:
        out[at, :] = value


def rest_back_kernel(*refs):
    pieces, out = refs[:-1], refs[-1]
    w = place()[4]
    rows = pieces[0].shape[0]
    size = rows * lax.axis_size("shard") // 8
    for group in range(4):
        for k, ref in enumerate(pieces):
            out[pl.ds(pl.multiple_of(group * size + (w ^ k) * rows, rows), rows), :] = ref[...]


def narrow_back_kernel(grad, sibling_grad, part, *refs):
    (*outs, grads), rows = refs, grad.shape[0]
    put(outs, slice(None), part[...])
    core = place()[0]
    grads[block(core, rows), :] = grad[...]
    grads[block(1 - core, rows), :] = sibling_grad[...]


def half_blocks(rows, sibling, parts, out):
    core, x, y, z, _ = place()
    first = (core == 0) != sibling
    size, quarter = parts[0].shape
    count = size // (4 * rows)
    for ((dy, dx), k), ref in zip((STAY,) + STEPS, parts):
        for group in range(4):
            to_y = jnp.where(first, y ^ dy, group >> 1)
            to_x = jnp.where(first, x ^ dx, group & 1)
            to_z = jnp.where(first, group, z ^ k)
            for w in range(count):
                at = (group * count + w) * rows
                out[block(8 * w + 2 * to_z + to_y, rows), block(to_x, quarter)] = ref[at:at + rows, :]


def write_moments(far, grads, m, v, m_out, v_out, new_m, new_v, sems):
    x = place()[1]
    rows, quarter = new_m.shape[1:]
    copies = []
    for side in range(2):
        at = block(2 * side + (x ^ far), quarter)
        grad = grads[side * rows:(side + 1) * rows, :].astype(F32)
        new_m[side], new_v[side] = adamw_moments(m[:, at], v[:, at], grad)
        for source, out in ((new_m, m_out), (new_v, v_out)):
            copies.append(pltpu.make_async_copy(source.at[side], out.at[:, at], sems.at[len(copies)]))
            copies[-1].start()
    return copies


def moments_kernel(m, v, grads, m_out, v_out, *scratch):
    for copy in write_moments(0, grads, m, v, m_out, v_out, *scratch):
        copy.wait()


def write_half(sibling, parts, out, half, sem):
    half_blocks(out.shape[0] // lax.axis_size("shard"), sibling, parts, half)
    copy = pltpu.make_async_copy(half, out.at[:, block(place()[0] ^ sibling, half.shape[1])], sem)
    copy.start()
    return copy


def write_own_kernel(m, v, grads, _m, _v, *refs):
    parts, (m_out, v_out, out, half, sem, *scratch) = refs[:1 + len(STEPS)], refs[1 + len(STEPS):]
    rows = write_half(0, parts, out, half, sem)
    for copy in write_moments(1, grads, m, v, m_out, v_out, *scratch):
        copy.wait()
    rows.wait()


def write_other_kernel(_, *refs):
    parts, (out, half, sem) = refs[:1 + len(STEPS)], refs[1 + len(STEPS):]
    write_half(1, parts, out, half, sem).wait()


def body(hidden_acts, out_cotangent, weight, first_moment, second_moment):
    rows, width = weight.shape
    tokens, all_rows = hidden_acts.shape
    half, quarter = width // 2, width // 4
    rest = lax.axis_size("shard") // 8
    wide_rows, narrow_rows = all_rows // 2, all_rows // 8

    away_cots, first = call(
        load_kernel, [shape((tokens, half), BF16), shape((tokens, quarter), BF16)], out_cotangent,
        far_in=(0,), scratch=[pltpu.SemaphoreType.DMA((2,))], limit=LOAD_LIMIT,
    )
    away, turned = call(
        away_kernel, [shape((all_rows, half), BF16), shape((all_rows, tokens), BF16)], hidden_acts, away_cots,
    )
    came = to_sibling(away)
    later = (half - quarter) // CHUNK
    kept = call(
        kept_kernel, [shape((all_rows, half), F32)], turned, first, out_cotangent,
        far_in=(2,), limit=KEPT_LIMIT,
        scratch=[pltpu.VMEM((later, tokens, CHUNK), BF16), pltpu.SemaphoreType.DMA((later,))],
    )[0]

    def split(kernel, size, parts, *args):
        kept, sent = shape((size, quarter), F32), shape((size, quarter), BF16)
        return call(kernel, [kept] + [sent] * (parts - 1), *args)

    own, *pieces = split(functools.partial(wide_kernel, rows), wide_rows, 4, kept, came)
    came = [wide_stage(piece, step) for step, piece in zip(STEPS, pieces)]
    own, sent = call(
        narrow_kernel, [shape((narrow_rows, quarter), F32), shape((wide_rows, quarter), BF16)], own, *came,
    )
    came = [narrow_stage(sent)]
    if rest > 1:
        own, *pieces = split(rest_kernel, rows, rest, own, *came)
        came = [along_rest(piece, k + 1) for k, piece in enumerate(pieces)]
    new_w, grad = call(
        functools.partial(update_kernel, rest > 1), [shape((rows, quarter), BF16)] * 2,
        weight, first_moment, second_moment, own, *came,
    )

    sibling_grad = to_sibling(grad)
    pieces = [along_rest(new_w, k) for k in range(1, rest)]
    part = call(rest_back_kernel, [shape((wide_rows, quarter), BF16)], new_w, *pieces)[0]
    *parts, grads = call(
        narrow_back_kernel,
        [shape((wide_rows, quarter), BF16)] * len(STEPS) + [shape((2 * rows, quarter), BF16)],
        grad, sibling_grad, narrow_stage(part),
    )
    came = [wide_stage(part, step) for step, part in zip(STEPS, parts)]
    far_grads = along_x(grads)
    moments = [shape((rows, width), F32)] * 2
    moments_scratch = [pltpu.VMEM((2, rows, quarter), F32)] * 2 + [pltpu.SemaphoreType.DMA((4,))]
    new_m, new_v = call(
        moments_kernel, moments, first_moment, second_moment, grads, far_out=2, scratch=moments_scratch,
    )
    came[0], far_grads, new_m, new_v = lax.optimization_barrier((came[0], far_grads, new_m, new_v))

    mine = [parts[-1]] + came
    others = [to_sibling(part) for part in mine]
    out = [shape((all_rows, width), BF16)]
    scratch = [pltpu.VMEM((all_rows, half), BF16), pltpu.SemaphoreType.DMA]
    new_m, new_v, new_w = call(
        write_own_kernel, moments + out, first_moment, second_moment, far_grads, new_m, new_v, *mine,
        far_in=(3, 4), far_out=3, scratch=scratch + moments_scratch, aliases={3: 0, 4: 1},
    )
    new_w = call(
        write_other_kernel, out, new_w, *others, far_in=(0,), far_out=1, scratch=scratch, aliases={0: 0},
    )[0]
    return new_w, new_m, new_v


def solution(mesh):
    return jax.shard_map(
        body,
        mesh=mesh,
        in_specs=(
            P(("rep", "shard"), None),
            P(("rep", "shard"), None),
            P("shard", None),
            P("shard", None),
            P("shard", None),
        ),
        out_specs=(P(), P("shard", None), P("shard", None)),
        check_vma=False,
    )
```

```python
import functools

import jax
import jax.numpy as jnp
from jax import lax
from jax.experimental import pallas as pl
from jax.experimental.pallas import tpu as pltpu
from jax.sharding import PartitionSpec as P

F32 = jnp.float32
BF16 = jnp.bfloat16
CHUNK = 512
LOAD_LIMIT = 48 * 1024 * 1024
KEPT_LIMIT = 50 * 1024 * 1024


def adamw_moments(first_moment, second_moment, grad):
    new_first = 0.9 * first_moment + 0.1 * grad
    new_second = 0.999 * second_moment + 0.001 * grad * grad
    return new_first, new_second


def adamw_weight(weight, new_first, new_second):
    corr_one = 0.9999734386011124
    corr_two = 0.0952078528
    wfloat = weight.astype(F32)
    update = new_first / corr_one / (jnp.sqrt(new_second / corr_two) + 1e-08)
    return (wfloat - 0.05 * (update + 0.1 * wfloat)).astype(BF16)


def shape(dims, kind):
    return jax.ShapeDtypeStruct(dims, kind)


def call(kernel, outs, *args, far_in=(), far_out=0, scratch=(), aliases=None, limit=48 * 1024 * 1024):
    near, far = pl.BlockSpec(memory_space=pltpu.VMEM), pl.BlockSpec(memory_space=pltpu.HBM)
    return pl.pallas_call(
        kernel,
        out_shape=outs,
        in_specs=[far if i in tuple(far_in) else near for i in range(len(args))],
        out_specs=[far if i < far_out else near for i in range(len(outs))],
        scratch_shapes=scratch,
        input_output_aliases=aliases or {},
        compiler_params=pltpu.CompilerParams(vmem_limit_bytes=limit),
    )(*args)


def exchange(value, other):
    reps, shards = lax.axis_size("rep"), lax.axis_size("shard")
    pairs = []
    for rep in range(reps):
        for shard in range(shards):
            to_rep, to_shard = other(rep, shard)
            pairs.append((rep * shards + shard, to_rep * shards + to_shard))
    return lax.ppermute(value, ("rep", "shard"), pairs)


def to_sibling(value):
    return exchange(value, lambda rep, shard: (rep ^ 1, shard))


SQUARE = ((1, 1), (1, 0), (0, 1))
LINE = (2, 3, 1)
STEPS = tuple(zip(SQUARE, LINE))
STAY = ((0, 0), 0)


def role_of(rep, shard):
    return (rep ^ (rep >> 1) ^ shard ^ (shard >> 1)) & 1


def partner(rep, shard, dy, dx, k):
    return rep ^ (2 * dx) ^ ((dy ^ dx ^ k) & 1), shard ^ dy ^ (2 * k)


def stage(value, step, square_role):
    (dy, dx), k = step
    return exchange(
        value,
        lambda rep, shard: partner(rep, shard, dy, dx, 0) if role_of(rep, shard) == square_role
        else partner(rep, shard, 0, 0, k),
    )


def wide_stage(value, step):
    return stage(value, step, 0)


def narrow_stage(value, step):
    return stage(value, step, 1)


def along_x(value):
    return exchange(value, lambda rep, shard: partner(rep, shard, 0, 1, 0))


def along_rest(value, k):
    return exchange(value, lambda rep, shard: (rep, shard ^ (8 * k)))


def place():
    rep, shard = lax.axis_index("rep"), lax.axis_index("shard")
    return role_of(rep, shard), rep >> 1, shard & 1, (shard >> 1) & 3, shard >> 3


def in_half(step, group):
    role, x, y, z, _ = place()
    (dy, dx), k = step
    first = role == 0
    return (
        jnp.where(first, y ^ dy, group >> 1), jnp.where(first, x ^ dx, group & 1), jnp.where(first, group, z ^ k),
    )


def group_of(step):
    role, x, y, z, _ = place()
    (dy, dx), k = step
    return jnp.where(role == 0, z ^ k, 2 * (y ^ dy) + (x ^ dx))


def block(index, size):
    return pl.ds(pl.multiple_of(index * size, size), size)


def load_kernel(cots_ref, away, first, sems):
    role = place()[0]
    copies = []
    for out, side in ((away, 1 - role), (first, role)):
        at = pl.ds(pl.multiple_of(side * away.shape[1], CHUNK), out.shape[1])
        copies.append(pltpu.make_async_copy(cots_ref.at[:, at], out, sems.at[len(copies)]))
        copies[-1].start()
    for copy in copies:
        copy.wait()


def away_kernel(acts, cots, out, turned):
    turned[...] = acts[...].T
    for i in range(out.shape[1] // CHUNK):
        at = slice(i * CHUNK, (i + 1) * CHUNK)
        out[:, at] = jnp.dot(turned[...], cots[:, at], preferred_element_type=F32).astype(BF16)


def kept_kernel(turned, first, cots_ref, out, cots, sems):
    role = place()[0]
    ready, count = first.shape[1] // CHUNK, out.shape[1] // CHUNK
    copies = []
    for i in range(ready, count):
        source = cots_ref.at[:, block(role * count + i, CHUNK)]
        copies.append(pltpu.make_async_copy(source, cots.at[i - ready], sems.at[i - ready]))
        copies[-1].start()
    for i in range(count):
        at = slice(i * CHUNK, (i + 1) * CHUNK)
        if i >= ready:
            copies[i - ready].wait()
        chunk = cots[i - ready] if i >= ready else first[:, at]
        out[:, at] = jnp.dot(turned[...], chunk, preferred_element_type=F32)


def wide_kernel(rows, kept, came, own, *pieces):
    quarter = own.shape[1]
    count = own.shape[0] // (4 * rows)
    for step, out in zip((STAY,) + STEPS, (own,) + pieces):
        for group in range(4):
            y, x, z = in_half(step, group)
            cols = block(x, quarter)
            for w in range(count):
                at = block(8 * w + 2 * z + y, rows)
                total = kept[at, cols] + came[at, cols].astype(F32)
                to = (group * count + w) * rows
                out[to:to + rows, :] = total.astype(out.dtype)


def narrow_kernel(kept, *refs):
    came, (own, *pieces) = refs[:len(STEPS)], refs[len(STEPS):]
    for step, out in zip((STAY,) + STEPS, [own] + pieces):
        at = block(group_of(step), out.shape[0])
        total = kept[at, :]
        for ref in came:
            total += ref[at, :].astype(F32)
        out[...] = total.astype(out.dtype)


def rest_kernel(kept, *refs):
    came, outs = refs[:len(STEPS)], refs[len(STEPS):]
    w = place()[4]
    for k, out in enumerate(outs):
        at = block(w ^ k, out.shape[0])
        total = kept[at, :]
        for ref in came:
            total += ref[at, :].astype(F32)
        out[...] = total.astype(out.dtype)


def update_kernel(w, m, v, own, *refs):
    pieces, (new_w, grad) = refs[:-2], refs[-2:]
    role, x, _, _, _ = place()
    total = own[...]
    for ref in pieces:
        total += ref[...].astype(F32)
    grad[...] = total.astype(BF16)
    at = block(role * 2 + x, total.shape[1])
    new_m, new_v = adamw_moments(m[:, at], v[:, at], total)
    new_w[...] = adamw_weight(w[:, at], new_m, new_v)


def put(outs, at, value):
    for out in outs:
        out[at, :] = value


def put(outs, at, value):
    for out in outs:
        out[at, :] = value


def rest_back_kernel(*refs):
    pieces, outs = refs[:-len(STEPS)], refs[-len(STEPS):]
    w = place()[4]
    rows = pieces[0].shape[0]
    for k, ref in enumerate(pieces):
        put(outs, block(w ^ k, rows), ref[...])


def narrow_back_kernel(grad, sibling_grad, own, *refs):
    parts, (*outs, grads) = (own,) + refs[:-1 - len(STEPS)], refs[-1 - len(STEPS):]
    size, rows = own.shape[0], grad.shape[0]
    for step, ref in zip((STAY,) + STEPS, parts):
        put(outs, block(group_of(step), size), ref[...])
    role = place()[0]
    grads[block(role, rows), :] = grad[...]
    grads[block(1 - role, rows), :] = sibling_grad[...]


def half_blocks(rows, sibling, parts, out):
    role, x, y, z, _ = place()
    first = (role == 0) != sibling
    size, quarter = parts[0].shape
    count = size // (4 * rows)
    for ((dy, dx), k), ref in zip((STAY,) + STEPS, parts):
        for group in range(4):
            to_y = jnp.where(first, y ^ dy, group >> 1)
            to_x = jnp.where(first, x ^ dx, group & 1)
            to_z = jnp.where(first, group, z ^ k)
            for w in range(count):
                at = (group * count + w) * rows
                out[block(8 * w + 2 * to_z + to_y, rows), block(to_x, quarter)] = ref[at:at + rows, :]


def write_moments(far, grads, m, v, m_out, v_out, new_m, new_v, sems):
    x = place()[1]
    rows, quarter = new_m.shape[1:]
    copies = []
    for side in range(2):
        at = block(2 * side + (x ^ far), quarter)
        grad = grads[side * rows:(side + 1) * rows, :].astype(F32)
        new_m[side], new_v[side] = adamw_moments(m[:, at], v[:, at], grad)
        for source, out in ((new_m, m_out), (new_v, v_out)):
            copies.append(pltpu.make_async_copy(source.at[side], out.at[:, at], sems.at[len(copies)]))
            copies[-1].start()
    return copies


def moments_kernel(m, v, grads, m_out, v_out, *scratch):
    for copy in write_moments(0, grads, m, v, m_out, v_out, *scratch):
        copy.wait()


def write_half(sibling, parts, out, half, sem):
    half_blocks(out.shape[0] // lax.axis_size("shard"), sibling, parts, half)
    copy = pltpu.make_async_copy(half, out.at[:, block(place()[0] ^ sibling, half.shape[1])], sem)
    copy.start()
    return copy


def write_own_kernel(m, v, grads, _m, _v, *refs):
    parts, (m_out, v_out, out, half, sem, *scratch) = refs[:1 + len(STEPS)], refs[1 + len(STEPS):]
    rows = write_half(0, parts, out, half, sem)
    for copy in write_moments(1, grads, m, v, m_out, v_out, *scratch):
        copy.wait()
    rows.wait()


def pack_kernel(*refs):
    *parts, out = refs
    size = parts[0].shape[0]
    for i, ref in enumerate(parts):
        out[i * size:(i + 1) * size, :] = ref[...]


def write_other_kernel(_, own, others, out, half, sem):
    size = own.shape[0]
    parts = [own] + [others.at[pl.ds(i * size, size), :] for i in range(len(STEPS))]
    write_half(1, parts, out, half, sem).wait()


def body(hidden_acts, out_cotangent, weight, first_moment, second_moment):
    rows, width = weight.shape
    tokens, all_rows = hidden_acts.shape
    half, quarter = width // 2, width // 4
    rest = lax.axis_size("shard") // 8
    wide_rows, narrow_rows = all_rows // 2, all_rows // 8

    away_cots, first = call(
        load_kernel, [shape((tokens, half), BF16), shape((tokens, quarter), BF16)], out_cotangent,
        far_in=(0,), scratch=[pltpu.SemaphoreType.DMA((2,))], limit=LOAD_LIMIT,
    )
    away, turned = call(
        away_kernel, [shape((all_rows, half), BF16), shape((all_rows, tokens), BF16)], hidden_acts, away_cots,
    )
    came = to_sibling(away)
    later = (half - quarter) // CHUNK
    kept = call(
        kept_kernel, [shape((all_rows, half), F32)], turned, first, out_cotangent,
        far_in=(2,), limit=KEPT_LIMIT,
        scratch=[pltpu.VMEM((later, tokens, CHUNK), BF16), pltpu.SemaphoreType.DMA((later,))],
    )[0]

    def split(kernel, size, parts, *args):
        kept, sent = shape((size, quarter), F32), shape((size, quarter), BF16)
        return call(kernel, [kept] + [sent] * (parts - 1), *args)

    own, *pieces = split(functools.partial(wide_kernel, rows), wide_rows, 4, kept, came)
    came = [wide_stage(piece, step) for step, piece in zip(STEPS, pieces)]
    own, *pieces = split(narrow_kernel, narrow_rows, 4, own, *came)
    came = [narrow_stage(piece, step) for step, piece in zip(STEPS, pieces)]
    if rest > 1:
        own, *pieces = split(rest_kernel, rows, rest, own, *came)
        came = [along_rest(piece, k + 1) for k, piece in enumerate(pieces)]
    new_w, grad = call(
        update_kernel, [shape((rows, quarter), BF16)] * 2, weight, first_moment, second_moment, own, *came,
    )

    sibling_grad = to_sibling(grad)
    pieces = [along_rest(new_w, k) for k in range(1, rest)]
    parts = call(rest_back_kernel, [shape((narrow_rows, quarter), BF16)] * len(STEPS), new_w, *pieces)
    came = [narrow_stage(part, step) for step, part in zip(STEPS, parts)]
    *parts, grads = call(
        narrow_back_kernel,
        [shape((wide_rows, quarter), BF16)] * len(STEPS) + [shape((2 * rows, quarter), BF16)],
        grad, sibling_grad, parts[-1], *came,
    )
    came = [wide_stage(part, step) for step, part in zip(STEPS, parts)]
    far_grads = along_x(grads)
    moments = [shape((rows, width), F32)] * 2
    moments_scratch = [pltpu.VMEM((2, rows, quarter), F32)] * 2 + [pltpu.SemaphoreType.DMA((4,))]
    new_m, new_v = call(
        moments_kernel, moments, first_moment, second_moment, grads, far_out=2, scratch=moments_scratch,
    )
    came[0], far_grads, new_m, new_v = lax.optimization_barrier((came[0], far_grads, new_m, new_v))

    mine = [parts[-1]] + came
    landed = call(pack_kernel, [shape((len(STEPS) * wide_rows, quarter), BF16)], *came)[0]
    others = [to_sibling(parts[-1]), to_sibling(landed)]
    out = [shape((all_rows, width), BF16)]
    scratch = [pltpu.VMEM((all_rows, half), BF16), pltpu.SemaphoreType.DMA]
    new_m, new_v, new_w = call(
        write_own_kernel, moments + out, first_moment, second_moment, far_grads, new_m, new_v, *mine,
        far_in=(3, 4), far_out=3, scratch=scratch + moments_scratch, aliases={3: 0, 4: 1},
    )
    new_w = call(
        write_other_kernel, out, new_w, *others, far_in=(0,), far_out=1, scratch=scratch, aliases={0: 0},
    )[0]
    return new_w, new_m, new_v


def solution(mesh):
    return jax.shard_map(
        body,
        mesh=mesh,
        in_specs=(
            P(("rep", "shard"), None),
            P(("rep", "shard"), None),
            P("shard", None),
            P("shard", None),
            P("shard", None),
        ),
        out_specs=(P(), P("shard", None), P("shard", None)),
        check_vma=False,
    )
```

```python
import functools

import jax
import jax.numpy as jnp
from jax import lax
from jax.experimental import pallas as pl
from jax.experimental.pallas import tpu as pltpu
from jax.sharding import PartitionSpec as P

F32 = jnp.float32
BF16 = jnp.bfloat16
CHUNK = 512
LOAD_LIMIT = 48 * 1024 * 1024
KEPT_LIMIT = 50 * 1024 * 1024


def adamw_moments(first_moment, second_moment, grad):
    new_first = 0.9 * first_moment + 0.1 * grad
    new_second = 0.999 * second_moment + 0.001 * grad * grad
    return new_first, new_second


def adamw_weight(weight, new_first, new_second):
    corr_one = 0.9999734386011124
    corr_two = 0.0952078528
    wfloat = weight.astype(F32)
    update = new_first / corr_one / (jnp.sqrt(new_second / corr_two) + 1e-08)
    return (wfloat - 0.05 * (update + 0.1 * wfloat)).astype(BF16)


def shape(dims, kind):
    return jax.ShapeDtypeStruct(dims, kind)


def call(kernel, outs, *args, far_in=(), far_out=0, scratch=(), aliases=None, limit=48 * 1024 * 1024):
    near, far = pl.BlockSpec(memory_space=pltpu.VMEM), pl.BlockSpec(memory_space=pltpu.HBM)
    return pl.pallas_call(
        kernel,
        out_shape=outs,
        in_specs=[far if i in tuple(far_in) else near for i in range(len(args))],
        out_specs=[far if i < far_out else near for i in range(len(outs))],
        scratch_shapes=scratch,
        input_output_aliases=aliases or {},
        compiler_params=pltpu.CompilerParams(vmem_limit_bytes=limit),
    )(*args)


def exchange(value, other):
    reps, shards = lax.axis_size("rep"), lax.axis_size("shard")
    pairs = []
    for rep in range(reps):
        for shard in range(shards):
            to_rep, to_shard = other(rep, shard)
            pairs.append((rep * shards + shard, to_rep * shards + to_shard))
    return lax.ppermute(value, ("rep", "shard"), pairs)


def to_sibling(value):
    return exchange(value, lambda rep, shard: (rep ^ 1, shard))


SQUARE = ((1, 1), (1, 0), (0, 1))
LINE = (2, 3, 1)
STEPS = tuple(zip(SQUARE, LINE))
STAY = ((0, 0), 0)


def role_of(rep, shard):
    return (rep ^ (rep >> 1) ^ shard ^ (shard >> 1)) & 1


def partner(rep, shard, dy, dx, k):
    return rep ^ (2 * dx) ^ ((dy ^ dx ^ k) & 1), shard ^ dy ^ (2 * k)


def stage(value, step, square_role):
    (dy, dx), k = step
    return exchange(
        value,
        lambda rep, shard: partner(rep, shard, dy, dx, 0) if role_of(rep, shard) == square_role
        else partner(rep, shard, 0, 0, k),
    )


def along_x(value):
    return exchange(value, lambda rep, shard: partner(rep, shard, 0, 1, 0))


def along_rest(value, k):
    return exchange(value, lambda rep, shard: (rep, shard ^ (8 * k)))


def place():
    rep, shard = lax.axis_index("rep"), lax.axis_index("shard")
    return role_of(rep, shard), rep >> 1, shard & 1, (shard >> 1) & 3, shard >> 3


def in_half(step, group):
    role, x, y, z, _ = place()
    (dy, dx), k = step
    first = role == 0
    return (
        jnp.where(first, y ^ dy, group >> 1), jnp.where(first, x ^ dx, group & 1), jnp.where(first, group, z ^ k),
    )


def group_of(step, line_role):
    role, x, y, z, _ = place()
    (dy, dx), k = step
    return jnp.where(role == line_role, z ^ k, 2 * (y ^ dy) + (x ^ dx))


def block(index, size):
    return pl.ds(pl.multiple_of(index * size, size), size)


def load_kernel(cots_ref, away, first, sems):
    role = place()[0]
    copies = []
    for out, side in ((away, 1 - role), (first, role)):
        at = pl.ds(pl.multiple_of(side * away.shape[1], CHUNK), out.shape[1])
        copies.append(pltpu.make_async_copy(cots_ref.at[:, at], out, sems.at[len(copies)]))
        copies[-1].start()
    for copy in copies:
        copy.wait()


def away_kernel(acts, cots, out, turned):
    turned[...] = acts[...].T
    for i in range(out.shape[1] // CHUNK):
        at = slice(i * CHUNK, (i + 1) * CHUNK)
        out[:, at] = jnp.dot(turned[...], cots[:, at], preferred_element_type=F32).astype(BF16)


def kept_kernel(turned, first, cots_ref, out, cots, sems):
    role = place()[0]
    ready, count = first.shape[1] // CHUNK, out.shape[1] // CHUNK
    copies = []
    for i in range(ready, count):
        source = cots_ref.at[:, block(role * count + i, CHUNK)]
        copies.append(pltpu.make_async_copy(source, cots.at[i - ready], sems.at[i - ready]))
        copies[-1].start()
    for i in range(count):
        at = slice(i * CHUNK, (i + 1) * CHUNK)
        if i >= ready:
            copies[i - ready].wait()
        chunk = cots[i - ready] if i >= ready else first[:, at]
        out[:, at] = jnp.dot(turned[...], chunk, preferred_element_type=F32)


def wide_kernel(rows, kept, came, own, *pieces):
    quarter = own.shape[1]
    count = own.shape[0] // (4 * rows)
    for step, out in zip((STAY,) + STEPS, (own,) + pieces):
        for group in range(4):
            y, x, z = in_half(step, group)
            cols = block(x, quarter)
            for w in range(count):
                at = block(8 * w + 2 * z + y, rows)
                total = kept[at, cols] + came[at, cols].astype(F32)
                to = (group * count + w) * rows
                out[to:to + rows, :] = total.astype(out.dtype)


def narrow_kernel(kept, *refs):
    came, (own, *pieces) = refs[:len(STEPS)], refs[len(STEPS):]
    for step, out in zip((STAY,) + STEPS, [own] + pieces):
        at = block(group_of(step, 0), out.shape[0])
        total = kept[at, :]
        for ref in came:
            total += ref[at, :].astype(F32)
        out[...] = total.astype(out.dtype)


def rest_kernel(kept, *refs):
    came, outs = refs[:len(STEPS)], refs[len(STEPS):]
    w = place()[4]
    for k, out in enumerate(outs):
        at = block(w ^ k, out.shape[0])
        total = kept[at, :]
        for ref in came:
            total += ref[at, :].astype(F32)
        out[...] = total.astype(out.dtype)


def update_kernel(w, m, v, own, *refs):
    pieces, (new_w, grad) = refs[:-2], refs[-2:]
    role, x, _, _, _ = place()
    total = own[...]
    for ref in pieces:
        total += ref[...].astype(F32)
    grad[...] = total.astype(BF16)
    at = block(role * 2 + x, total.shape[1])
    new_m, new_v = adamw_moments(m[:, at], v[:, at], total)
    new_w[...] = adamw_weight(w[:, at], new_m, new_v)


def put(outs, at, value):
    for out in outs:
        out[at, :] = value


def put(outs, at, value):
    for out in outs:
        out[at, :] = value


def rest_back_kernel(*refs):
    pieces, outs = refs[:-len(STEPS)], refs[-len(STEPS):]
    w = place()[4]
    rows = pieces[0].shape[0]
    for k, ref in enumerate(pieces):
        put(outs, block(w ^ k, rows), ref[...])


def narrow_back_kernel(own, *refs):
    parts, outs = (own,) + refs[:-len(STEPS)], refs[-len(STEPS):]
    for step, ref in zip((STAY,) + STEPS, parts):
        put(outs, block(group_of(step, 1), own.shape[0]), ref[...])


def half_blocks(sibling, parts, out):
    role, x, y, z, _ = place()
    square = (role == 1) != sibling
    size, quarter = parts[0].shape
    rows = out.shape[0] // lax.axis_size("shard")
    count = size // (4 * rows)
    for ((dy, dx), k), ref in zip((STAY,) + STEPS, parts):
        for group in range(4):
            to_y = jnp.where(square, y ^ dy, group >> 1)
            to_x = jnp.where(square, x ^ dx, group & 1)
            to_z = jnp.where(square, group, z ^ k)
            for w in range(count):
                at = (group * count + w) * rows
                out[block(8 * w + 2 * to_z + to_y, rows), block(to_x, quarter)] = ref[at:at + rows, :]


def write(sibling, parts, grads, m, v, w_out, m_out, v_out, half, new_m, new_v, sems):
    role, x, _, _, _ = place()
    side = role ^ sibling
    half_blocks(sibling, parts, half)
    copies = [pltpu.make_async_copy(half, w_out.at[:, block(side, half.shape[1])], sems.at[0])]
    copies[0].start()
    for far, grad in enumerate(grads):
        at = block(2 * side + (x ^ far), grad.shape[1])
        new_m[far], new_v[far] = adamw_moments(m[:, at], v[:, at], grad[...].astype(F32))
        for source, out in ((new_m, m_out), (new_v, v_out)):
            copies.append(pltpu.make_async_copy(source.at[far], out.at[:, at], sems.at[len(copies)]))
            copies[-1].start()
    for copy in copies:
        copy.wait()


def pack_kernel(*refs):
    *parts, _, out = refs
    at = 0
    for ref in parts:
        out[at:at + ref.shape[0], :] = ref[...]
        at += ref.shape[0]


def write_own_kernel(m, v, grad, far_grad, *refs):
    parts, refs = refs[:1 + len(STEPS)], refs[1 + len(STEPS):]
    write(0, parts, (grad, far_grad), m, v, *refs)


def write_other_kernel(m, v, own, landed, _w, _m, _v, *refs):
    size, rows = own.shape[0], m.shape[0]
    sizes = [size] * len(STEPS) + [rows] * 2
    parts, at = [], 0
    for count in sizes:
        parts.append(landed.at[pl.ds(at, count), :])
        at += count
    write(1, [own] + parts[:len(STEPS)], parts[len(STEPS):], m, v, *refs)


def body(hidden_acts, out_cotangent, weight, first_moment, second_moment):
    rows, width = weight.shape
    tokens, all_rows = hidden_acts.shape
    half, quarter = width // 2, width // 4
    rest = lax.axis_size("shard") // 8
    wide_rows, narrow_rows = all_rows // 2, all_rows // 8

    away_cots, first = call(
        load_kernel, [shape((tokens, half), BF16), shape((tokens, quarter), BF16)], out_cotangent,
        far_in=(0,), scratch=[pltpu.SemaphoreType.DMA((2,))], limit=LOAD_LIMIT,
    )
    away, turned = call(
        away_kernel, [shape((all_rows, half), BF16), shape((all_rows, tokens), BF16)], hidden_acts, away_cots,
    )
    came = to_sibling(away)
    later = (half - quarter) // CHUNK
    kept = call(
        kept_kernel, [shape((all_rows, half), F32)], turned, first, out_cotangent,
        far_in=(2,), limit=KEPT_LIMIT,
        scratch=[pltpu.VMEM((later, tokens, CHUNK), BF16), pltpu.SemaphoreType.DMA((later,))],
    )[0]

    def split(kernel, size, parts, *args):
        kept, sent = shape((size, quarter), F32), shape((size, quarter), BF16)
        return call(kernel, [kept] + [sent] * (parts - 1), *args)

    own, *pieces = split(functools.partial(wide_kernel, rows), wide_rows, 4, kept, came)
    came = [stage(piece, step, 0) for step, piece in zip(STEPS, pieces)]
    own, *pieces = split(narrow_kernel, narrow_rows, 4, own, *came)
    came = [stage(piece, step, 1) for step, piece in zip(STEPS, pieces)]
    if rest > 1:
        own, *pieces = split(rest_kernel, rows, rest, own, *came)
        came = [along_rest(piece, k + 1) for k, piece in enumerate(pieces)]
    new_w, grad = call(
        update_kernel, [shape((rows, quarter), BF16)] * 2, weight, first_moment, second_moment, own, *came,
    )

    pieces = [along_rest(new_w, k) for k in range(1, rest)]
    parts = call(rest_back_kernel, [shape((narrow_rows, quarter), BF16)] * len(STEPS), new_w, *pieces)
    came = [stage(part, step, 0) for step, part in zip(STEPS, parts)]
    parts = call(narrow_back_kernel, [shape((wide_rows, quarter), BF16)] * len(STEPS), parts[-1], *came)
    came = [stage(part, step, 1) for step, part in zip(STEPS, parts)]
    far_grad, own = along_x(grad), to_sibling(parts[-1])
    came[0], far_grad = lax.optimization_barrier((came[0], far_grad))

    landed = to_sibling(call(
        pack_kernel, [shape((len(STEPS) * wide_rows + 2 * rows, quarter), BF16)], *came, grad, far_grad, own,
    )[0])
    outs = [shape((all_rows, width), BF16), shape((rows, width), F32), shape((rows, width), F32)]
    scratch = [pltpu.VMEM((all_rows, half), BF16)] + [pltpu.VMEM((2, rows, quarter), F32)] * 2
    scratch += [pltpu.SemaphoreType.DMA((5,))]
    written = call(
        write_own_kernel, outs, first_moment, second_moment, grad, far_grad, parts[-1], *came,
        far_out=3, scratch=scratch,
    )
    return tuple(call(
        write_other_kernel, outs, first_moment, second_moment, own, landed, *written,
        far_in=(4, 5, 6), far_out=3, scratch=scratch, aliases={4: 0, 5: 1, 6: 2},
    ))


def solution(mesh):
    return jax.shard_map(
        body,
        mesh=mesh,
        in_specs=(
            P(("rep", "shard"), None),
            P(("rep", "shard"), None),
            P("shard", None),
            P("shard", None),
            P("shard", None),
        ),
        out_specs=(P(), P("shard", None), P("shard", None)),
        check_vma=False,
    )
```

```python
import functools

import jax
import jax.numpy as jnp
from jax import lax
from jax.experimental import pallas as pl
from jax.experimental.pallas import tpu as pltpu
from jax.sharding import PartitionSpec as P

F32 = jnp.float32
BF16 = jnp.bfloat16
CHUNK = 512
PARTS = 4
LOAD_LIMIT = 48 * 1024 * 1024
KEPT_LIMIT = 50 * 1024 * 1024


def adamw_moments(first_moment, second_moment, grad):
    new_first = 0.9 * first_moment + 0.1 * grad
    new_second = 0.999 * second_moment + 0.001 * grad * grad
    return new_first, new_second


def adamw_weight(weight, new_first, new_second):
    corr_one = 0.9999734386011124
    corr_two = 0.0952078528
    wfloat = weight.astype(F32)
    update = new_first / corr_one / (jnp.sqrt(new_second / corr_two) + 1e-08)
    return (wfloat - 0.05 * (update + 0.1 * wfloat)).astype(BF16)


def shape(dims, kind):
    return jax.ShapeDtypeStruct(dims, kind)


def call(kernel, outs, *args, far_in=(), far_out=0, scratch=(), aliases=None, limit=48 * 1024 * 1024):
    near, far = pl.BlockSpec(memory_space=pltpu.VMEM), pl.BlockSpec(memory_space=pltpu.HBM)
    return pl.pallas_call(
        kernel,
        out_shape=outs,
        in_specs=[far if i in tuple(far_in) else near for i in range(len(args))],
        out_specs=[far if i < far_out else near for i in range(len(outs))],
        scratch_shapes=scratch,
        input_output_aliases=aliases or {},
        compiler_params=pltpu.CompilerParams(vmem_limit_bytes=limit),
    )(*args)


def exchange(value, other):
    reps, shards = lax.axis_size("rep"), lax.axis_size("shard")
    pairs = []
    for rep in range(reps):
        for shard in range(shards):
            to_rep, to_shard = other(rep, shard)
            pairs.append((rep * shards + shard, to_rep * shards + to_shard))
    return lax.ppermute(value, ("rep", "shard"), pairs)


def to_sibling(value):
    return exchange(value, lambda rep, shard: (rep ^ 1, shard))


SQUARE = ((1, 1), (1, 0), (0, 1))
LINE = (2, 3, 1)
STEPS = tuple(zip(SQUARE, LINE))
STAY = ((0, 0), 0)


def role_of(rep, shard):
    return (rep ^ (rep >> 1) ^ shard ^ (shard >> 1)) & 1


def partner(rep, shard, dy, dx, k):
    return rep ^ (2 * dx) ^ ((dy ^ dx ^ k) & 1), shard ^ dy ^ (2 * k)


def stage(value, step, square_role):
    (dy, dx), k = step
    return exchange(
        value,
        lambda rep, shard: partner(rep, shard, dy, dx, 0) if role_of(rep, shard) == square_role
        else partner(rep, shard, 0, 0, k),
    )


def along_x(value):
    return exchange(value, lambda rep, shard: partner(rep, shard, 0, 1, 0))


def along_rest(value, k):
    return exchange(value, lambda rep, shard: (rep, shard ^ (8 * k)))


def place():
    rep, shard = lax.axis_index("rep"), lax.axis_index("shard")
    return role_of(rep, shard), rep >> 1, shard & 1, (shard >> 1) & 3, shard >> 3


def in_half(step, group):
    role, x, y, z, _ = place()
    (dy, dx), k = step
    first = role == 0
    return (
        jnp.where(first, y ^ dy, group >> 1), jnp.where(first, x ^ dx, group & 1), jnp.where(first, group, z ^ k),
    )


def group_of(step, line_role):
    role, x, y, z, _ = place()
    (dy, dx), k = step
    return jnp.where(role == line_role, z ^ k, 2 * (y ^ dy) + (x ^ dx))


def block(index, size):
    return pl.ds(pl.multiple_of(index * size, size), size)


def in_parts(source, out, sems, copies):
    rows = out.shape[0] // PARTS
    for i in range(PARTS):
        at = pl.ds(i * rows, rows)
        copies.append(pltpu.make_async_copy(source.at[at, :], out.at[at, :], sems.at[len(copies)]))
        copies[-1].start()


def load_kernel(cots_ref, away, first, sems):
    role = place()[0]
    copies = []
    for out, side in ((away, 1 - role), (first, role)):
        at = pl.ds(pl.multiple_of(side * away.shape[1], CHUNK), out.shape[1])
        in_parts(cots_ref.at[:, at], out, sems, copies)
    for copy in copies:
        copy.wait()


def away_kernel(acts, cots, out, turned):
    turned[...] = acts[...].T
    for i in range(out.shape[1] // CHUNK):
        at = slice(i * CHUNK, (i + 1) * CHUNK)
        out[:, at] = jnp.dot(turned[...], cots[:, at], preferred_element_type=F32).astype(BF16)


def kept_kernel(turned, first, cots_ref, out, cots, sems):
    role = place()[0]
    skip, later = first.shape[1], cots.shape[1]
    copies = []
    at = pl.ds(pl.multiple_of(role * out.shape[1] + skip, CHUNK), later)
    in_parts(cots_ref.at[:, at], cots, sems, copies)
    for i in range(skip // CHUNK):
        at = slice(i * CHUNK, (i + 1) * CHUNK)
        out[:, at] = jnp.dot(turned[...], first[:, at], preferred_element_type=F32)
    for copy in copies:
        copy.wait()
    for i in range(later // CHUNK):
        at = slice(i * CHUNK, (i + 1) * CHUNK)
        out[:, skip + i * CHUNK:skip + (i + 1) * CHUNK] = jnp.dot(
            turned[...], cots[:, at], preferred_element_type=F32)


def wide_kernel(rows, kept, came, own, *pieces):
    quarter = own.shape[1]
    count = own.shape[0] // (4 * rows)
    for step, out in zip((STAY,) + STEPS, (own,) + pieces):
        for group in range(4):
            y, x, z = in_half(step, group)
            cols = block(x, quarter)
            for w in range(count):
                at = block(8 * w + 2 * z + y, rows)
                total = kept[at, cols] + came[at, cols].astype(F32)
                to = (group * count + w) * rows
                out[to:to + rows, :] = total.astype(out.dtype)


def narrow_kernel(kept, *refs):
    came, (own, *pieces) = refs[:len(STEPS)], refs[len(STEPS):]
    for step, out in zip((STAY,) + STEPS, [own] + pieces):
        at = block(group_of(step, 0), out.shape[0])
        total = kept[at, :]
        for ref in came:
            total += ref[at, :].astype(F32)
        out[...] = total.astype(out.dtype)


def rest_kernel(kept, *refs):
    came, outs = refs[:len(STEPS)], refs[len(STEPS):]
    w = place()[4]
    for k, out in enumerate(outs):
        at = block(w ^ k, out.shape[0])
        total = kept[at, :]
        for ref in came:
            total += ref[at, :].astype(F32)
        out[...] = total.astype(out.dtype)


def update_kernel(w, m, v, own, *refs):
    pieces, (new_w, grad) = refs[:-2], refs[-2:]
    role, x, _, _, _ = place()
    total = own[...]
    for ref in pieces:
        total += ref[...].astype(F32)
    grad[...] = total.astype(BF16)
    at = block(role * 2 + x, total.shape[1])
    new_m, new_v = adamw_moments(m[:, at], v[:, at], total)
    new_w[...] = adamw_weight(w[:, at], new_m, new_v)


def put(outs, at, value):
    for out in outs:
        out[at, :] = value


def put(outs, at, value):
    for out in outs:
        out[at, :] = value


def rest_back_kernel(*refs):
    pieces, outs = refs[:-len(STEPS)], refs[-len(STEPS):]
    w = place()[4]
    rows = pieces[0].shape[0]
    for k, ref in enumerate(pieces):
        put(outs, block(w ^ k, rows), ref[...])


def narrow_back_kernel(own, *refs):
    parts, outs = (own,) + refs[:-len(STEPS)], refs[-len(STEPS):]
    for step, ref in zip((STAY,) + STEPS, parts):
        put(outs, block(group_of(step, 1), own.shape[0]), ref[...])


def half_blocks(sibling, parts, out):
    role, x, y, z, _ = place()
    square = (role == 1) != sibling
    size, quarter = parts[0].shape
    rows = out.shape[0] // lax.axis_size("shard")
    count = size // (4 * rows)
    for ((dy, dx), k), ref in zip((STAY,) + STEPS, parts):
        for group in range(4):
            to_y = jnp.where(square, y ^ dy, group >> 1)
            to_x = jnp.where(square, x ^ dx, group & 1)
            to_z = jnp.where(square, group, z ^ k)
            for w in range(count):
                at = (group * count + w) * rows
                out[block(8 * w + 2 * to_z + to_y, rows), block(to_x, quarter)] = ref[at:at + rows, :]


def write(sibling, parts, grads, m, v, w_out, m_out, v_out, half, new_m, new_v, sems):
    role, x, _, _, _ = place()
    side = role ^ sibling
    half_blocks(sibling, parts, half)
    copies = []
    in_parts(half, w_out.at[:, block(side, half.shape[1])], sems, copies)
    for far, grad in enumerate(grads):
        at = block(2 * side + (x ^ far), grad.shape[1])
        new_m[far], new_v[far] = adamw_moments(m[:, at], v[:, at], grad[...].astype(F32))
        for source, out in ((new_m, m_out), (new_v, v_out)):
            copies.append(pltpu.make_async_copy(source.at[far], out.at[:, at], sems.at[len(copies)]))
            copies[-1].start()
    for copy in copies:
        copy.wait()


def pack_kernel(*refs):
    *parts, _, out = refs
    at = 0
    for ref in parts:
        out[at:at + ref.shape[0], :] = ref[...]
        at += ref.shape[0]


def write_own_kernel(m, v, grad, far_grad, *refs):
    parts, refs = refs[:1 + len(STEPS)], refs[1 + len(STEPS):]
    write(0, parts, (grad, far_grad), m, v, *refs)


def write_other_kernel(m, v, own, landed, _w, _m, _v, *refs):
    size, rows = own.shape[0], m.shape[0]
    sizes = [size] * len(STEPS) + [rows] * 2
    parts, at = [], 0
    for count in sizes:
        parts.append(landed.at[pl.ds(at, count), :])
        at += count
    write(1, [own] + parts[:len(STEPS)], parts[len(STEPS):], m, v, *refs)


def body(hidden_acts, out_cotangent, weight, first_moment, second_moment):
    rows, width = weight.shape
    tokens, all_rows = hidden_acts.shape
    half, quarter = width // 2, width // 4
    rest = lax.axis_size("shard") // 8
    wide_rows, narrow_rows = all_rows // 2, all_rows // 8

    later = CHUNK
    away_cots, first = call(
        load_kernel, [shape((tokens, half), BF16), shape((tokens, half - later), BF16)], out_cotangent,
        far_in=(0,), scratch=[pltpu.SemaphoreType.DMA((2 * PARTS,))], limit=LOAD_LIMIT,
    )
    away, turned = call(
        away_kernel, [shape((all_rows, half), BF16), shape((all_rows, tokens), BF16)], hidden_acts, away_cots,
    )
    came = to_sibling(away)
    kept = call(
        kept_kernel, [shape((all_rows, half), F32)], turned, first, out_cotangent,
        far_in=(2,), limit=KEPT_LIMIT,
        scratch=[pltpu.VMEM((tokens, later), BF16), pltpu.SemaphoreType.DMA((PARTS,))],
    )[0]

    def split(kernel, size, parts, *args):
        kept, sent = shape((size, quarter), F32), shape((size, quarter), BF16)
        return call(kernel, [kept] + [sent] * (parts - 1), *args)

    own, *pieces = split(functools.partial(wide_kernel, rows), wide_rows, 4, kept, came)
    came = [stage(piece, step, 0) for step, piece in zip(STEPS, pieces)]
    own, *pieces = split(narrow_kernel, narrow_rows, 4, own, *came)
    came = [stage(piece, step, 1) for step, piece in zip(STEPS, pieces)]
    if rest > 1:
        own, *pieces = split(rest_kernel, rows, rest, own, *came)
        came = [along_rest(piece, k + 1) for k, piece in enumerate(pieces)]
    new_w, grad = call(
        update_kernel, [shape((rows, quarter), BF16)] * 2, weight, first_moment, second_moment, own, *came,
    )

    pieces = [along_rest(new_w, k) for k in range(1, rest)]
    parts = call(rest_back_kernel, [shape((narrow_rows, quarter), BF16)] * len(STEPS), new_w, *pieces)
    came = [stage(part, step, 0) for step, part in zip(STEPS, parts)]
    parts = call(narrow_back_kernel, [shape((wide_rows, quarter), BF16)] * len(STEPS), parts[-1], *came)
    came = [stage(part, step, 1) for step, part in zip(STEPS, parts)]
    far_grad, own = along_x(grad), to_sibling(parts[-1])
    came[0], far_grad = lax.optimization_barrier((came[0], far_grad))

    landed = to_sibling(call(
        pack_kernel, [shape((len(STEPS) * wide_rows + 2 * rows, quarter), BF16)], *came, grad, far_grad, own,
    )[0])
    outs = [shape((all_rows, width), BF16), shape((rows, width), F32), shape((rows, width), F32)]
    scratch = [pltpu.VMEM((all_rows, half), BF16)] + [pltpu.VMEM((2, rows, quarter), F32)] * 2
    scratch += [pltpu.SemaphoreType.DMA((PARTS + 4,))]
    written = call(
        write_own_kernel, outs, first_moment, second_moment, grad, far_grad, parts[-1], *came,
        far_out=3, scratch=scratch,
    )
    return tuple(call(
        write_other_kernel, outs, first_moment, second_moment, own, landed, *written,
        far_in=(4, 5, 6), far_out=3, scratch=scratch, aliases={4: 0, 5: 1, 6: 2},
    ))


def solution(mesh):
    return jax.shard_map(
        body,
        mesh=mesh,
        in_specs=(
            P(("rep", "shard"), None),
            P(("rep", "shard"), None),
            P("shard", None),
            P("shard", None),
            P("shard", None),
        ),
        out_specs=(P(), P("shard", None), P("shard", None)),
        check_vma=False,
    )
```

```python
import functools

import jax
import jax.numpy as jnp
from jax import lax
from jax.experimental import pallas as pl
from jax.experimental.pallas import tpu as pltpu
from jax.sharding import PartitionSpec as P

F32 = jnp.float32
BF16 = jnp.bfloat16
CHUNK = 512
LOAD_LIMIT = 48 * 1024 * 1024
KEPT_LIMIT = 50 * 1024 * 1024


def adamw_moments(first_moment, second_moment, grad):
    new_first = 0.9 * first_moment + 0.1 * grad
    new_second = 0.999 * second_moment + 0.001 * grad * grad
    return new_first, new_second


def adamw_weight(weight, new_first, new_second):
    corr_one = 0.9999734386011124
    corr_two = 0.0952078528
    wfloat = weight.astype(F32)
    update = new_first / corr_one / (jnp.sqrt(new_second / corr_two) + 1e-08)
    return (wfloat - 0.05 * (update + 0.1 * wfloat)).astype(BF16)


def shape(dims, kind):
    return jax.ShapeDtypeStruct(dims, kind)


def call(kernel, outs, *args, far_in=(), far_out=0, scratch=(), aliases=None, limit=48 * 1024 * 1024):
    near, far = pl.BlockSpec(memory_space=pltpu.VMEM), pl.BlockSpec(memory_space=pltpu.HBM)
    return pl.pallas_call(
        kernel,
        out_shape=outs,
        in_specs=[far if i in tuple(far_in) else near for i in range(len(args))],
        out_specs=[far if i < far_out else near for i in range(len(outs))],
        scratch_shapes=scratch,
        input_output_aliases=aliases or {},
        compiler_params=pltpu.CompilerParams(vmem_limit_bytes=limit),
    )(*args)


def exchange(value, other):
    reps, shards = lax.axis_size("rep"), lax.axis_size("shard")
    pairs = []
    for rep in range(reps):
        for shard in range(shards):
            to_rep, to_shard = other(rep, shard)
            pairs.append((rep * shards + shard, to_rep * shards + to_shard))
    return lax.ppermute(value, ("rep", "shard"), pairs)


def to_sibling(value):
    return exchange(value, lambda rep, shard: (rep ^ 1, shard))


SQUARE = ((1, 1), (1, 0), (0, 1))
STEPS = tuple(zip(SQUARE, (2, 3, 1)))
BACK_STEPS = tuple(zip(SQUARE, (3, 2, 1)))
STAY = ((0, 0), 0)


def role_of(rep, shard):
    return (rep ^ (rep >> 1) ^ shard ^ (shard >> 1)) & 1


def partner(rep, shard, dy, dx, k):
    return rep ^ (2 * dx) ^ ((dy ^ dx ^ k) & 1), shard ^ dy ^ (2 * k)


def stage(value, step, square_role):
    (dy, dx), k = step
    return exchange(
        value,
        lambda rep, shard: partner(rep, shard, dy, dx, 0) if role_of(rep, shard) == square_role
        else partner(rep, shard, 0, 0, k),
    )


def along_x(value):
    return exchange(value, lambda rep, shard: partner(rep, shard, 0, 1, 0))


def along_rest(value, k):
    return exchange(value, lambda rep, shard: (rep, shard ^ (8 * k)))


def place():
    rep, shard = lax.axis_index("rep"), lax.axis_index("shard")
    return role_of(rep, shard), rep >> 1, shard & 1, (shard >> 1) & 3, shard >> 3


def in_half(step, group):
    role, x, y, z, _ = place()
    (dy, dx), k = step
    first = role == 0
    return (
        jnp.where(first, y ^ dy, group >> 1), jnp.where(first, x ^ dx, group & 1), jnp.where(first, group, z ^ k),
    )


def group_of(step, line_role):
    role, x, y, z, _ = place()
    (dy, dx), k = step
    return jnp.where(role == line_role, z ^ k, 2 * (y ^ dy) + (x ^ dx))


def block(index, size):
    return pl.ds(pl.multiple_of(index * size, size), size)


def load_kernel(cots_ref, away, first, sems):
    role = place()[0]
    copies = []
    for out, side in ((away, 1 - role), (first, role)):
        at = pl.ds(pl.multiple_of(side * away.shape[1], CHUNK), out.shape[1])
        copies.append(pltpu.make_async_copy(cots_ref.at[:, at], out, sems.at[len(copies)]))
        copies[-1].start()
    for copy in copies:
        copy.wait()


def away_kernel(acts, cots, out, turned):
    turned[...] = acts[...].T
    for i in range(out.shape[1] // CHUNK):
        at = slice(i * CHUNK, (i + 1) * CHUNK)
        out[:, at] = jnp.dot(turned[...], cots[:, at], preferred_element_type=F32).astype(BF16)


def kept_kernel(turned, first, cots_ref, out, cots, sems):
    role = place()[0]
    ready, count = first.shape[1] // CHUNK, out.shape[1] // CHUNK
    copies = []
    for i in range(ready, count):
        source = cots_ref.at[:, block(role * count + i, CHUNK)]
        copies.append(pltpu.make_async_copy(source, cots.at[i - ready], sems.at[i - ready]))
        copies[-1].start()
    for i in range(count):
        at = slice(i * CHUNK, (i + 1) * CHUNK)
        if i >= ready:
            copies[i - ready].wait()
        chunk = cots[i - ready] if i >= ready else first[:, at]
        out[:, at] = jnp.dot(turned[...], chunk, preferred_element_type=F32)


def wide_kernel(rows, kept, came, own, *pieces):
    quarter = own.shape[1]
    count = own.shape[0] // (4 * rows)
    for step, out in zip((STAY,) + STEPS, (own,) + pieces):
        for group in range(4):
            y, x, z = in_half(step, group)
            cols = block(x, quarter)
            for w in range(count):
                at = block(8 * w + 2 * z + y, rows)
                total = kept[at, cols] + came[at, cols].astype(F32)
                to = (group * count + w) * rows
                out[to:to + rows, :] = total.astype(out.dtype)


def narrow_kernel(kept, *refs):
    came, (own, *pieces) = refs[:len(STEPS)], refs[len(STEPS):]
    for step, out in zip((STAY,) + STEPS, [own] + pieces):
        at = block(group_of(step, 0), out.shape[0])
        total = kept[at, :]
        for ref in came:
            total += ref[at, :].astype(F32)
        out[...] = total.astype(out.dtype)


def rest_kernel(kept, *refs):
    came, outs = refs[:len(STEPS)], refs[len(STEPS):]
    w = place()[4]
    for k, out in enumerate(outs):
        at = block(w ^ k, out.shape[0])
        total = kept[at, :]
        for ref in came:
            total += ref[at, :].astype(F32)
        out[...] = total.astype(out.dtype)


def update_kernel(w, m, v, own, *refs):
    pieces, (new_w, grad) = refs[:-2], refs[-2:]
    role, x, _, _, _ = place()
    total = own[...]
    for ref in pieces:
        total += ref[...].astype(F32)
    grad[...] = total.astype(BF16)
    at = block(role * 2 + x, total.shape[1])
    new_m, new_v = adamw_moments(m[:, at], v[:, at], total)
    new_w[...] = adamw_weight(w[:, at], new_m, new_v)


def put(outs, at, value):
    for out in outs:
        out[at, :] = value


def put(outs, at, value):
    for out in outs:
        out[at, :] = value


def rest_back_kernel(*refs):
    pieces, outs = refs[:-len(STEPS)], refs[-len(STEPS):]
    w = place()[4]
    rows = pieces[0].shape[0]
    for k, ref in enumerate(pieces):
        put(outs, block(w ^ k, rows), ref[...])


def narrow_back_kernel(own, *refs):
    parts, outs = (own,) + refs[:-len(STEPS)], refs[-len(STEPS):]
    for step, ref in zip((STAY,) + BACK_STEPS, parts):
        put(outs, block(group_of(step, 1), own.shape[0]), ref[...])


def half_blocks(sibling, parts, out):
    role, x, y, z, _ = place()
    square = (role == 1) != sibling
    size, quarter = parts[0].shape
    rows = out.shape[0] // lax.axis_size("shard")
    count = size // (4 * rows)
    for ((dy, dx), k), ref in zip((STAY,) + BACK_STEPS, parts):
        for group in range(4):
            to_y = jnp.where(square, y ^ dy, group >> 1)
            to_x = jnp.where(square, x ^ dx, group & 1)
            to_z = jnp.where(square, group, z ^ k)
            for w in range(count):
                at = (group * count + w) * rows
                out[block(8 * w + 2 * to_z + to_y, rows), block(to_x, quarter)] = ref[at:at + rows, :]


def write(sibling, parts, grads, m, v, w_out, m_out, v_out, half, new_m, new_v, sems):
    role, x, _, _, _ = place()
    side = role ^ sibling
    half_blocks(sibling, parts, half)
    copies = [pltpu.make_async_copy(half, w_out.at[:, block(side, half.shape[1])], sems.at[0])]
    copies[0].start()
    for far, grad in enumerate(grads):
        at = block(2 * side + (x ^ far), grad.shape[1])
        new_m[far], new_v[far] = adamw_moments(m[:, at], v[:, at], grad[...].astype(F32))
        for source, out in ((new_m, m_out), (new_v, v_out)):
            copies.append(pltpu.make_async_copy(source.at[far], out.at[:, at], sems.at[len(copies)]))
            copies[-1].start()
    for copy in copies:
        copy.wait()


def pack_kernel(*refs):
    *parts, _, out = refs
    at = 0
    for ref in parts:
        out[at:at + ref.shape[0], :] = ref[...]
        at += ref.shape[0]


def write_own_kernel(m, v, grad, far_grad, *refs):
    parts, refs = refs[:1 + len(STEPS)], refs[1 + len(STEPS):]
    write(0, parts, (grad, far_grad), m, v, *refs)


def write_other_kernel(m, v, own, landed, _w, _m, _v, *refs):
    size, rows = own.shape[0], m.shape[0]
    sizes = [size] * len(STEPS) + [rows] * 2
    parts, at = [], 0
    for count in sizes:
        parts.append(landed.at[pl.ds(at, count), :])
        at += count
    write(1, [own] + parts[:len(STEPS)], parts[len(STEPS):], m, v, *refs)


def body(hidden_acts, out_cotangent, weight, first_moment, second_moment):
    rows, width = weight.shape
    tokens, all_rows = hidden_acts.shape
    half, quarter = width // 2, width // 4
    rest = lax.axis_size("shard") // 8
    wide_rows, narrow_rows = all_rows // 2, all_rows // 8

    away_cots, first = call(
        load_kernel, [shape((tokens, half), BF16), shape((tokens, CHUNK), BF16)], out_cotangent,
        far_in=(0,), scratch=[pltpu.SemaphoreType.DMA((2,))], limit=LOAD_LIMIT,
    )
    away, turned = call(
        away_kernel, [shape((all_rows, half), BF16), shape((all_rows, tokens), BF16)], hidden_acts, away_cots,
    )
    came = to_sibling(away)
    later = half // CHUNK - 1
    kept = call(
        kept_kernel, [shape((all_rows, half), F32)], turned, first, out_cotangent,
        far_in=(2,), limit=KEPT_LIMIT,
        scratch=[pltpu.VMEM((later, tokens, CHUNK), BF16), pltpu.SemaphoreType.DMA((later,))],
    )[0]

    def split(kernel, size, parts, *args):
        kept, sent = shape((size, quarter), F32), shape((size, quarter), BF16)
        return call(kernel, [kept] + [sent] * (parts - 1), *args)

    own, *pieces = split(functools.partial(wide_kernel, rows), wide_rows, 4, kept, came)
    came = [stage(piece, step, 0) for step, piece in zip(STEPS, pieces)]
    own, *pieces = split(narrow_kernel, narrow_rows, 4, own, *came)
    came = [stage(piece, step, 1) for step, piece in zip(STEPS, pieces)]
    if rest > 1:
        own, *pieces = split(rest_kernel, rows, rest, own, *came)
        came = [along_rest(piece, k + 1) for k, piece in enumerate(pieces)]
    new_w, grad = call(
        update_kernel, [shape((rows, quarter), BF16)] * 2, weight, first_moment, second_moment, own, *came,
    )

    pieces = [along_rest(new_w, k) for k in range(1, rest)]
    parts = call(rest_back_kernel, [shape((narrow_rows, quarter), BF16)] * len(STEPS), new_w, *pieces)
    came = [stage(part, step, 0) for step, part in zip(BACK_STEPS, parts)]
    parts = call(narrow_back_kernel, [shape((wide_rows, quarter), BF16)] * len(STEPS), parts[-1], *came)
    came = [stage(part, step, 1) for step, part in zip(BACK_STEPS, parts)]
    far_grad, own = along_x(grad), to_sibling(parts[-1])
    came[0], far_grad = lax.optimization_barrier((came[0], far_grad))

    landed = to_sibling(call(
        pack_kernel, [shape((len(STEPS) * wide_rows + 2 * rows, quarter), BF16)], *came, grad, far_grad, own,
    )[0])
    outs = [shape((all_rows, width), BF16), shape((rows, width), F32), shape((rows, width), F32)]
    scratch = [pltpu.VMEM((all_rows, half), BF16)] + [pltpu.VMEM((2, rows, quarter), F32)] * 2
    scratch += [pltpu.SemaphoreType.DMA((5,))]
    written = call(
        write_own_kernel, outs, first_moment, second_moment, grad, far_grad, parts[-1], *came,
        far_out=3, scratch=scratch,
    )
    return tuple(call(
        write_other_kernel, outs, first_moment, second_moment, own, landed, *written,
        far_in=(4, 5, 6), far_out=3, scratch=scratch, aliases={4: 0, 5: 1, 6: 2},
    ))


def solution(mesh):
    return jax.shard_map(
        body,
        mesh=mesh,
        in_specs=(
            P(("rep", "shard"), None),
            P(("rep", "shard"), None),
            P("shard", None),
            P("shard", None),
            P("shard", None),
        ),
        out_specs=(P(), P("shard", None), P("shard", None)),
        check_vma=False,
    )
```

```python
import functools

import jax
import jax.numpy as jnp
from jax import lax
from jax.experimental import pallas as pl
from jax.experimental.pallas import tpu as pltpu
from jax.sharding import PartitionSpec as P

F32 = jnp.float32
BF16 = jnp.bfloat16
CHUNK = 512
LOAD_LIMIT = 48 * 1024 * 1024
KEPT_LIMIT = 50 * 1024 * 1024


def adamw_moments(first_moment, second_moment, grad):
    new_first = 0.9 * first_moment + 0.1 * grad
    new_second = 0.999 * second_moment + 0.001 * grad * grad
    return new_first, new_second


def adamw_weight(weight, new_first, new_second):
    corr_one = 0.9999734386011124
    corr_two = 0.0952078528
    wfloat = weight.astype(F32)
    update = new_first / corr_one / (jnp.sqrt(new_second / corr_two) + 1e-08)
    return (wfloat - 0.05 * (update + 0.1 * wfloat)).astype(BF16)


def shape(dims, kind):
    return jax.ShapeDtypeStruct(dims, kind)


def call(kernel, outs, *args, far_in=(), far_out=0, scratch=(), aliases=None, limit=48 * 1024 * 1024):
    near, far = pl.BlockSpec(memory_space=pltpu.VMEM), pl.BlockSpec(memory_space=pltpu.HBM)
    return pl.pallas_call(
        kernel,
        out_shape=outs,
        in_specs=[far if i in tuple(far_in) else near for i in range(len(args))],
        out_specs=[far if i < far_out else near for i in range(len(outs))],
        scratch_shapes=scratch,
        input_output_aliases=aliases or {},
        compiler_params=pltpu.CompilerParams(vmem_limit_bytes=limit),
    )(*args)


def exchange(value, other):
    reps, shards = lax.axis_size("rep"), lax.axis_size("shard")
    pairs = []
    for rep in range(reps):
        for shard in range(shards):
            to_rep, to_shard = other(rep, shard)
            pairs.append((rep * shards + shard, to_rep * shards + to_shard))
    return lax.ppermute(value, ("rep", "shard"), pairs)


def to_sibling(value):
    return exchange(value, lambda rep, shard: (rep ^ 1, shard))


SQUARE = ((1, 1), (1, 0), (0, 1))
LINE = (2, 3, 1)
STEPS = tuple(zip(SQUARE, LINE))
STAY = ((0, 0), 0)


def role_of(rep, shard):
    return (rep ^ (rep >> 1) ^ shard ^ (shard >> 1)) & 1


def partner(rep, shard, dy, dx, k):
    return rep ^ (2 * dx) ^ ((dy ^ dx ^ k) & 1), shard ^ dy ^ (2 * k)


def stage(value, step, square_role):
    (dy, dx), k = step
    return exchange(
        value,
        lambda rep, shard: partner(rep, shard, dy, dx, 0) if role_of(rep, shard) == square_role
        else partner(rep, shard, 0, 0, k),
    )


def along_x(value):
    return exchange(value, lambda rep, shard: partner(rep, shard, 0, 1, 0))


def along_rest(value, k):
    return exchange(value, lambda rep, shard: (rep, shard ^ (8 * k)))


def place():
    rep, shard = lax.axis_index("rep"), lax.axis_index("shard")
    return role_of(rep, shard), rep >> 1, shard & 1, (shard >> 1) & 3, shard >> 3


def in_half(step, group):
    role, x, y, z, _ = place()
    (dy, dx), k = step
    first = role == 0
    return (
        jnp.where(first, y ^ dy, group >> 1), jnp.where(first, x ^ dx, group & 1), jnp.where(first, group, z ^ k),
    )


def group_of(step, line_role):
    role, x, y, z, _ = place()
    (dy, dx), k = step
    return jnp.where(role == line_role, z ^ k, 2 * (y ^ dy) + (x ^ dx))


def block(index, size):
    return pl.ds(pl.multiple_of(index * size, size), size)


def load_kernel(cots_ref, away, first, sems):
    role = place()[0]
    copies = []
    for out, side in ((away, 1 - role), (first, role)):
        at = pl.ds(pl.multiple_of(side * away.shape[1], CHUNK), out.shape[1])
        copies.append(pltpu.make_async_copy(cots_ref.at[:, at], out, sems.at[len(copies)]))
        copies[-1].start()
    for copy in copies:
        copy.wait()


def away_kernel(acts, cots, out, turned):
    turned[...] = acts[...].T
    for i in range(out.shape[1] // CHUNK):
        at = slice(i * CHUNK, (i + 1) * CHUNK)
        out[:, at] = jnp.dot(turned[...], cots[:, at], preferred_element_type=F32).astype(BF16)


def kept_kernel(turned, first, cots_ref, out, cots, sems):
    role = place()[0]
    ready, count = first.shape[1] // CHUNK, out.shape[1] // CHUNK
    copies = []
    for i in range(ready, count):
        source = cots_ref.at[:, block(role * count + i, CHUNK)]
        copies.append(pltpu.make_async_copy(source, cots.at[i - ready], sems.at[i - ready]))
        copies[-1].start()
    for i in range(count):
        at = slice(i * CHUNK, (i + 1) * CHUNK)
        if i >= ready:
            copies[i - ready].wait()
        chunk = cots[i - ready] if i >= ready else first[:, at]
        out[:, at] = jnp.dot(turned[...], chunk, preferred_element_type=F32)


def wide_kernel(rows, kept, came, own, *pieces):
    quarter = own.shape[1]
    count = own.shape[0] // (4 * rows)
    for step, out in zip((STAY,) + STEPS, (own,) + pieces):
        for group in range(4):
            y, x, z = in_half(step, group)
            cols = block(x, quarter)
            for w in range(count):
                at = block(8 * w + 2 * z + y, rows)
                total = kept[at, cols] + came[at, cols].astype(F32)
                to = (group * count + w) * rows
                out[to:to + rows, :] = total.astype(out.dtype)


def narrow_kernel(kept, *refs):
    came, (own, *pieces) = refs[:len(STEPS)], refs[len(STEPS):]
    for step, out in zip((STAY,) + STEPS, [own] + pieces):
        at = block(group_of(step, 0), out.shape[0])
        total = kept[at, :]
        for ref in came:
            total += ref[at, :].astype(F32)
        out[...] = total.astype(out.dtype)


def rest_kernel(kept, *refs):
    came, outs = refs[:len(STEPS)], refs[len(STEPS):]
    w = place()[4]
    for k, out in enumerate(outs):
        at = block(w ^ k, out.shape[0])
        total = kept[at, :]
        for ref in came:
            total += ref[at, :].astype(F32)
        out[...] = total.astype(out.dtype)


def update_kernel(w, m, v, own, *refs):
    pieces, (new_w, grad) = refs[:-2], refs[-2:]
    role, x, _, _, _ = place()
    total = own[...]
    for ref in pieces:
        total += ref[...].astype(F32)
    grad[...] = total.astype(BF16)
    at = block(role * 2 + x, total.shape[1])
    new_m, new_v = adamw_moments(m[:, at], v[:, at], total)
    new_w[...] = adamw_weight(w[:, at], new_m, new_v)


def put(outs, at, value):
    for out in outs:
        out[at, :] = value


def put(outs, at, value):
    for out in outs:
        out[at, :] = value


def rest_back_kernel(*refs):
    pieces, outs = refs[:-len(STEPS)], refs[-len(STEPS):]
    w = place()[4]
    rows = pieces[0].shape[0]
    for k, ref in enumerate(pieces):
        put(outs, block(w ^ k, rows), ref[...])


def narrow_back_kernel(own, *refs):
    parts, outs = (own,) + refs[:-len(STEPS)], refs[-len(STEPS):]
    for step, ref in zip((STAY,) + STEPS, parts):
        put(outs, block(group_of(step, 1), own.shape[0]), ref[...])


def half_blocks(sibling, parts, out):
    role, x, y, z, _ = place()
    square = (role == 1) != sibling
    size, quarter = parts[0].shape
    rows = out.shape[0] // lax.axis_size("shard")
    count = size // (4 * rows)
    for ((dy, dx), k), ref in zip((STAY,) + STEPS, parts):
        for group in range(4):
            to_y = jnp.where(square, y ^ dy, group >> 1)
            to_x = jnp.where(square, x ^ dx, group & 1)
            to_z = jnp.where(square, group, z ^ k)
            for w in range(count):
                at = (group * count + w) * rows
                out[block(8 * w + 2 * to_z + to_y, rows), block(to_x, quarter)] = ref[at:at + rows, :]


def write(sibling, parts, grads, m, v, w_out, m_out, v_out, half, new_m, new_v, sems):
    role, x, _, _, _ = place()
    side = role ^ sibling
    half_blocks(sibling, parts, half)
    copies = [pltpu.make_async_copy(half, w_out.at[:, block(side, half.shape[1])], sems.at[0])]
    copies[0].start()
    for far, grad in enumerate(grads):
        at = block(2 * side + (x ^ far), grad.shape[1])
        new_m[far], new_v[far] = adamw_moments(m[:, at], v[:, at], grad[...].astype(F32))
        for source, out in ((new_m, m_out), (new_v, v_out)):
            copies.append(pltpu.make_async_copy(source.at[far], out.at[:, at], sems.at[len(copies)]))
            copies[-1].start()
    for copy in copies:
        copy.wait()


def pack_kernel(*refs):
    *parts, _, out = refs
    at = 0
    for ref in parts:
        out[at:at + ref.shape[0], :] = ref[...]
        at += ref.shape[0]


def write_own_kernel(m, v, grad, far_grad, *refs):
    parts, refs = refs[:1 + len(STEPS)], refs[1 + len(STEPS):]
    write(0, parts, (grad, far_grad), m, v, *refs)


def write_other_kernel(m, v, own, landed, _w, _m, _v, *refs):
    size, rows = own.shape[0], m.shape[0]
    sizes = [size] * len(STEPS) + [rows] * 2
    parts, at = [], 0
    for count in sizes:
        parts.append(landed.at[pl.ds(at, count), :])
        at += count
    write(1, [own] + parts[:len(STEPS)], parts[len(STEPS):], m, v, *refs)


def body(hidden_acts, out_cotangent, weight, first_moment, second_moment):
    rows, width = weight.shape
    tokens, all_rows = hidden_acts.shape
    half, quarter = width // 2, width // 4
    rest = lax.axis_size("shard") // 8
    wide_rows, narrow_rows = all_rows // 2, all_rows // 8

    away_cots, first = call(
        load_kernel, [shape((tokens, half), BF16), shape((tokens, CHUNK), BF16)], out_cotangent,
        far_in=(0,), scratch=[pltpu.SemaphoreType.DMA((2,))], limit=LOAD_LIMIT,
    )
    away, turned = call(
        away_kernel, [shape((all_rows, half), BF16), shape((all_rows, tokens), BF16)], hidden_acts, away_cots,
    )
    came = to_sibling(away)
    later = half // CHUNK - 1
    kept = call(
        kept_kernel, [shape((all_rows, half), F32)], turned, first, out_cotangent,
        far_in=(2,), limit=KEPT_LIMIT,
        scratch=[pltpu.VMEM((later, tokens, CHUNK), BF16), pltpu.SemaphoreType.DMA((later,))],
    )[0]

    def split(kernel, size, parts, *args):
        kept, sent = shape((size, quarter), F32), shape((size, quarter), BF16)
        return call(kernel, [kept] + [sent] * (parts - 1), *args)

    own, *pieces = split(functools.partial(wide_kernel, rows), wide_rows, 4, kept, came)
    came = [stage(piece, step, 0) for step, piece in zip(STEPS, pieces)]
    own, *pieces = split(narrow_kernel, narrow_rows, 4, own, *came)
    came = [stage(piece, step, 1) for step, piece in zip(STEPS, pieces)]
    if rest > 1:
        own, *pieces = split(rest_kernel, rows, rest, own, *came)
        came = [along_rest(piece, k + 1) for k, piece in enumerate(pieces)]
    new_w, grad = call(
        update_kernel, [shape((rows, quarter), BF16)] * 2, weight, first_moment, second_moment, own, *came,
    )

    pieces = [along_rest(new_w, k) for k in range(1, rest)]
    parts = call(rest_back_kernel, [shape((narrow_rows, quarter), BF16)] * len(STEPS), new_w, *pieces)
    came = [stage(part, step, 0) for step, part in zip(STEPS, parts)]
    parts = call(narrow_back_kernel, [shape((wide_rows, quarter), BF16)] * len(STEPS), parts[-1], *came)
    came = [stage(part, step, 1) for step, part in zip(STEPS, parts)]
    far_grad, own = along_x(grad), to_sibling(parts[-1])
    came[0], far_grad = lax.optimization_barrier((came[0], far_grad))

    landed = to_sibling(call(
        pack_kernel, [shape((len(STEPS) * wide_rows + 2 * rows, quarter), BF16)], *came, grad, far_grad, own,
    )[0])
    outs = [shape((all_rows, width), BF16), shape((rows, width), F32), shape((rows, width), F32)]
    scratch = [pltpu.VMEM((all_rows, half), BF16)] + [pltpu.VMEM((2, rows, quarter), F32)] * 2
    scratch += [pltpu.SemaphoreType.DMA((5,))]
    written = call(
        write_own_kernel, outs, first_moment, second_moment, grad, far_grad, parts[-1], *came,
        far_out=3, scratch=scratch,
    )
    return tuple(call(
        write_other_kernel, outs, first_moment, second_moment, own, landed, *written,
        far_in=(4, 5, 6), far_out=3, scratch=scratch, aliases={4: 0, 5: 1, 6: 2},
    ))


def solution(mesh):
    return jax.shard_map(
        body,
        mesh=mesh,
        in_specs=(
            P(("rep", "shard"), None),
            P(("rep", "shard"), None),
            P("shard", None),
            P("shard", None),
            P("shard", None),
        ),
        out_specs=(P(), P("shard", None), P("shard", None)),
        check_vma=False,
    )
```

```python
import functools

import jax
import jax.numpy as jnp
from jax import lax
from jax.experimental import pallas as pl
from jax.experimental.pallas import tpu as pltpu
from jax.sharding import PartitionSpec as P

F32 = jnp.float32
BF16 = jnp.bfloat16
CHUNK = 512
LOAD_LIMIT = 48 * 1024 * 1024
KEPT_LIMIT = 50 * 1024 * 1024


def adamw_moments(first_moment, second_moment, grad):
    new_first = 0.9 * first_moment + 0.1 * grad
    new_second = 0.999 * second_moment + 0.001 * grad * grad
    return new_first, new_second


def adamw_weight(weight, new_first, new_second):
    corr_one = 0.9999734386011124
    corr_two = 0.0952078528
    wfloat = weight.astype(F32)
    update = new_first / corr_one / (jnp.sqrt(new_second / corr_two) + 1e-08)
    return (wfloat - 0.05 * (update + 0.1 * wfloat)).astype(BF16)


def shape(dims, kind):
    return jax.ShapeDtypeStruct(dims, kind)


def call(kernel, outs, *args, far_in=(), far_out=0, scratch=(), aliases=None, limit=48 * 1024 * 1024):
    near, far = pl.BlockSpec(memory_space=pltpu.VMEM), pl.BlockSpec(memory_space=pltpu.HBM)
    return pl.pallas_call(
        kernel,
        out_shape=outs,
        in_specs=[far if i in tuple(far_in) else near for i in range(len(args))],
        out_specs=[far if i < far_out else near for i in range(len(outs))],
        scratch_shapes=scratch,
        input_output_aliases=aliases or {},
        compiler_params=pltpu.CompilerParams(vmem_limit_bytes=limit),
    )(*args)


def exchange(value, other):
    reps, shards = lax.axis_size("rep"), lax.axis_size("shard")
    pairs = []
    for rep in range(reps):
        for shard in range(shards):
            to_rep, to_shard = other(rep, shard)
            pairs.append((rep * shards + shard, to_rep * shards + to_shard))
    return lax.ppermute(value, ("rep", "shard"), pairs)


def to_sibling(value):
    return exchange(value, lambda rep, shard: (rep ^ 1, shard))


SQUARE = ((1, 1), (1, 0), (0, 1))
LINE = (2, 3, 1)
STEPS = tuple(zip(SQUARE, LINE))
STAY = ((0, 0), 0)


def role_of(rep, shard):
    return (rep ^ (rep >> 1) ^ shard ^ (shard >> 1)) & 1


def partner(rep, shard, dy, dx, k):
    return rep ^ (2 * dx) ^ ((dy ^ dx ^ k) & 1), shard ^ dy ^ (2 * k)


def stage(value, step, square_role):
    (dy, dx), k = step
    return exchange(
        value,
        lambda rep, shard: partner(rep, shard, dy, dx, 0) if role_of(rep, shard) == square_role
        else partner(rep, shard, 0, 0, k),
    )


def along_x(value):
    return exchange(value, lambda rep, shard: partner(rep, shard, 0, 1, 0))


def along_rest(value, k):
    return exchange(value, lambda rep, shard: (rep, shard ^ (8 * k)))


def place():
    rep, shard = lax.axis_index("rep"), lax.axis_index("shard")
    return role_of(rep, shard), rep >> 1, shard & 1, (shard >> 1) & 3, shard >> 3


def in_half(step, group):
    role, x, y, z, _ = place()
    (dy, dx), k = step
    first = role == 0
    return (
        jnp.where(first, y ^ dy, group >> 1), jnp.where(first, x ^ dx, group & 1), jnp.where(first, group, z ^ k),
    )


def group_of(step, line_role):
    role, x, y, z, _ = place()
    (dy, dx), k = step
    return jnp.where(role == line_role, z ^ k, 2 * (y ^ dy) + (x ^ dx))


def block(index, size):
    return pl.ds(pl.multiple_of(index * size, size), size)


def load_kernel(cots_ref, away, first, sems):
    role = place()[0]
    copies = []
    for out, side in ((away, 1 - role), (first, role)):
        at = pl.ds(pl.multiple_of(side * away.shape[1], CHUNK), out.shape[1])
        copies.append(pltpu.make_async_copy(cots_ref.at[:, at], out, sems.at[len(copies)]))
        copies[-1].start()
    for copy in copies:
        copy.wait()


def away_kernel(acts, cots, out, turned):
    turned[...] = acts[...].T
    for i in range(out.shape[1] // CHUNK):
        at = slice(i * CHUNK, (i + 1) * CHUNK)
        out[:, at] = jnp.dot(turned[...], cots[:, at], preferred_element_type=F32).astype(BF16)


def kept_kernel(turned, first, cots_ref, out, cots, sems):
    role = place()[0]
    ready, count = first.shape[1] // CHUNK, out.shape[1] // CHUNK
    copies = []
    for i in range(ready, count):
        source = cots_ref.at[:, block(role * count + i, CHUNK)]
        copies.append(pltpu.make_async_copy(source, cots.at[i - ready], sems.at[i - ready]))
        copies[-1].start()
    for i in range(count):
        at = slice(i * CHUNK, (i + 1) * CHUNK)
        if i >= ready:
            copies[i - ready].wait()
        chunk = cots[i - ready] if i >= ready else first[:, at]
        out[:, at] = jnp.dot(turned[...], chunk, preferred_element_type=F32)


def wide_kernel(rows, kept, came, own, *pieces):
    quarter = own.shape[1]
    count = own.shape[0] // (4 * rows)
    for step, out in zip((STAY,) + STEPS, (own,) + pieces):
        for group in range(4):
            y, x, z = in_half(step, group)
            cols = block(x, quarter)
            for w in range(count):
                at = block(8 * w + 2 * z + y, rows)
                total = kept[at, cols] + came[at, cols].astype(F32)
                to = (group * count + w) * rows
                out[to:to + rows, :] = total.astype(out.dtype)


def narrow_kernel(kept, *refs):
    came, (own, *pieces) = refs[:len(STEPS)], refs[len(STEPS):]
    for step, out in zip((STAY,) + STEPS, [own] + pieces):
        at = block(group_of(step, 0), out.shape[0])
        total = kept[at, :]
        for ref in came:
            total += ref[at, :].astype(F32)
        out[...] = total.astype(out.dtype)


def rest_kernel(kept, *refs):
    came, outs = refs[:len(STEPS)], refs[len(STEPS):]
    w = place()[4]
    for k, out in enumerate(outs):
        at = block(w ^ k, out.shape[0])
        total = kept[at, :]
        for ref in came:
            total += ref[at, :].astype(F32)
        out[...] = total.astype(out.dtype)


def update_kernel(w, m, v, own, *refs):
    pieces, (new_w, grad) = refs[:-2], refs[-2:]
    role, x, _, _, _ = place()
    total = own[...]
    for ref in pieces:
        total += ref[...].astype(F32)
    grad[...] = total.astype(BF16)
    at = block(role * 2 + x, total.shape[1])
    new_m, new_v = adamw_moments(m[:, at], v[:, at], total)
    new_w[...] = adamw_weight(w[:, at], new_m, new_v)


def put(outs, at, value):
    for out in outs:
        out[at, :] = value


def put(outs, at, value):
    for out in outs:
        out[at, :] = value


def rest_back_kernel(grad, *refs):
    pieces, (*outs, last) = refs[:-1 - len(STEPS)], refs[-1 - len(STEPS):]
    w = place()[4]
    rows = grad.shape[0]
    for k, ref in enumerate(pieces):
        put(outs, block(w ^ k, rows), ref[...])
    last[...] = grad[...]


def narrow_back_kernel(own, *refs):
    parts, outs = (own,) + refs[:len(STEPS)], refs[-len(STEPS):]
    for step, ref in zip((STAY,) + STEPS, parts):
        put(outs, block(group_of(step, 1), own.shape[0]), ref[...])


def half_blocks(sibling, parts, out):
    role, x, y, z, _ = place()
    square = (role == 1) != sibling
    size, quarter = parts[0].shape
    rows = out.shape[0] // lax.axis_size("shard")
    count = size // (4 * rows)
    for ((dy, dx), k), ref in zip((STAY,) + STEPS, parts):
        for group in range(4):
            to_y = jnp.where(square, y ^ dy, group >> 1)
            to_x = jnp.where(square, x ^ dx, group & 1)
            to_z = jnp.where(square, group, z ^ k)
            for w in range(count):
                at = (group * count + w) * rows
                out[block(8 * w + 2 * to_z + to_y, rows), block(to_x, quarter)] = ref[at:at + rows, :]


def write(sibling, parts, grads, m, v, w_out, m_out, v_out, half, new_m, new_v, sems):
    role, x, _, _, _ = place()
    side = role ^ sibling
    half_blocks(sibling, parts, half)
    copies = [pltpu.make_async_copy(half, w_out.at[:, block(side, half.shape[1])], sems.at[0])]
    copies[0].start()
    for far, grad in enumerate(grads):
        at = block(2 * side + (x ^ far), grad.shape[1])
        new_m[far], new_v[far] = adamw_moments(m[:, at], v[:, at], grad[...].astype(F32))
        for source, out in ((new_m, m_out), (new_v, v_out)):
            copies.append(pltpu.make_async_copy(source.at[far], out.at[:, at], sems.at[len(copies)]))
            copies[-1].start()
    for copy in copies:
        copy.wait()


def pack_kernel(*refs):
    *parts, _, out = refs
    at = 0
    for ref in parts:
        out[at:at + ref.shape[0], :] = ref[...]
        at += ref.shape[0]


def write_own_kernel(m, v, grad, far_grad, *refs):
    parts, refs = refs[:1 + len(STEPS)], refs[1 + len(STEPS):]
    write(0, parts, (grad, far_grad), m, v, *refs)


def write_other_kernel(m, v, own, landed, _w, _m, _v, *refs):
    size, rows = own.shape[0], m.shape[0]
    sizes = [size] * len(STEPS) + [rows] * 2
    parts, at = [], 0
    for count in sizes:
        parts.append(landed.at[pl.ds(at, count), :])
        at += count
    write(1, [own] + parts[:len(STEPS)], parts[len(STEPS):], m, v, *refs)


def body(hidden_acts, out_cotangent, weight, first_moment, second_moment):
    rows, width = weight.shape
    tokens, all_rows = hidden_acts.shape
    half, quarter = width // 2, width // 4
    rest = lax.axis_size("shard") // 8
    wide_rows, narrow_rows = all_rows // 2, all_rows // 8

    away_cots, first = call(
        load_kernel, [shape((tokens, half), BF16), shape((tokens, CHUNK), BF16)], out_cotangent,
        far_in=(0,), scratch=[pltpu.SemaphoreType.DMA((2,))], limit=LOAD_LIMIT,
    )
    away, turned = call(
        away_kernel, [shape((all_rows, half), BF16), shape((all_rows, tokens), BF16)], hidden_acts, away_cots,
    )
    came = to_sibling(away)
    later = half // CHUNK - 1
    kept = call(
        kept_kernel, [shape((all_rows, half), F32)], turned, first, out_cotangent,
        far_in=(2,), limit=KEPT_LIMIT,
        scratch=[pltpu.VMEM((later, tokens, CHUNK), BF16), pltpu.SemaphoreType.DMA((later,))],
    )[0]

    def split(kernel, size, parts, *args):
        kept, sent = shape((size, quarter), F32), shape((size, quarter), BF16)
        return call(kernel, [kept] + [sent] * (parts - 1), *args)

    own, *pieces = split(functools.partial(wide_kernel, rows), wide_rows, 4, kept, came)
    came = [stage(piece, step, 0) for step, piece in zip(STEPS, pieces)]
    own, *pieces = split(narrow_kernel, narrow_rows, 4, own, *came)
    came = [stage(piece, step, 1) for step, piece in zip(STEPS, pieces)]
    if rest > 1:
        own, *pieces = split(rest_kernel, rows, rest, own, *came)
        came = [along_rest(piece, k + 1) for k, piece in enumerate(pieces)]
    new_w, grad = call(
        update_kernel, [shape((rows, quarter), BF16)] * 2, weight, first_moment, second_moment, own, *came,
    )

    pieces = [along_rest(new_w, k) for k in range(1, rest)]
    *parts, far_grad = call(
        rest_back_kernel,
        [shape((narrow_rows, quarter), BF16)] * len(STEPS) + [shape((rows, quarter), BF16)], grad, new_w, *pieces,
    )
    came = [stage(part, step, 0) for step, part in zip(STEPS, parts)]
    far_grad = along_x(far_grad)
    parts = call(
        narrow_back_kernel, [shape((wide_rows, quarter), BF16)] * len(STEPS), parts[-1], *came, far_grad,
    )
    came = [stage(part, step, 1) for step, part in zip(STEPS, parts)]
    own = to_sibling(parts[-1])

    landed = to_sibling(call(
        pack_kernel, [shape((len(STEPS) * wide_rows + 2 * rows, quarter), BF16)], *came, grad, far_grad, own,
    )[0])
    outs = [shape((all_rows, width), BF16), shape((rows, width), F32), shape((rows, width), F32)]
    scratch = [pltpu.VMEM((all_rows, half), BF16)] + [pltpu.VMEM((2, rows, quarter), F32)] * 2
    scratch += [pltpu.SemaphoreType.DMA((5,))]
    written = call(
        write_own_kernel, outs, first_moment, second_moment, grad, far_grad, parts[-1], *came,
        far_out=3, scratch=scratch,
    )
    return tuple(call(
        write_other_kernel, outs, first_moment, second_moment, own, landed, *written,
        far_in=(4, 5, 6), far_out=3, scratch=scratch, aliases={4: 0, 5: 1, 6: 2},
    ))


def solution(mesh):
    return jax.shard_map(
        body,
        mesh=mesh,
        in_specs=(
            P(("rep", "shard"), None),
            P(("rep", "shard"), None),
            P("shard", None),
            P("shard", None),
            P("shard", None),
        ),
        out_specs=(P(), P("shard", None), P("shard", None)),
        check_vma=False,
    )
```

```python
import functools

import jax
import jax.numpy as jnp
from jax import lax
from jax.experimental import pallas as pl
from jax.experimental.pallas import tpu as pltpu
from jax.sharding import PartitionSpec as P

F32 = jnp.float32
BF16 = jnp.bfloat16
CHUNK = 512
LOAD_LIMIT = 48 * 1024 * 1024
KEPT_LIMIT = 50 * 1024 * 1024


def adamw_moments(first_moment, second_moment, grad):
    new_first = 0.9 * first_moment + 0.1 * grad
    new_second = 0.999 * second_moment + 0.001 * grad * grad
    return new_first, new_second


def adamw_weight(weight, new_first, new_second):
    corr_one = 0.9999734386011124
    corr_two = 0.0952078528
    wfloat = weight.astype(F32)
    update = new_first / corr_one / (jnp.sqrt(new_second / corr_two) + 1e-08)
    return (wfloat - 0.05 * (update + 0.1 * wfloat)).astype(BF16)


def shape(dims, kind):
    return jax.ShapeDtypeStruct(dims, kind)


def call(kernel, outs, *args, far_in=(), far_out=0, scratch=(), aliases=None, limit=48 * 1024 * 1024):
    near, far = pl.BlockSpec(memory_space=pltpu.VMEM), pl.BlockSpec(memory_space=pltpu.HBM)
    return pl.pallas_call(
        kernel,
        out_shape=outs,
        in_specs=[far if i in tuple(far_in) else near for i in range(len(args))],
        out_specs=[far if i < far_out else near for i in range(len(outs))],
        scratch_shapes=scratch,
        input_output_aliases=aliases or {},
        compiler_params=pltpu.CompilerParams(vmem_limit_bytes=limit),
    )(*args)


def exchange(value, other):
    reps, shards = lax.axis_size("rep"), lax.axis_size("shard")
    pairs = []
    for rep in range(reps):
        for shard in range(shards):
            to_rep, to_shard = other(rep, shard)
            pairs.append((rep * shards + shard, to_rep * shards + to_shard))
    return lax.ppermute(value, ("rep", "shard"), pairs)


def to_sibling(value):
    return exchange(value, lambda rep, shard: (rep ^ 1, shard))


SQUARE = ((1, 1), (1, 0), (0, 1))
LINE = (2, 3, 1)
STEPS = tuple(zip(SQUARE, LINE))
STAY = ((0, 0), 0)


def role_of(rep, shard):
    return (rep ^ (rep >> 1) ^ shard ^ (shard >> 1)) & 1


def partner(rep, shard, dy, dx, k):
    return rep ^ (2 * dx) ^ ((dy ^ dx ^ k) & 1), shard ^ dy ^ (2 * k)


def stage(value, step, square_role):
    (dy, dx), k = step
    return exchange(
        value,
        lambda rep, shard: partner(rep, shard, dy, dx, 0) if role_of(rep, shard) == square_role
        else partner(rep, shard, 0, 0, k),
    )


def along_x(value):
    return exchange(value, lambda rep, shard: partner(rep, shard, 0, 1, 0))


def along_rest(value, k):
    return exchange(value, lambda rep, shard: (rep, shard ^ (8 * k)))


def place():
    rep, shard = lax.axis_index("rep"), lax.axis_index("shard")
    return role_of(rep, shard), rep >> 1, shard & 1, (shard >> 1) & 3, shard >> 3


def in_half(step, group):
    role, x, y, z, _ = place()
    (dy, dx), k = step
    first = role == 0
    return (
        jnp.where(first, y ^ dy, group >> 1), jnp.where(first, x ^ dx, group & 1), jnp.where(first, group, z ^ k),
    )


def group_of(step, line_role):
    role, x, y, z, _ = place()
    (dy, dx), k = step
    return jnp.where(role == line_role, z ^ k, 2 * (y ^ dy) + (x ^ dx))


def block(index, size):
    return pl.ds(pl.multiple_of(index * size, size), size)


def load_kernel(cots_ref, away, first, sems):
    role = place()[0]
    copies = []
    for out, side in ((away, 1 - role), (first, role)):
        at = pl.ds(pl.multiple_of(side * away.shape[1], CHUNK), out.shape[1])
        copies.append(pltpu.make_async_copy(cots_ref.at[:, at], out, sems.at[len(copies)]))
        copies[-1].start()
    for copy in copies:
        copy.wait()


def away_kernel(acts, cots, out, turned):
    turned[...] = acts[...].T
    for i in range(out.shape[1] // CHUNK):
        at = slice(i * CHUNK, (i + 1) * CHUNK)
        out[:, at] = jnp.dot(turned[...], cots[:, at], preferred_element_type=F32).astype(BF16)


def kept_kernel(turned, first, cots_ref, out, cots, sems):
    role = place()[0]
    ready, count = first.shape[1] // CHUNK, out.shape[1] // CHUNK
    copies = []
    for i in range(ready, count):
        source = cots_ref.at[:, block(role * count + i, CHUNK)]
        copies.append(pltpu.make_async_copy(source, cots.at[i - ready], sems.at[i - ready]))
        copies[-1].start()
    for i in range(count):
        at = slice(i * CHUNK, (i + 1) * CHUNK)
        if i >= ready:
            copies[i - ready].wait()
        chunk = cots[i - ready] if i >= ready else first[:, at]
        out[:, at] = jnp.dot(turned[...], chunk, preferred_element_type=F32)


def wide_kernel(rows, kept, came, own, *pieces):
    quarter = own.shape[1]
    count = own.shape[0] // (4 * rows)
    for step, out in zip((STAY,) + STEPS, (own,) + pieces):
        for group in range(4):
            y, x, z = in_half(step, group)
            cols = block(x, quarter)
            for w in range(count):
                at = block(8 * w + 2 * z + y, rows)
                total = kept[at, cols] + came[at, cols].astype(F32)
                to = (group * count + w) * rows
                out[to:to + rows, :] = total.astype(out.dtype)


def narrow_kernel(kept, *refs):
    came, (own, *pieces) = refs[:len(STEPS)], refs[len(STEPS):]
    for step, out in zip((STAY,) + STEPS, [own] + pieces):
        at = block(group_of(step, 0), out.shape[0])
        total = kept[at, :]
        for ref in came:
            total += ref[at, :].astype(F32)
        out[...] = total.astype(out.dtype)


def rest_kernel(kept, *refs):
    came, outs = refs[:len(STEPS)], refs[len(STEPS):]
    w = place()[4]
    for k, out in enumerate(outs):
        at = block(w ^ k, out.shape[0])
        total = kept[at, :]
        for ref in came:
            total += ref[at, :].astype(F32)
        out[...] = total.astype(out.dtype)


def update_kernel(w, m, v, own, *refs):
    pieces, (new_w, grad) = refs[:-2], refs[-2:]
    role, x, _, _, _ = place()
    total = own[...]
    for ref in pieces:
        total += ref[...].astype(F32)
    grad[...] = total.astype(BF16)
    at = block(role * 2 + x, total.shape[1])
    new_m, new_v = adamw_moments(m[:, at], v[:, at], total)
    new_w[...] = adamw_weight(w[:, at], new_m, new_v)


def put(outs, at, value):
    for out in outs:
        out[at, :] = value


def put(outs, at, value):
    for out in outs:
        out[at, :] = value


def rest_back_kernel(grad, *refs):
    pieces, (*outs, last) = refs[:-1 - len(STEPS)], refs[-1 - len(STEPS):]
    w = place()[4]
    rows = grad.shape[0]
    for k, ref in enumerate(pieces):
        put(outs, block(w ^ k, rows), ref[...])
    last[...] = grad[...]


def narrow_back_kernel(own, *refs):
    parts, outs = (own,) + refs[:len(STEPS)], refs[-len(STEPS):]
    for step, ref in zip((STAY,) + STEPS, parts):
        put(outs, block(group_of(step, 1), own.shape[0]), ref[...])


def half_blocks(sibling, parts, out):
    role, x, y, z, _ = place()
    square = (role == 1) != sibling
    size, quarter = parts[0].shape
    rows = out.shape[0] // lax.axis_size("shard")
    count = size // (4 * rows)
    for ((dy, dx), k), ref in zip((STAY,) + STEPS, parts):
        for group in range(4):
            to_y = jnp.where(square, y ^ dy, group >> 1)
            to_x = jnp.where(square, x ^ dx, group & 1)
            to_z = jnp.where(square, group, z ^ k)
            for w in range(count):
                at = (group * count + w) * rows
                out[block(8 * w + 2 * to_z + to_y, rows), block(to_x, quarter)] = ref[at:at + rows, :]


def pack_kernel(*refs):
    *parts, out = refs
    at = 0
    for ref in parts:
        out[at:at + ref.shape[0], :] = ref[...]
        at += ref.shape[0]


def write_half(sibling, parts, out, half, sem):
    half_blocks(sibling, parts, half)
    copy = pltpu.make_async_copy(half, out.at[:, block(place()[0] ^ sibling, half.shape[1])], sem)
    copy.start()
    return copy


def write_own_kernel(m, v, grad, far_grad, early, *refs):
    parts, (w_out, m_out, v_out, half, sem, new_m, new_v, sems) = refs[:1 + len(STEPS)], refs[1 + len(STEPS):]
    copies = [write_half(0, parts, w_out, half, sem)]
    role, x, _, _, _ = place()
    rows = grad.shape[0]
    tail = early.shape[0] - 2 * rows
    grads = [grad, far_grad] + [early.at[pl.ds(tail + i * rows, rows), :] for i in range(2)]
    for i, ref in enumerate(grads):
        cols = block(2 * (role ^ (i >> 1)) + (x ^ (i & 1)), grad.shape[1])
        new_m[:, cols], new_v[:, cols] = adamw_moments(m[:, cols], v[:, cols], ref[...].astype(F32))
    for i, (source, out) in enumerate(((new_m, m_out), (new_v, v_out))):
        copies.append(pltpu.make_async_copy(source, out, sems.at[i]))
        copies[-1].start()
    for copy in copies:
        copy.wait()


def write_other_kernel(early, late, _, out, half, sem):
    size = late.shape[0] // 2
    parts = [ref.at[pl.ds(i * size, size), :] for ref in (early, late) for i in range(2)]
    write_half(1, parts, out, half, sem).wait()


def body(hidden_acts, out_cotangent, weight, first_moment, second_moment):
    rows, width = weight.shape
    tokens, all_rows = hidden_acts.shape
    half, quarter = width // 2, width // 4
    rest = lax.axis_size("shard") // 8
    wide_rows, narrow_rows = all_rows // 2, all_rows // 8

    away_cots, first = call(
        load_kernel, [shape((tokens, half), BF16), shape((tokens, CHUNK), BF16)], out_cotangent,
        far_in=(0,), scratch=[pltpu.SemaphoreType.DMA((2,))], limit=LOAD_LIMIT,
    )
    away, turned = call(
        away_kernel, [shape((all_rows, half), BF16), shape((all_rows, tokens), BF16)], hidden_acts, away_cots,
    )
    came = to_sibling(away)
    later = half // CHUNK - 1
    kept = call(
        kept_kernel, [shape((all_rows, half), F32)], turned, first, out_cotangent,
        far_in=(2,), limit=KEPT_LIMIT,
        scratch=[pltpu.VMEM((later, tokens, CHUNK), BF16), pltpu.SemaphoreType.DMA((later,))],
    )[0]

    def split(kernel, size, parts, *args):
        kept, sent = shape((size, quarter), F32), shape((size, quarter), BF16)
        return call(kernel, [kept] + [sent] * (parts - 1), *args)

    own, *pieces = split(functools.partial(wide_kernel, rows), wide_rows, 4, kept, came)
    came = [stage(piece, step, 0) for step, piece in zip(STEPS, pieces)]
    own, *pieces = split(narrow_kernel, narrow_rows, 4, own, *came)
    came = [stage(piece, step, 1) for step, piece in zip(STEPS, pieces)]
    if rest > 1:
        own, *pieces = split(rest_kernel, rows, rest, own, *came)
        came = [along_rest(piece, k + 1) for k, piece in enumerate(pieces)]
    new_w, grad = call(
        update_kernel, [shape((rows, quarter), BF16)] * 2, weight, first_moment, second_moment, own, *came,
    )

    pieces = [along_rest(new_w, k) for k in range(1, rest)]
    *parts, far_grad = call(
        rest_back_kernel,
        [shape((narrow_rows, quarter), BF16)] * len(STEPS) + [shape((rows, quarter), BF16)], grad, new_w, *pieces,
    )
    came = [stage(part, step, 0) for step, part in zip(STEPS, parts)]
    far_grad = along_x(far_grad)
    parts = call(
        narrow_back_kernel, [shape((wide_rows, quarter), BF16)] * len(STEPS), parts[-1], *came, far_grad,
    )
    came = [stage(part, step, 1) for step, part in zip(STEPS, parts)]

    def swapped(size, *args):
        return to_sibling(call(pack_kernel, [shape((size, quarter), BF16)], *args)[0])

    early = swapped(2 * wide_rows + 2 * rows, parts[-1], came[0], grad, far_grad)
    late = swapped(2 * wide_rows, came[1], came[2])
    new_w = [shape((all_rows, width), BF16)]
    moments = [shape((rows, width), F32)] * 2
    scratch = [pltpu.VMEM((all_rows, half), BF16), pltpu.SemaphoreType.DMA]
    written, new_m, new_v = call(
        write_own_kernel, new_w + moments, first_moment, second_moment, grad, far_grad, early, parts[-1], *came,
        far_out=3, scratch=scratch + [pltpu.VMEM((rows, width), F32)] * 2 + [pltpu.SemaphoreType.DMA((2,))],
    )
    written = call(
        write_other_kernel, new_w, early, late, written, far_in=(2,), far_out=1, scratch=scratch, aliases={2: 0},
    )[0]
    return written, new_m, new_v


def solution(mesh):
    return jax.shard_map(
        body,
        mesh=mesh,
        in_specs=(
            P(("rep", "shard"), None),
            P(("rep", "shard"), None),
            P("shard", None),
            P("shard", None),
            P("shard", None),
        ),
        out_specs=(P(), P("shard", None), P("shard", None)),
        check_vma=False,
    )
```

```python
import functools

import jax
import jax.numpy as jnp
from jax import lax
from jax.experimental import pallas as pl
from jax.experimental.pallas import tpu as pltpu
from jax.sharding import PartitionSpec as P

F32 = jnp.float32
BF16 = jnp.bfloat16
CHUNK = 512
LOAD_LIMIT = 48 * 1024 * 1024
KEPT_LIMIT = 50 * 1024 * 1024


def adamw_moments(first_moment, second_moment, grad):
    new_first = 0.9 * first_moment + 0.1 * grad
    new_second = 0.999 * second_moment + 0.001 * grad * grad
    return new_first, new_second


def adamw_weight(weight, new_first, new_second):
    corr_one = 0.9999734386011124
    corr_two = 0.0952078528
    wfloat = weight.astype(F32)
    update = new_first / corr_one / (jnp.sqrt(new_second / corr_two) + 1e-08)
    return (wfloat - 0.05 * (update + 0.1 * wfloat)).astype(BF16)


def shape(dims, kind):
    return jax.ShapeDtypeStruct(dims, kind)


def call(kernel, outs, *args, far_in=(), far_out=0, scratch=(), aliases=None, limit=48 * 1024 * 1024):
    near, far = pl.BlockSpec(memory_space=pltpu.VMEM), pl.BlockSpec(memory_space=pltpu.HBM)
    return pl.pallas_call(
        kernel,
        out_shape=outs,
        in_specs=[far if i in tuple(far_in) else near for i in range(len(args))],
        out_specs=[far if i < far_out else near for i in range(len(outs))],
        scratch_shapes=scratch,
        input_output_aliases=aliases or {},
        compiler_params=pltpu.CompilerParams(vmem_limit_bytes=limit),
    )(*args)


def exchange(value, other):
    reps, shards = lax.axis_size("rep"), lax.axis_size("shard")
    pairs = []
    for rep in range(reps):
        for shard in range(shards):
            to_rep, to_shard = other(rep, shard)
            pairs.append((rep * shards + shard, to_rep * shards + to_shard))
    return lax.ppermute(value, ("rep", "shard"), pairs)


def to_sibling(value):
    return exchange(value, lambda rep, shard: (rep ^ 1, shard))


SQUARE = ((1, 1), (1, 0), (0, 1))
LINE = (2, 3, 1)
STEPS = tuple(zip(SQUARE, LINE))
STAY = ((0, 0), 0)


def role_of(rep, shard):
    return (rep ^ (rep >> 1) ^ shard ^ (shard >> 1)) & 1


def partner(rep, shard, dy, dx, k):
    return rep ^ (2 * dx) ^ ((dy ^ dx ^ k) & 1), shard ^ dy ^ (2 * k)


def stage(value, step, square_role):
    (dy, dx), k = step
    return exchange(
        value,
        lambda rep, shard: partner(rep, shard, dy, dx, 0) if role_of(rep, shard) == square_role
        else partner(rep, shard, 0, 0, k),
    )


def along_x(value):
    return exchange(value, lambda rep, shard: partner(rep, shard, 0, 1, 0))


def along_rest(value, k):
    return exchange(value, lambda rep, shard: (rep, shard ^ (8 * k)))


def place():
    rep, shard = lax.axis_index("rep"), lax.axis_index("shard")
    return role_of(rep, shard), rep >> 1, shard & 1, (shard >> 1) & 3, shard >> 3


def in_half(step, group):
    role, x, y, z, _ = place()
    (dy, dx), k = step
    first = role == 0
    return (
        jnp.where(first, y ^ dy, group >> 1), jnp.where(first, x ^ dx, group & 1), jnp.where(first, group, z ^ k),
    )


def group_of(step, line_role):
    role, x, y, z, _ = place()
    (dy, dx), k = step
    return jnp.where(role == line_role, z ^ k, 2 * (y ^ dy) + (x ^ dx))


def block(index, size):
    return pl.ds(pl.multiple_of(index * size, size), size)


def load_kernel(cots_ref, away, sem):
    copy = pltpu.make_async_copy(cots_ref.at[:, block(1 - place()[0], away.shape[1])], away, sem)
    copy.start()
    copy.wait()


def away_kernel(acts, cots, out, turned):
    turned[...] = acts[...].T
    for i in range(out.shape[1] // CHUNK):
        at = slice(i * CHUNK, (i + 1) * CHUNK)
        out[:, at] = jnp.dot(turned[...], cots[:, at], preferred_element_type=F32).astype(BF16)


def kept_kernel(turned, cots_ref, out, cots, sems):
    role = place()[0]
    count = cots.shape[0]
    copies = []
    for i in range(count):
        source = cots_ref.at[:, block(role * count + i, CHUNK)]
        copies.append(pltpu.make_async_copy(source, cots.at[i], sems.at[i]))
        copies[-1].start()
    for i in range(count):
        copies[i].wait()
        at = slice(i * CHUNK, (i + 1) * CHUNK)
        out[:, at] = jnp.dot(turned[...], cots[i], preferred_element_type=F32)


def wide_kernel(rows, kept, came, own, *pieces):
    quarter = own.shape[1]
    count = own.shape[0] // (4 * rows)
    for step, out in zip((STAY,) + STEPS, (own,) + pieces):
        for group in range(4):
            y, x, z = in_half(step, group)
            cols = block(x, quarter)
            for w in range(count):
                at = block(8 * w + 2 * z + y, rows)
                total = kept[at, cols] + came[at, cols].astype(F32)
                to = (group * count + w) * rows
                out[to:to + rows, :] = total.astype(out.dtype)


def narrow_kernel(kept, *refs):
    came, (own, *pieces) = refs[:len(STEPS)], refs[len(STEPS):]
    for step, out in zip((STAY,) + STEPS, [own] + pieces):
        at = block(group_of(step, 0), out.shape[0])
        total = kept[at, :]
        for ref in came:
            total += ref[at, :].astype(F32)
        out[...] = total.astype(out.dtype)


def rest_kernel(kept, *refs):
    came, outs = refs[:len(STEPS)], refs[len(STEPS):]
    w = place()[4]
    for k, out in enumerate(outs):
        at = block(w ^ k, out.shape[0])
        total = kept[at, :]
        for ref in came:
            total += ref[at, :].astype(F32)
        out[...] = total.astype(out.dtype)


def update_kernel(w, m, v, own, *refs):
    pieces, (new_w, grad) = refs[:-2], refs[-2:]
    role, x, _, _, _ = place()
    total = own[...]
    for ref in pieces:
        total += ref[...].astype(F32)
    grad[...] = total.astype(BF16)
    at = block(role * 2 + x, total.shape[1])
    new_m, new_v = adamw_moments(m[:, at], v[:, at], total)
    new_w[...] = adamw_weight(w[:, at], new_m, new_v)


def put(outs, at, value):
    for out in outs:
        out[at, :] = value


def put(outs, at, value):
    for out in outs:
        out[at, :] = value


def rest_back_kernel(grad, *refs):
    pieces, (*outs, last) = refs[:-1 - len(STEPS)], refs[-1 - len(STEPS):]
    w = place()[4]
    rows = grad.shape[0]
    for k, ref in enumerate(pieces):
        put(outs, block(w ^ k, rows), ref[...])
    last[...] = grad[...]


def narrow_back_kernel(own, *refs):
    parts, outs = (own,) + refs[:len(STEPS)], refs[-len(STEPS):]
    for step, ref in zip((STAY,) + STEPS, parts):
        put(outs, block(group_of(step, 1), own.shape[0]), ref[...])


def half_blocks(sibling, parts, out):
    role, x, y, z, _ = place()
    square = (role == 1) != sibling
    size, quarter = parts[0].shape
    rows = out.shape[0] // lax.axis_size("shard")
    count = size // (4 * rows)
    for ((dy, dx), k), ref in zip((STAY,) + STEPS, parts):
        for group in range(4):
            to_y = jnp.where(square, y ^ dy, group >> 1)
            to_x = jnp.where(square, x ^ dx, group & 1)
            to_z = jnp.where(square, group, z ^ k)
            for w in range(count):
                at = (group * count + w) * rows
                out[block(8 * w + 2 * to_z + to_y, rows), block(to_x, quarter)] = ref[at:at + rows, :]


def pack_kernel(*refs):
    *parts, out = refs
    at = 0
    for ref in parts:
        out[at:at + ref.shape[0], :] = ref[...]
        at += ref.shape[0]


def write_half(sibling, parts, out, half, sem):
    half_blocks(sibling, parts, half)
    copy = pltpu.make_async_copy(half, out.at[:, block(place()[0] ^ sibling, half.shape[1])], sem)
    copy.start()
    return copy


def write_own_kernel(m, v, grad, far_grad, early, *refs):
    parts, (w_out, m_out, v_out, half, sem, new_m, new_v, sems) = refs[:1 + len(STEPS)], refs[1 + len(STEPS):]
    copies = [write_half(0, parts, w_out, half, sem)]
    role, x, _, _, _ = place()
    rows = grad.shape[0]
    tail = early.shape[0] - 2 * rows
    grads = [grad, far_grad] + [early.at[pl.ds(tail + i * rows, rows), :] for i in range(2)]
    for i, ref in enumerate(grads):
        cols = block(2 * (role ^ (i >> 1)) + (x ^ (i & 1)), grad.shape[1])
        new_m[:, cols], new_v[:, cols] = adamw_moments(m[:, cols], v[:, cols], ref[...].astype(F32))
    for i, (source, out) in enumerate(((new_m, m_out), (new_v, v_out))):
        copies.append(pltpu.make_async_copy(source, out, sems.at[i]))
        copies[-1].start()
    for copy in copies:
        copy.wait()


def write_other_kernel(early, late, _, out, half, sem):
    size = late.shape[0] // 2
    parts = [ref.at[pl.ds(i * size, size), :] for ref in (early, late) for i in range(2)]
    write_half(1, parts, out, half, sem).wait()


def body(hidden_acts, out_cotangent, weight, first_moment, second_moment):
    rows, width = weight.shape
    tokens, all_rows = hidden_acts.shape
    half, quarter = width // 2, width // 4
    rest = lax.axis_size("shard") // 8
    wide_rows, narrow_rows = all_rows // 2, all_rows // 8

    away_cots = call(
        load_kernel, [shape((tokens, half), BF16)], out_cotangent,
        far_in=(0,), scratch=[pltpu.SemaphoreType.DMA], limit=LOAD_LIMIT,
    )[0]
    away, turned = call(
        away_kernel, [shape((all_rows, half), BF16), shape((all_rows, tokens), BF16)], hidden_acts, away_cots,
    )
    came = to_sibling(away)
    count = half // CHUNK
    kept = call(
        kept_kernel, [shape((all_rows, half), F32)], turned, out_cotangent, far_in=(1,), limit=KEPT_LIMIT,
        scratch=[pltpu.VMEM((count, tokens, CHUNK), BF16), pltpu.SemaphoreType.DMA((count,))],
    )[0]

    def split(kernel, size, parts, *args):
        kept, sent = shape((size, quarter), F32), shape((size, quarter), BF16)
        return call(kernel, [kept] + [sent] * (parts - 1), *args)

    own, *pieces = split(functools.partial(wide_kernel, rows), wide_rows, 4, kept, came)
    came = [stage(piece, step, 0) for step, piece in zip(STEPS, pieces)]
    own, *pieces = split(narrow_kernel, narrow_rows, 4, own, *came)
    came = [stage(piece, step, 1) for step, piece in zip(STEPS, pieces)]
    if rest > 1:
        own, *pieces = split(rest_kernel, rows, rest, own, *came)
        came = [along_rest(piece, k + 1) for k, piece in enumerate(pieces)]
    new_w, grad = call(
        update_kernel, [shape((rows, quarter), BF16)] * 2, weight, first_moment, second_moment, own, *came,
    )

    pieces = [along_rest(new_w, k) for k in range(1, rest)]
    *parts, far_grad = call(
        rest_back_kernel,
        [shape((narrow_rows, quarter), BF16)] * len(STEPS) + [shape((rows, quarter), BF16)], grad, new_w, *pieces,
    )
    came = [stage(part, step, 0) for step, part in zip(STEPS, parts)]
    far_grad = along_x(far_grad)
    parts = call(
        narrow_back_kernel, [shape((wide_rows, quarter), BF16)] * len(STEPS), parts[-1], *came, far_grad,
    )
    came = [stage(part, step, 1) for step, part in zip(STEPS, parts)]

    def swapped(size, *args):
        return to_sibling(call(pack_kernel, [shape((size, quarter), BF16)], *args)[0])

    early = swapped(2 * wide_rows + 2 * rows, parts[-1], came[0], grad, far_grad)
    late = swapped(2 * wide_rows, came[1], came[2])
    new_w = [shape((all_rows, width), BF16)]
    moments = [shape((rows, width), F32)] * 2
    scratch = [pltpu.VMEM((all_rows, half), BF16), pltpu.SemaphoreType.DMA]
    written, new_m, new_v = call(
        write_own_kernel, new_w + moments, first_moment, second_moment, grad, far_grad, early, parts[-1], *came,
        far_out=3, scratch=scratch + [pltpu.VMEM((rows, width), F32)] * 2 + [pltpu.SemaphoreType.DMA((2,))],
    )
    written = call(
        write_other_kernel, new_w, early, late, written, far_in=(2,), far_out=1, scratch=scratch, aliases={2: 0},
    )[0]
    return written, new_m, new_v


def solution(mesh):
    return jax.shard_map(
        body,
        mesh=mesh,
        in_specs=(
            P(("rep", "shard"), None),
            P(("rep", "shard"), None),
            P("shard", None),
            P("shard", None),
            P("shard", None),
        ),
        out_specs=(P(), P("shard", None), P("shard", None)),
        check_vma=False,
    )
```

```python
import functools

import jax
import jax.numpy as jnp
from jax import lax
from jax.experimental import pallas as pl
from jax.experimental.pallas import tpu as pltpu
from jax.sharding import PartitionSpec as P

F32 = jnp.float32
BF16 = jnp.bfloat16
CHUNK = 512
LOAD_LIMIT = 48 * 1024 * 1024
KEPT_LIMIT = 50 * 1024 * 1024


def adamw_moments(first_moment, second_moment, grad):
    new_first = 0.9 * first_moment + 0.1 * grad
    new_second = 0.999 * second_moment + 0.001 * grad * grad
    return new_first, new_second


def adamw_weight(weight, new_first, new_second):
    corr_one = 0.9999734386011124
    corr_two = 0.0952078528
    wfloat = weight.astype(F32)
    update = new_first / corr_one / (jnp.sqrt(new_second / corr_two) + 1e-08)
    return (wfloat - 0.05 * (update + 0.1 * wfloat)).astype(BF16)


def shape(dims, kind):
    return jax.ShapeDtypeStruct(dims, kind)


def call(kernel, outs, *args, far_in=(), far_out=0, scratch=(), aliases=None, limit=48 * 1024 * 1024):
    near, far = pl.BlockSpec(memory_space=pltpu.VMEM), pl.BlockSpec(memory_space=pltpu.HBM)
    return pl.pallas_call(
        kernel,
        out_shape=outs,
        in_specs=[far if i in tuple(far_in) else near for i in range(len(args))],
        out_specs=[far if i < far_out else near for i in range(len(outs))],
        scratch_shapes=scratch,
        input_output_aliases=aliases or {},
        compiler_params=pltpu.CompilerParams(vmem_limit_bytes=limit),
    )(*args)


def exchange(value, other):
    reps, shards = lax.axis_size("rep"), lax.axis_size("shard")
    pairs = []
    for rep in range(reps):
        for shard in range(shards):
            to_rep, to_shard = other(rep, shard)
            pairs.append((rep * shards + shard, to_rep * shards + to_shard))
    return lax.ppermute(value, ("rep", "shard"), pairs)


def to_sibling(value):
    return exchange(value, lambda rep, shard: (rep ^ 1, shard))


SQUARE = ((1, 1), (0, 1), (1, 0))
LINE = (2, 3, 1)
STEPS = tuple(zip(SQUARE, LINE))
STAY = ((0, 0), 0)


def role_of(rep, shard):
    return (rep ^ (rep >> 1) ^ shard ^ (shard >> 1)) & 1


def partner(rep, shard, dy, dx, k):
    return rep ^ (2 * dx) ^ ((dy ^ dx ^ k) & 1), shard ^ dy ^ (2 * k)


def stage(value, step, square_role):
    (dy, dx), k = step
    return exchange(
        value,
        lambda rep, shard: partner(rep, shard, dy, dx, 0) if role_of(rep, shard) == square_role
        else partner(rep, shard, 0, 0, k),
    )


def along_x(value):
    return exchange(value, lambda rep, shard: partner(rep, shard, 0, 1, 0))


def along_rest(value, k):
    return exchange(value, lambda rep, shard: (rep, shard ^ (8 * k)))


def place():
    rep, shard = lax.axis_index("rep"), lax.axis_index("shard")
    return role_of(rep, shard), rep >> 1, shard & 1, (shard >> 1) & 3, shard >> 3


def in_half(step, group):
    role, x, y, z, _ = place()
    (dy, dx), k = step
    first = role == 0
    return (
        jnp.where(first, y ^ dy, group >> 1), jnp.where(first, x ^ dx, group & 1), jnp.where(first, group, z ^ k),
    )


def group_of(step, line_role):
    role, x, y, z, _ = place()
    (dy, dx), k = step
    return jnp.where(role == line_role, z ^ k, 2 * (y ^ dy) + (x ^ dx))


def block(index, size):
    return pl.ds(pl.multiple_of(index * size, size), size)


def load_kernel(cots_ref, away, sem):
    copy = pltpu.make_async_copy(cots_ref.at[:, block(1 - place()[0], away.shape[1])], away, sem)
    copy.start()
    copy.wait()


def away_kernel(acts, cots, out, turned):
    turned[...] = acts[...].T
    for i in range(out.shape[1] // CHUNK):
        at = slice(i * CHUNK, (i + 1) * CHUNK)
        out[:, at] = jnp.dot(turned[...], cots[:, at], preferred_element_type=F32).astype(BF16)


def kept_kernel(turned, cots_ref, out, cots, sems):
    role = place()[0]
    count = cots.shape[0]
    copies = []
    for i in range(count):
        source = cots_ref.at[:, block(role * count + i, CHUNK)]
        copies.append(pltpu.make_async_copy(source, cots.at[i], sems.at[i]))
        copies[-1].start()
    for i in range(count):
        copies[i].wait()
        at = slice(i * CHUNK, (i + 1) * CHUNK)
        out[:, at] = jnp.dot(turned[...], cots[i], preferred_element_type=F32)


def wide_kernel(rows, kept, came, own, *pieces):
    quarter = own.shape[1]
    count = own.shape[0] // (4 * rows)
    for step, out in zip((STAY,) + STEPS, (own,) + pieces):
        for group in range(4):
            y, x, z = in_half(step, group)
            cols = block(x, quarter)
            for w in range(count):
                at = block(8 * w + 2 * z + y, rows)
                total = kept[at, cols] + came[at, cols].astype(F32)
                to = (group * count + w) * rows
                out[to:to + rows, :] = total.astype(out.dtype)


def narrow_kernel(kept, *refs):
    came, (own, *pieces) = refs[:len(STEPS)], refs[len(STEPS):]
    for step, out in zip((STAY,) + STEPS, [own] + pieces):
        at = block(group_of(step, 0), out.shape[0])
        total = kept[at, :]
        for ref in came:
            total += ref[at, :].astype(F32)
        out[...] = total.astype(out.dtype)


def rest_kernel(kept, *refs):
    came, outs = refs[:len(STEPS)], refs[len(STEPS):]
    w = place()[4]
    for k, out in enumerate(outs):
        at = block(w ^ k, out.shape[0])
        total = kept[at, :]
        for ref in came:
            total += ref[at, :].astype(F32)
        out[...] = total.astype(out.dtype)


def update_kernel(w, m, v, own, *refs):
    pieces, (new_w, grad) = refs[:-2], refs[-2:]
    role, x, _, _, _ = place()
    total = own[...]
    for ref in pieces:
        total += ref[...].astype(F32)
    grad[...] = total.astype(BF16)
    at = block(role * 2 + x, total.shape[1])
    new_m, new_v = adamw_moments(m[:, at], v[:, at], total)
    new_w[...] = adamw_weight(w[:, at], new_m, new_v)


def put(outs, at, value):
    for out in outs:
        out[at, :] = value


def put(outs, at, value):
    for out in outs:
        out[at, :] = value


def rest_back_kernel(grad, *refs):
    pieces, (*outs, last) = refs[:-1 - len(STEPS)], refs[-1 - len(STEPS):]
    w = place()[4]
    rows = grad.shape[0]
    for k, ref in enumerate(pieces):
        put(outs, block(w ^ k, rows), ref[...])
    last[...] = grad[...]


def narrow_back_kernel(own, *refs):
    parts, outs = (own,) + refs[:len(STEPS)], refs[-len(STEPS):]
    for step, ref in zip((STAY,) + STEPS, parts):
        put(outs, block(group_of(step, 1), own.shape[0]), ref[...])


def half_blocks(sibling, parts, out):
    role, x, y, z, _ = place()
    square = (role == 1) != sibling
    size, quarter = parts[0].shape
    rows = out.shape[0] // lax.axis_size("shard")
    count = size // (4 * rows)
    for ((dy, dx), k), ref in zip((STAY,) + STEPS, parts):
        for group in range(4):
            to_y = jnp.where(square, y ^ dy, group >> 1)
            to_x = jnp.where(square, x ^ dx, group & 1)
            to_z = jnp.where(square, group, z ^ k)
            for w in range(count):
                at = (group * count + w) * rows
                out[block(8 * w + 2 * to_z + to_y, rows), block(to_x, quarter)] = ref[at:at + rows, :]


def pack_kernel(*refs):
    *parts, out = refs
    at = 0
    for ref in parts:
        out[at:at + ref.shape[0], :] = ref[...]
        at += ref.shape[0]


def write_half(sibling, parts, out, half, sem):
    half_blocks(sibling, parts, half)
    copy = pltpu.make_async_copy(half, out.at[:, block(place()[0] ^ sibling, half.shape[1])], sem)
    copy.start()
    return copy


def write_own_kernel(m, v, grad, far_grad, early, *refs):
    parts, (w_out, m_out, v_out, half, sem, new_m, new_v, sems) = refs[:1 + len(STEPS)], refs[1 + len(STEPS):]
    copies = [write_half(0, parts, w_out, half, sem)]
    role, x, _, _, _ = place()
    rows = grad.shape[0]
    tail = early.shape[0] - 2 * rows
    grads = [grad, far_grad] + [early.at[pl.ds(tail + i * rows, rows), :] for i in range(2)]
    for i, ref in enumerate(grads):
        cols = block(2 * (role ^ (i >> 1)) + (x ^ (i & 1)), grad.shape[1])
        new_m[:, cols], new_v[:, cols] = adamw_moments(m[:, cols], v[:, cols], ref[...].astype(F32))
    for i, (source, out) in enumerate(((new_m, m_out), (new_v, v_out))):
        copies.append(pltpu.make_async_copy(source, out, sems.at[i]))
        copies[-1].start()
    for copy in copies:
        copy.wait()


def write_other_kernel(early, late, _, out, half, sem):
    size = late.shape[0] // 2
    parts = [ref.at[pl.ds(i * size, size), :] for ref in (early, late) for i in range(2)]
    write_half(1, parts, out, half, sem).wait()


def body(hidden_acts, out_cotangent, weight, first_moment, second_moment):
    rows, width = weight.shape
    tokens, all_rows = hidden_acts.shape
    half, quarter = width // 2, width // 4
    rest = lax.axis_size("shard") // 8
    wide_rows, narrow_rows = all_rows // 2, all_rows // 8

    away_cots = call(
        load_kernel, [shape((tokens, half), BF16)], out_cotangent,
        far_in=(0,), scratch=[pltpu.SemaphoreType.DMA], limit=LOAD_LIMIT,
    )[0]
    away, turned = call(
        away_kernel, [shape((all_rows, half), BF16), shape((all_rows, tokens), BF16)], hidden_acts, away_cots,
    )
    came = to_sibling(away)
    count = half // CHUNK
    kept = call(
        kept_kernel, [shape((all_rows, half), F32)], turned, out_cotangent, far_in=(1,), limit=KEPT_LIMIT,
        scratch=[pltpu.VMEM((count, tokens, CHUNK), BF16), pltpu.SemaphoreType.DMA((count,))],
    )[0]

    def split(kernel, size, parts, *args):
        kept, sent = shape((size, quarter), F32), shape((size, quarter), BF16)
        return call(kernel, [kept] + [sent] * (parts - 1), *args)

    own, *pieces = split(functools.partial(wide_kernel, rows), wide_rows, 4, kept, came)
    came = [stage(piece, step, 0) for step, piece in zip(STEPS, pieces)]
    own, *pieces = split(narrow_kernel, narrow_rows, 4, own, *came)
    came = [stage(piece, step, 1) for step, piece in zip(STEPS, pieces)]
    if rest > 1:
        own, *pieces = split(rest_kernel, rows, rest, own, *came)
        came = [along_rest(piece, k + 1) for k, piece in enumerate(pieces)]
    new_w, grad = call(
        update_kernel, [shape((rows, quarter), BF16)] * 2, weight, first_moment, second_moment, own, *came,
    )

    pieces = [along_rest(new_w, k) for k in range(1, rest)]
    *parts, far_grad = call(
        rest_back_kernel,
        [shape((narrow_rows, quarter), BF16)] * len(STEPS) + [shape((rows, quarter), BF16)], grad, new_w, *pieces,
    )
    came = [stage(part, step, 0) for step, part in zip(STEPS, parts)]
    far_grad = along_x(far_grad)
    parts = call(
        narrow_back_kernel, [shape((wide_rows, quarter), BF16)] * len(STEPS), parts[-1], *came, far_grad,
    )
    came = [stage(part, step, 1) for step, part in zip(STEPS, parts)]

    def swapped(size, *args):
        return to_sibling(call(pack_kernel, [shape((size, quarter), BF16)], *args)[0])

    early = swapped(2 * wide_rows + 2 * rows, parts[-1], came[0], grad, far_grad)
    late = swapped(2 * wide_rows, came[1], came[2])
    new_w = [shape((all_rows, width), BF16)]
    moments = [shape((rows, width), F32)] * 2
    scratch = [pltpu.VMEM((all_rows, half), BF16), pltpu.SemaphoreType.DMA]
    written, new_m, new_v = call(
        write_own_kernel, new_w + moments, first_moment, second_moment, grad, far_grad, early, parts[-1], *came,
        far_out=3, scratch=scratch + [pltpu.VMEM((rows, width), F32)] * 2 + [pltpu.SemaphoreType.DMA((2,))],
    )
    written = call(
        write_other_kernel, new_w, early, late, written, far_in=(2,), far_out=1, scratch=scratch, aliases={2: 0},
    )[0]
    return written, new_m, new_v


def solution(mesh):
    return jax.shard_map(
        body,
        mesh=mesh,
        in_specs=(
            P(("rep", "shard"), None),
            P(("rep", "shard"), None),
            P("shard", None),
            P("shard", None),
            P("shard", None),
        ),
        out_specs=(P(), P("shard", None), P("shard", None)),
        check_vma=False,
    )
```

```python
import functools

import jax
import jax.numpy as jnp
from jax import lax
from jax.experimental import pallas as pl
from jax.experimental.pallas import tpu as pltpu
from jax.sharding import PartitionSpec as P

F32 = jnp.float32
BF16 = jnp.bfloat16
CHUNK = 512
LOAD_LIMIT = 48 * 1024 * 1024
KEPT_LIMIT = 50 * 1024 * 1024


def adamw_moments(first_moment, second_moment, grad):
    new_first = 0.9 * first_moment + 0.1 * grad
    new_second = 0.999 * second_moment + 0.001 * grad * grad
    return new_first, new_second


def adamw_weight(weight, new_first, new_second):
    corr_one = 0.9999734386011124
    corr_two = 0.0952078528
    wfloat = weight.astype(F32)
    update = new_first / corr_one / (jnp.sqrt(new_second / corr_two) + 1e-08)
    return (wfloat - 0.05 * (update + 0.1 * wfloat)).astype(BF16)


def shape(dims, kind):
    return jax.ShapeDtypeStruct(dims, kind)


def call(kernel, outs, *args, far_in=(), far_out=0, scratch=(), aliases=None, limit=48 * 1024 * 1024):
    near, far = pl.BlockSpec(memory_space=pltpu.VMEM), pl.BlockSpec(memory_space=pltpu.HBM)
    return pl.pallas_call(
        kernel,
        out_shape=outs,
        in_specs=[far if i in tuple(far_in) else near for i in range(len(args))],
        out_specs=[far if i < far_out else near for i in range(len(outs))],
        scratch_shapes=scratch,
        input_output_aliases=aliases or {},
        compiler_params=pltpu.CompilerParams(vmem_limit_bytes=limit),
    )(*args)


def exchange(value, other):
    reps, shards = lax.axis_size("rep"), lax.axis_size("shard")
    pairs = []
    for rep in range(reps):
        for shard in range(shards):
            to_rep, to_shard = other(rep, shard)
            pairs.append((rep * shards + shard, to_rep * shards + to_shard))
    return lax.ppermute(value, ("rep", "shard"), pairs)


def to_sibling(value):
    return exchange(value, lambda rep, shard: (rep ^ 1, shard))


SQUARE = ((1, 1), (1, 0), (0, 1))
LINE = (2, 3, 1)
STEPS = tuple(zip(SQUARE, LINE))
STAY = ((0, 0), 0)


def role_of(rep, shard):
    return (rep ^ (rep >> 1) ^ shard ^ (shard >> 1) ^ 1) & 1


def partner(rep, shard, dy, dx, k):
    return rep ^ (2 * dx) ^ ((dy ^ dx ^ k) & 1), shard ^ dy ^ (2 * k)


def stage(value, step, square_role):
    (dy, dx), k = step
    return exchange(
        value,
        lambda rep, shard: partner(rep, shard, dy, dx, 0) if role_of(rep, shard) == square_role
        else partner(rep, shard, 0, 0, k),
    )


def along_x(value):
    return exchange(value, lambda rep, shard: partner(rep, shard, 0, 1, 0))


def along_rest(value, k):
    return exchange(value, lambda rep, shard: (rep, shard ^ (8 * k)))


def place():
    rep, shard = lax.axis_index("rep"), lax.axis_index("shard")
    return role_of(rep, shard), rep >> 1, shard & 1, (shard >> 1) & 3, shard >> 3


def in_half(step, group):
    role, x, y, z, _ = place()
    (dy, dx), k = step
    first = role == 0
    return (
        jnp.where(first, y ^ dy, group >> 1), jnp.where(first, x ^ dx, group & 1), jnp.where(first, group, z ^ k),
    )


def group_of(step, line_role):
    role, x, y, z, _ = place()
    (dy, dx), k = step
    return jnp.where(role == line_role, z ^ k, 2 * (y ^ dy) + (x ^ dx))


def block(index, size):
    return pl.ds(pl.multiple_of(index * size, size), size)


def load_kernel(cots_ref, away, sem):
    copy = pltpu.make_async_copy(cots_ref.at[:, block(1 - place()[0], away.shape[1])], away, sem)
    copy.start()
    copy.wait()


def away_kernel(acts, cots, out, turned):
    turned[...] = acts[...].T
    for i in range(out.shape[1] // CHUNK):
        at = slice(i * CHUNK, (i + 1) * CHUNK)
        out[:, at] = jnp.dot(turned[...], cots[:, at], preferred_element_type=F32).astype(BF16)


def kept_kernel(turned, cots_ref, out, cots, sems):
    role = place()[0]
    count = cots.shape[0]
    copies = []
    for i in range(count):
        source = cots_ref.at[:, block(role * count + i, CHUNK)]
        copies.append(pltpu.make_async_copy(source, cots.at[i], sems.at[i]))
        copies[-1].start()
    for i in range(count):
        copies[i].wait()
        at = slice(i * CHUNK, (i + 1) * CHUNK)
        out[:, at] = jnp.dot(turned[...], cots[i], preferred_element_type=F32)


def wide_kernel(rows, kept, came, own, *pieces):
    quarter = own.shape[1]
    count = own.shape[0] // (4 * rows)
    for step, out in zip((STAY,) + STEPS, (own,) + pieces):
        for group in range(4):
            y, x, z = in_half(step, group)
            cols = block(x, quarter)
            for w in range(count):
                at = block(8 * w + 2 * z + y, rows)
                total = kept[at, cols] + came[at, cols].astype(F32)
                to = (group * count + w) * rows
                out[to:to + rows, :] = total.astype(out.dtype)


def narrow_kernel(kept, *refs):
    came, (own, *pieces) = refs[:len(STEPS)], refs[len(STEPS):]
    for step, out in zip((STAY,) + STEPS, [own] + pieces):
        at = block(group_of(step, 0), out.shape[0])
        total = kept[at, :]
        for ref in came:
            total += ref[at, :].astype(F32)
        out[...] = total.astype(out.dtype)


def rest_kernel(kept, *refs):
    came, outs = refs[:len(STEPS)], refs[len(STEPS):]
    w = place()[4]
    for k, out in enumerate(outs):
        at = block(w ^ k, out.shape[0])
        total = kept[at, :]
        for ref in came:
            total += ref[at, :].astype(F32)
        out[...] = total.astype(out.dtype)


def update_kernel(w, m, v, own, *refs):
    pieces, (new_w, grad) = refs[:-2], refs[-2:]
    role, x, _, _, _ = place()
    total = own[...]
    for ref in pieces:
        total += ref[...].astype(F32)
    grad[...] = total.astype(BF16)
    at = block(role * 2 + x, total.shape[1])
    new_m, new_v = adamw_moments(m[:, at], v[:, at], total)
    new_w[...] = adamw_weight(w[:, at], new_m, new_v)


def put(outs, at, value):
    for out in outs:
        out[at, :] = value


def put(outs, at, value):
    for out in outs:
        out[at, :] = value


def rest_back_kernel(grad, *refs):
    pieces, (*outs, last) = refs[:-1 - len(STEPS)], refs[-1 - len(STEPS):]
    w = place()[4]
    rows = grad.shape[0]
    for k, ref in enumerate(pieces):
        put(outs, block(w ^ k, rows), ref[...])
    last[...] = grad[...]


def narrow_back_kernel(own, *refs):
    parts, outs = (own,) + refs[:len(STEPS)], refs[-len(STEPS):]
    for step, ref in zip((STAY,) + STEPS, parts):
        put(outs, block(group_of(step, 1), own.shape[0]), ref[...])


def half_blocks(sibling, parts, out):
    role, x, y, z, _ = place()
    square = (role == 1) != sibling
    size, quarter = parts[0].shape
    rows = out.shape[0] // lax.axis_size("shard")
    count = size // (4 * rows)
    for ((dy, dx), k), ref in zip((STAY,) + STEPS, parts):
        for group in range(4):
            to_y = jnp.where(square, y ^ dy, group >> 1)
            to_x = jnp.where(square, x ^ dx, group & 1)
            to_z = jnp.where(square, group, z ^ k)
            for w in range(count):
                at = (group * count + w) * rows
                out[block(8 * w + 2 * to_z + to_y, rows), block(to_x, quarter)] = ref[at:at + rows, :]


def pack_kernel(*refs):
    *parts, out = refs
    at = 0
    for ref in parts:
        out[at:at + ref.shape[0], :] = ref[...]
        at += ref.shape[0]


def write_half(sibling, parts, out, half, sem):
    half_blocks(sibling, parts, half)
    copy = pltpu.make_async_copy(half, out.at[:, block(place()[0] ^ sibling, half.shape[1])], sem)
    copy.start()
    return copy


def write_own_kernel(m, v, grad, far_grad, early, *refs):
    parts, (w_out, m_out, v_out, half, sem, new_m, new_v, sems) = refs[:1 + len(STEPS)], refs[1 + len(STEPS):]
    copies = [write_half(0, parts, w_out, half, sem)]
    role, x, _, _, _ = place()
    rows = grad.shape[0]
    tail = early.shape[0] - 2 * rows
    grads = [grad, far_grad] + [early.at[pl.ds(tail + i * rows, rows), :] for i in range(2)]
    for i, ref in enumerate(grads):
        cols = block(2 * (role ^ (i >> 1)) + (x ^ (i & 1)), grad.shape[1])
        new_m[:, cols], new_v[:, cols] = adamw_moments(m[:, cols], v[:, cols], ref[...].astype(F32))
    for i, (source, out) in enumerate(((new_m, m_out), (new_v, v_out))):
        copies.append(pltpu.make_async_copy(source, out, sems.at[i]))
        copies[-1].start()
    for copy in copies:
        copy.wait()


def write_other_kernel(early, late, _, out, half, sem):
    size = late.shape[0] // 2
    parts = [ref.at[pl.ds(i * size, size), :] for ref in (early, late) for i in range(2)]
    write_half(1, parts, out, half, sem).wait()


def body(hidden_acts, out_cotangent, weight, first_moment, second_moment):
    rows, width = weight.shape
    tokens, all_rows = hidden_acts.shape
    half, quarter = width // 2, width // 4
    rest = lax.axis_size("shard") // 8
    wide_rows, narrow_rows = all_rows // 2, all_rows // 8

    away_cots = call(
        load_kernel, [shape((tokens, half), BF16)], out_cotangent,
        far_in=(0,), scratch=[pltpu.SemaphoreType.DMA], limit=LOAD_LIMIT,
    )[0]
    away, turned = call(
        away_kernel, [shape((all_rows, half), BF16), shape((all_rows, tokens), BF16)], hidden_acts, away_cots,
    )
    came = to_sibling(away)
    count = half // CHUNK
    kept = call(
        kept_kernel, [shape((all_rows, half), F32)], turned, out_cotangent, far_in=(1,), limit=KEPT_LIMIT,
        scratch=[pltpu.VMEM((count, tokens, CHUNK), BF16), pltpu.SemaphoreType.DMA((count,))],
    )[0]

    def split(kernel, size, parts, *args):
        kept, sent = shape((size, quarter), F32), shape((size, quarter), BF16)
        return call(kernel, [kept] + [sent] * (parts - 1), *args)

    own, *pieces = split(functools.partial(wide_kernel, rows), wide_rows, 4, kept, came)
    came = [stage(piece, step, 0) for step, piece in zip(STEPS, pieces)]
    own, *pieces = split(narrow_kernel, narrow_rows, 4, own, *came)
    came = [stage(piece, step, 1) for step, piece in zip(STEPS, pieces)]
    if rest > 1:
        own, *pieces = split(rest_kernel, rows, rest, own, *came)
        came = [along_rest(piece, k + 1) for k, piece in enumerate(pieces)]
    new_w, grad = call(
        update_kernel, [shape((rows, quarter), BF16)] * 2, weight, first_moment, second_moment, own, *came,
    )

    pieces = [along_rest(new_w, k) for k in range(1, rest)]
    *parts, far_grad = call(
        rest_back_kernel,
        [shape((narrow_rows, quarter), BF16)] * len(STEPS) + [shape((rows, quarter), BF16)], grad, new_w, *pieces,
    )
    came = [stage(part, step, 0) for step, part in zip(STEPS, parts)]
    far_grad = along_x(far_grad)
    parts = call(
        narrow_back_kernel, [shape((wide_rows, quarter), BF16)] * len(STEPS), parts[-1], *came, far_grad,
    )
    came = [stage(part, step, 1) for step, part in zip(STEPS, parts)]

    def swapped(size, *args):
        return to_sibling(call(pack_kernel, [shape((size, quarter), BF16)], *args)[0])

    early = swapped(2 * wide_rows + 2 * rows, parts[-1], came[0], grad, far_grad)
    late = swapped(2 * wide_rows, came[1], came[2])
    new_w = [shape((all_rows, width), BF16)]
    moments = [shape((rows, width), F32)] * 2
    scratch = [pltpu.VMEM((all_rows, half), BF16), pltpu.SemaphoreType.DMA]
    written, new_m, new_v = call(
        write_own_kernel, new_w + moments, first_moment, second_moment, grad, far_grad, early, parts[-1], *came,
        far_out=3, scratch=scratch + [pltpu.VMEM((rows, width), F32)] * 2 + [pltpu.SemaphoreType.DMA((2,))],
    )
    written = call(
        write_other_kernel, new_w, early, late, written, far_in=(2,), far_out=1, scratch=scratch, aliases={2: 0},
    )[0]
    return written, new_m, new_v


def solution(mesh):
    return jax.shard_map(
        body,
        mesh=mesh,
        in_specs=(
            P(("rep", "shard"), None),
            P(("rep", "shard"), None),
            P("shard", None),
            P("shard", None),
            P("shard", None),
        ),
        out_specs=(P(), P("shard", None), P("shard", None)),
        check_vma=False,
    )
```

```python
import functools

import jax
import jax.numpy as jnp
from jax import lax
from jax.experimental import pallas as pl
from jax.experimental.pallas import tpu as pltpu
from jax.sharding import PartitionSpec as P

F32 = jnp.float32
BF16 = jnp.bfloat16
CHUNK = 256
LOAD_LIMIT = 48 * 1024 * 1024
KEPT_LIMIT = 50 * 1024 * 1024


def adamw_moments(first_moment, second_moment, grad):
    new_first = 0.9 * first_moment + 0.1 * grad
    new_second = 0.999 * second_moment + 0.001 * grad * grad
    return new_first, new_second


def adamw_weight(weight, new_first, new_second):
    corr_one = 0.9999734386011124
    corr_two = 0.0952078528
    wfloat = weight.astype(F32)
    update = new_first / corr_one / (jnp.sqrt(new_second / corr_two) + 1e-08)
    return (wfloat - 0.05 * (update + 0.1 * wfloat)).astype(BF16)


def shape(dims, kind):
    return jax.ShapeDtypeStruct(dims, kind)


def call(kernel, outs, *args, far_in=(), far_out=0, scratch=(), aliases=None, limit=48 * 1024 * 1024):
    near, far = pl.BlockSpec(memory_space=pltpu.VMEM), pl.BlockSpec(memory_space=pltpu.HBM)
    return pl.pallas_call(
        kernel,
        out_shape=outs,
        in_specs=[far if i in tuple(far_in) else near for i in range(len(args))],
        out_specs=[far if i < far_out else near for i in range(len(outs))],
        scratch_shapes=scratch,
        input_output_aliases=aliases or {},
        compiler_params=pltpu.CompilerParams(vmem_limit_bytes=limit),
    )(*args)


def exchange(value, other):
    reps, shards = lax.axis_size("rep"), lax.axis_size("shard")
    pairs = []
    for rep in range(reps):
        for shard in range(shards):
            to_rep, to_shard = other(rep, shard)
            pairs.append((rep * shards + shard, to_rep * shards + to_shard))
    return lax.ppermute(value, ("rep", "shard"), pairs)


def to_sibling(value):
    return exchange(value, lambda rep, shard: (rep ^ 1, shard))


SQUARE = ((1, 1), (1, 0), (0, 1))
LINE = (2, 3, 1)
STEPS = tuple(zip(SQUARE, LINE))
STAY = ((0, 0), 0)


def role_of(rep, shard):
    return (rep ^ (rep >> 1) ^ shard ^ (shard >> 1)) & 1


def partner(rep, shard, dy, dx, k):
    return rep ^ (2 * dx) ^ ((dy ^ dx ^ k) & 1), shard ^ dy ^ (2 * k)


def stage(value, step, square_role):
    (dy, dx), k = step
    return exchange(
        value,
        lambda rep, shard: partner(rep, shard, dy, dx, 0) if role_of(rep, shard) == square_role
        else partner(rep, shard, 0, 0, k),
    )


def along_x(value):
    return exchange(value, lambda rep, shard: partner(rep, shard, 0, 1, 0))


def along_rest(value, k):
    return exchange(value, lambda rep, shard: (rep, shard ^ (8 * k)))


def place():
    rep, shard = lax.axis_index("rep"), lax.axis_index("shard")
    return role_of(rep, shard), rep >> 1, shard & 1, (shard >> 1) & 3, shard >> 3


def in_half(step, group):
    role, x, y, z, _ = place()
    (dy, dx), k = step
    first = role == 0
    return (
        jnp.where(first, y ^ dy, group >> 1), jnp.where(first, x ^ dx, group & 1), jnp.where(first, group, z ^ k),
    )


def group_of(step, line_role):
    role, x, y, z, _ = place()
    (dy, dx), k = step
    return jnp.where(role == line_role, z ^ k, 2 * (y ^ dy) + (x ^ dx))


def block(index, size):
    return pl.ds(pl.multiple_of(index * size, size), size)


def load_kernel(cots_ref, away, sem):
    copy = pltpu.make_async_copy(cots_ref.at[:, block(1 - place()[0], away.shape[1])], away, sem)
    copy.start()
    copy.wait()


def away_kernel(acts, cots, out, turned):
    turned[...] = acts[...].T
    for i in range(out.shape[1] // CHUNK):
        at = slice(i * CHUNK, (i + 1) * CHUNK)
        out[:, at] = jnp.dot(turned[...], cots[:, at], preferred_element_type=F32).astype(BF16)


def kept_kernel(turned, cots_ref, out, cots, sems):
    role = place()[0]
    count = cots.shape[0]
    copies = []
    for i in range(count):
        source = cots_ref.at[:, block(role * count + i, CHUNK)]
        copies.append(pltpu.make_async_copy(source, cots.at[i], sems.at[i]))
        copies[-1].start()
    for i in range(count):
        copies[i].wait()
        at = slice(i * CHUNK, (i + 1) * CHUNK)
        out[:, at] = jnp.dot(turned[...], cots[i], preferred_element_type=F32)


def wide_kernel(rows, kept, came, own, *pieces):
    quarter = own.shape[1]
    count = own.shape[0] // (4 * rows)
    for step, out in zip((STAY,) + STEPS, (own,) + pieces):
        for group in range(4):
            y, x, z = in_half(step, group)
            cols = block(x, quarter)
            for w in range(count):
                at = block(8 * w + 2 * z + y, rows)
                total = kept[at, cols] + came[at, cols].astype(F32)
                to = (group * count + w) * rows
                out[to:to + rows, :] = total.astype(out.dtype)


def narrow_kernel(kept, *refs):
    came, (own, *pieces) = refs[:len(STEPS)], refs[len(STEPS):]
    for step, out in zip((STAY,) + STEPS, [own] + pieces):
        at = block(group_of(step, 0), out.shape[0])
        total = kept[at, :]
        for ref in came:
            total += ref[at, :].astype(F32)
        out[...] = total.astype(out.dtype)


def rest_kernel(kept, *refs):
    came, outs = refs[:len(STEPS)], refs[len(STEPS):]
    w = place()[4]
    for k, out in enumerate(outs):
        at = block(w ^ k, out.shape[0])
        total = kept[at, :]
        for ref in came:
            total += ref[at, :].astype(F32)
        out[...] = total.astype(out.dtype)


def update_kernel(w, m, v, own, *refs):
    pieces, (new_w, grad) = refs[:-2], refs[-2:]
    role, x, _, _, _ = place()
    total = own[...]
    for ref in pieces:
        total += ref[...].astype(F32)
    grad[...] = total.astype(BF16)
    at = block(role * 2 + x, total.shape[1])
    new_m, new_v = adamw_moments(m[:, at], v[:, at], total)
    new_w[...] = adamw_weight(w[:, at], new_m, new_v)


def put(outs, at, value):
    for out in outs:
        out[at, :] = value


def put(outs, at, value):
    for out in outs:
        out[at, :] = value


def rest_back_kernel(grad, *refs):
    pieces, (*outs, last) = refs[:-1 - len(STEPS)], refs[-1 - len(STEPS):]
    w = place()[4]
    rows = grad.shape[0]
    for k, ref in enumerate(pieces):
        put(outs, block(w ^ k, rows), ref[...])
    last[...] = grad[...]


def narrow_back_kernel(own, *refs):
    parts, outs = (own,) + refs[:len(STEPS)], refs[-len(STEPS):]
    for step, ref in zip((STAY,) + STEPS, parts):
        put(outs, block(group_of(step, 1), own.shape[0]), ref[...])


def half_blocks(sibling, parts, out):
    role, x, y, z, _ = place()
    square = (role == 1) != sibling
    size, quarter = parts[0].shape
    rows = out.shape[0] // lax.axis_size("shard")
    count = size // (4 * rows)
    for ((dy, dx), k), ref in zip((STAY,) + STEPS, parts):
        for group in range(4):
            to_y = jnp.where(square, y ^ dy, group >> 1)
            to_x = jnp.where(square, x ^ dx, group & 1)
            to_z = jnp.where(square, group, z ^ k)
            for w in range(count):
                at = (group * count + w) * rows
                out[block(8 * w + 2 * to_z + to_y, rows), block(to_x, quarter)] = ref[at:at + rows, :]


def pack_kernel(*refs):
    *parts, out = refs
    at = 0
    for ref in parts:
        out[at:at + ref.shape[0], :] = ref[...]
        at += ref.shape[0]


def write_half(sibling, parts, out, half, sem):
    half_blocks(sibling, parts, half)
    copy = pltpu.make_async_copy(half, out.at[:, block(place()[0] ^ sibling, half.shape[1])], sem)
    copy.start()
    return copy


def write_own_kernel(m, v, grad, far_grad, early, *refs):
    parts, (w_out, m_out, v_out, half, sem, new_m, new_v, sems) = refs[:1 + len(STEPS)], refs[1 + len(STEPS):]
    copies = [write_half(0, parts, w_out, half, sem)]
    role, x, _, _, _ = place()
    rows = grad.shape[0]
    tail = early.shape[0] - 2 * rows
    grads = [grad, far_grad] + [early.at[pl.ds(tail + i * rows, rows), :] for i in range(2)]
    for i, ref in enumerate(grads):
        cols = block(2 * (role ^ (i >> 1)) + (x ^ (i & 1)), grad.shape[1])
        new_m[:, cols], new_v[:, cols] = adamw_moments(m[:, cols], v[:, cols], ref[...].astype(F32))
    for i, (source, out) in enumerate(((new_m, m_out), (new_v, v_out))):
        copies.append(pltpu.make_async_copy(source, out, sems.at[i]))
        copies[-1].start()
    for copy in copies:
        copy.wait()


def write_other_kernel(early, late, _, out, half, sem):
    size = late.shape[0] // 2
    parts = [ref.at[pl.ds(i * size, size), :] for ref in (early, late) for i in range(2)]
    write_half(1, parts, out, half, sem).wait()


def body(hidden_acts, out_cotangent, weight, first_moment, second_moment):
    rows, width = weight.shape
    tokens, all_rows = hidden_acts.shape
    half, quarter = width // 2, width // 4
    rest = lax.axis_size("shard") // 8
    wide_rows, narrow_rows = all_rows // 2, all_rows // 8

    away_cots = call(
        load_kernel, [shape((tokens, half), BF16)], out_cotangent,
        far_in=(0,), scratch=[pltpu.SemaphoreType.DMA], limit=LOAD_LIMIT,
    )[0]
    away, turned = call(
        away_kernel, [shape((all_rows, half), BF16), shape((all_rows, tokens), BF16)], hidden_acts, away_cots,
    )
    came = to_sibling(away)
    count = half // CHUNK
    kept = call(
        kept_kernel, [shape((all_rows, half), F32)], turned, out_cotangent, far_in=(1,), limit=KEPT_LIMIT,
        scratch=[pltpu.VMEM((count, tokens, CHUNK), BF16), pltpu.SemaphoreType.DMA((count,))],
    )[0]

    def split(kernel, size, parts, *args):
        kept, sent = shape((size, quarter), F32), shape((size, quarter), BF16)
        return call(kernel, [kept] + [sent] * (parts - 1), *args)

    own, *pieces = split(functools.partial(wide_kernel, rows), wide_rows, 4, kept, came)
    came = [stage(piece, step, 0) for step, piece in zip(STEPS, pieces)]
    own, *pieces = split(narrow_kernel, narrow_rows, 4, own, *came)
    came = [stage(piece, step, 1) for step, piece in zip(STEPS, pieces)]
    if rest > 1:
        own, *pieces = split(rest_kernel, rows, rest, own, *came)
        came = [along_rest(piece, k + 1) for k, piece in enumerate(pieces)]
    new_w, grad = call(
        update_kernel, [shape((rows, quarter), BF16)] * 2, weight, first_moment, second_moment, own, *came,
    )

    pieces = [along_rest(new_w, k) for k in range(1, rest)]
    *parts, far_grad = call(
        rest_back_kernel,
        [shape((narrow_rows, quarter), BF16)] * len(STEPS) + [shape((rows, quarter), BF16)], grad, new_w, *pieces,
    )
    came = [stage(part, step, 0) for step, part in zip(STEPS, parts)]
    far_grad = along_x(far_grad)
    parts = call(
        narrow_back_kernel, [shape((wide_rows, quarter), BF16)] * len(STEPS), parts[-1], *came, far_grad,
    )
    came = [stage(part, step, 1) for step, part in zip(STEPS, parts)]

    def swapped(size, *args):
        return to_sibling(call(pack_kernel, [shape((size, quarter), BF16)], *args)[0])

    early = swapped(2 * wide_rows + 2 * rows, parts[-1], came[0], grad, far_grad)
    late = swapped(2 * wide_rows, came[1], came[2])
    new_w = [shape((all_rows, width), BF16)]
    moments = [shape((rows, width), F32)] * 2
    scratch = [pltpu.VMEM((all_rows, half), BF16), pltpu.SemaphoreType.DMA]
    written, new_m, new_v = call(
        write_own_kernel, new_w + moments, first_moment, second_moment, grad, far_grad, early, parts[-1], *came,
        far_out=3, scratch=scratch + [pltpu.VMEM((rows, width), F32)] * 2 + [pltpu.SemaphoreType.DMA((2,))],
    )
    written = call(
        write_other_kernel, new_w, early, late, written, far_in=(2,), far_out=1, scratch=scratch, aliases={2: 0},
    )[0]
    return written, new_m, new_v


def solution(mesh):
    return jax.shard_map(
        body,
        mesh=mesh,
        in_specs=(
            P(("rep", "shard"), None),
            P(("rep", "shard"), None),
            P("shard", None),
            P("shard", None),
            P("shard", None),
        ),
        out_specs=(P(), P("shard", None), P("shard", None)),
        check_vma=False,
    )
```

```python
import functools

import jax
import jax.numpy as jnp
from jax import lax
from jax.experimental import pallas as pl
from jax.experimental.pallas import tpu as pltpu
from jax.sharding import PartitionSpec as P

F32 = jnp.float32
BF16 = jnp.bfloat16
CHUNK = 1024
LOAD_LIMIT = 48 * 1024 * 1024
KEPT_LIMIT = 50 * 1024 * 1024


def adamw_moments(first_moment, second_moment, grad):
    new_first = 0.9 * first_moment + 0.1 * grad
    new_second = 0.999 * second_moment + 0.001 * grad * grad
    return new_first, new_second


def adamw_weight(weight, new_first, new_second):
    corr_one = 0.9999734386011124
    corr_two = 0.0952078528
    wfloat = weight.astype(F32)
    update = new_first / corr_one / (jnp.sqrt(new_second / corr_two) + 1e-08)
    return (wfloat - 0.05 * (update + 0.1 * wfloat)).astype(BF16)


def shape(dims, kind):
    return jax.ShapeDtypeStruct(dims, kind)


def call(kernel, outs, *args, far_in=(), far_out=0, scratch=(), aliases=None, limit=48 * 1024 * 1024):
    near, far = pl.BlockSpec(memory_space=pltpu.VMEM), pl.BlockSpec(memory_space=pltpu.HBM)
    return pl.pallas_call(
        kernel,
        out_shape=outs,
        in_specs=[far if i in tuple(far_in) else near for i in range(len(args))],
        out_specs=[far if i < far_out else near for i in range(len(outs))],
        scratch_shapes=scratch,
        input_output_aliases=aliases or {},
        compiler_params=pltpu.CompilerParams(vmem_limit_bytes=limit),
    )(*args)


def exchange(value, other):
    reps, shards = lax.axis_size("rep"), lax.axis_size("shard")
    pairs = []
    for rep in range(reps):
        for shard in range(shards):
            to_rep, to_shard = other(rep, shard)
            pairs.append((rep * shards + shard, to_rep * shards + to_shard))
    return lax.ppermute(value, ("rep", "shard"), pairs)


def to_sibling(value):
    return exchange(value, lambda rep, shard: (rep ^ 1, shard))


SQUARE = ((1, 1), (1, 0), (0, 1))
LINE = (2, 3, 1)
STEPS = tuple(zip(SQUARE, LINE))
STAY = ((0, 0), 0)


def role_of(rep, shard):
    return (rep ^ (rep >> 1) ^ shard ^ (shard >> 1)) & 1


def partner(rep, shard, dy, dx, k):
    return rep ^ (2 * dx) ^ ((dy ^ dx ^ k) & 1), shard ^ dy ^ (2 * k)


def stage(value, step, square_role):
    (dy, dx), k = step
    return exchange(
        value,
        lambda rep, shard: partner(rep, shard, dy, dx, 0) if role_of(rep, shard) == square_role
        else partner(rep, shard, 0, 0, k),
    )


def along_x(value):
    return exchange(value, lambda rep, shard: partner(rep, shard, 0, 1, 0))


def along_rest(value, k):
    return exchange(value, lambda rep, shard: (rep, shard ^ (8 * k)))


def place():
    rep, shard = lax.axis_index("rep"), lax.axis_index("shard")
    return role_of(rep, shard), rep >> 1, shard & 1, (shard >> 1) & 3, shard >> 3


def in_half(step, group):
    role, x, y, z, _ = place()
    (dy, dx), k = step
    first = role == 0
    return (
        jnp.where(first, y ^ dy, group >> 1), jnp.where(first, x ^ dx, group & 1), jnp.where(first, group, z ^ k),
    )


def group_of(step, line_role):
    role, x, y, z, _ = place()
    (dy, dx), k = step
    return jnp.where(role == line_role, z ^ k, 2 * (y ^ dy) + (x ^ dx))


def block(index, size):
    return pl.ds(pl.multiple_of(index * size, size), size)


def load_kernel(cots_ref, away, sem):
    copy = pltpu.make_async_copy(cots_ref.at[:, block(1 - place()[0], away.shape[1])], away, sem)
    copy.start()
    copy.wait()


def away_kernel(acts, cots, out, turned):
    turned[...] = acts[...].T
    for i in range(out.shape[1] // CHUNK):
        at = slice(i * CHUNK, (i + 1) * CHUNK)
        out[:, at] = jnp.dot(turned[...], cots[:, at], preferred_element_type=F32).astype(BF16)


def kept_kernel(turned, cots_ref, out, cots, sems):
    role = place()[0]
    count = cots.shape[0]
    copies = []
    for i in range(count):
        source = cots_ref.at[:, block(role * count + i, CHUNK)]
        copies.append(pltpu.make_async_copy(source, cots.at[i], sems.at[i]))
        copies[-1].start()
    for i in range(count):
        copies[i].wait()
        at = slice(i * CHUNK, (i + 1) * CHUNK)
        out[:, at] = jnp.dot(turned[...], cots[i], preferred_element_type=F32)


def wide_kernel(rows, kept, came, own, *pieces):
    quarter = own.shape[1]
    count = own.shape[0] // (4 * rows)
    for step, out in zip((STAY,) + STEPS, (own,) + pieces):
        for group in range(4):
            y, x, z = in_half(step, group)
            cols = block(x, quarter)
            for w in range(count):
                at = block(8 * w + 2 * z + y, rows)
                total = kept[at, cols] + came[at, cols].astype(F32)
                to = (group * count + w) * rows
                out[to:to + rows, :] = total.astype(out.dtype)


def narrow_kernel(kept, *refs):
    came, (own, *pieces) = refs[:len(STEPS)], refs[len(STEPS):]
    for step, out in zip((STAY,) + STEPS, [own] + pieces):
        at = block(group_of(step, 0), out.shape[0])
        total = kept[at, :]
        for ref in came:
            total += ref[at, :].astype(F32)
        out[...] = total.astype(out.dtype)


def rest_kernel(kept, *refs):
    came, outs = refs[:len(STEPS)], refs[len(STEPS):]
    w = place()[4]
    for k, out in enumerate(outs):
        at = block(w ^ k, out.shape[0])
        total = kept[at, :]
        for ref in came:
            total += ref[at, :].astype(F32)
        out[...] = total.astype(out.dtype)


def update_kernel(w, m, v, own, *refs):
    pieces, (new_w, grad) = refs[:-2], refs[-2:]
    role, x, _, _, _ = place()
    total = own[...]
    for ref in pieces:
        total += ref[...].astype(F32)
    grad[...] = total.astype(BF16)
    at = block(role * 2 + x, total.shape[1])
    new_m, new_v = adamw_moments(m[:, at], v[:, at], total)
    new_w[...] = adamw_weight(w[:, at], new_m, new_v)


def put(outs, at, value):
    for out in outs:
        out[at, :] = value


def put(outs, at, value):
    for out in outs:
        out[at, :] = value


def rest_back_kernel(grad, *refs):
    pieces, (*outs, last) = refs[:-1 - len(STEPS)], refs[-1 - len(STEPS):]
    w = place()[4]
    rows = grad.shape[0]
    for k, ref in enumerate(pieces):
        put(outs, block(w ^ k, rows), ref[...])
    last[...] = grad[...]


def narrow_back_kernel(own, *refs):
    parts, outs = (own,) + refs[:len(STEPS)], refs[-len(STEPS):]
    for step, ref in zip((STAY,) + STEPS, parts):
        put(outs, block(group_of(step, 1), own.shape[0]), ref[...])


def half_blocks(sibling, parts, out):
    role, x, y, z, _ = place()
    square = (role == 1) != sibling
    size, quarter = parts[0].shape
    rows = out.shape[0] // lax.axis_size("shard")
    count = size // (4 * rows)
    for ((dy, dx), k), ref in zip((STAY,) + STEPS, parts):
        for group in range(4):
            to_y = jnp.where(square, y ^ dy, group >> 1)
            to_x = jnp.where(square, x ^ dx, group & 1)
            to_z = jnp.where(square, group, z ^ k)
            for w in range(count):
                at = (group * count + w) * rows
                out[block(8 * w + 2 * to_z + to_y, rows), block(to_x, quarter)] = ref[at:at + rows, :]


def pack_kernel(*refs):
    *parts, out = refs
    at = 0
    for ref in parts:
        out[at:at + ref.shape[0], :] = ref[...]
        at += ref.shape[0]


def write_half(sibling, parts, out, half, sem):
    half_blocks(sibling, parts, half)
    copy = pltpu.make_async_copy(half, out.at[:, block(place()[0] ^ sibling, half.shape[1])], sem)
    copy.start()
    return copy


def write_own_kernel(m, v, grad, far_grad, early, *refs):
    parts, (w_out, m_out, v_out, half, sem, new_m, new_v, sems) = refs[:1 + len(STEPS)], refs[1 + len(STEPS):]
    copies = [write_half(0, parts, w_out, half, sem)]
    role, x, _, _, _ = place()
    rows = grad.shape[0]
    tail = early.shape[0] - 2 * rows
    grads = [grad, far_grad] + [early.at[pl.ds(tail + i * rows, rows), :] for i in range(2)]
    for i, ref in enumerate(grads):
        cols = block(2 * (role ^ (i >> 1)) + (x ^ (i & 1)), grad.shape[1])
        new_m[:, cols], new_v[:, cols] = adamw_moments(m[:, cols], v[:, cols], ref[...].astype(F32))
    for i, (source, out) in enumerate(((new_m, m_out), (new_v, v_out))):
        copies.append(pltpu.make_async_copy(source, out, sems.at[i]))
        copies[-1].start()
    for copy in copies:
        copy.wait()


def write_other_kernel(early, late, _, out, half, sem):
    size = late.shape[0] // 2
    parts = [ref.at[pl.ds(i * size, size), :] for ref in (early, late) for i in range(2)]
    write_half(1, parts, out, half, sem).wait()


def body(hidden_acts, out_cotangent, weight, first_moment, second_moment):
    rows, width = weight.shape
    tokens, all_rows = hidden_acts.shape
    half, quarter = width // 2, width // 4
    rest = lax.axis_size("shard") // 8
    wide_rows, narrow_rows = all_rows // 2, all_rows // 8

    away_cots = call(
        load_kernel, [shape((tokens, half), BF16)], out_cotangent,
        far_in=(0,), scratch=[pltpu.SemaphoreType.DMA], limit=LOAD_LIMIT,
    )[0]
    away, turned = call(
        away_kernel, [shape((all_rows, half), BF16), shape((all_rows, tokens), BF16)], hidden_acts, away_cots,
    )
    came = to_sibling(away)
    count = half // CHUNK
    kept = call(
        kept_kernel, [shape((all_rows, half), F32)], turned, out_cotangent, far_in=(1,), limit=KEPT_LIMIT,
        scratch=[pltpu.VMEM((count, tokens, CHUNK), BF16), pltpu.SemaphoreType.DMA((count,))],
    )[0]

    def split(kernel, size, parts, *args):
        kept, sent = shape((size, quarter), F32), shape((size, quarter), BF16)
        return call(kernel, [kept] + [sent] * (parts - 1), *args)

    own, *pieces = split(functools.partial(wide_kernel, rows), wide_rows, 4, kept, came)
    came = [stage(piece, step, 0) for step, piece in zip(STEPS, pieces)]
    own, *pieces = split(narrow_kernel, narrow_rows, 4, own, *came)
    came = [stage(piece, step, 1) for step, piece in zip(STEPS, pieces)]
    if rest > 1:
        own, *pieces = split(rest_kernel, rows, rest, own, *came)
        came = [along_rest(piece, k + 1) for k, piece in enumerate(pieces)]
    new_w, grad = call(
        update_kernel, [shape((rows, quarter), BF16)] * 2, weight, first_moment, second_moment, own, *came,
    )

    pieces = [along_rest(new_w, k) for k in range(1, rest)]
    *parts, far_grad = call(
        rest_back_kernel,
        [shape((narrow_rows, quarter), BF16)] * len(STEPS) + [shape((rows, quarter), BF16)], grad, new_w, *pieces,
    )
    came = [stage(part, step, 0) for step, part in zip(STEPS, parts)]
    far_grad = along_x(far_grad)
    parts = call(
        narrow_back_kernel, [shape((wide_rows, quarter), BF16)] * len(STEPS), parts[-1], *came, far_grad,
    )
    came = [stage(part, step, 1) for step, part in zip(STEPS, parts)]

    def swapped(size, *args):
        return to_sibling(call(pack_kernel, [shape((size, quarter), BF16)], *args)[0])

    early = swapped(2 * wide_rows + 2 * rows, parts[-1], came[0], grad, far_grad)
    late = swapped(2 * wide_rows, came[1], came[2])
    new_w = [shape((all_rows, width), BF16)]
    moments = [shape((rows, width), F32)] * 2
    scratch = [pltpu.VMEM((all_rows, half), BF16), pltpu.SemaphoreType.DMA]
    written, new_m, new_v = call(
        write_own_kernel, new_w + moments, first_moment, second_moment, grad, far_grad, early, parts[-1], *came,
        far_out=3, scratch=scratch + [pltpu.VMEM((rows, width), F32)] * 2 + [pltpu.SemaphoreType.DMA((2,))],
    )
    written = call(
        write_other_kernel, new_w, early, late, written, far_in=(2,), far_out=1, scratch=scratch, aliases={2: 0},
    )[0]
    return written, new_m, new_v


def solution(mesh):
    return jax.shard_map(
        body,
        mesh=mesh,
        in_specs=(
            P(("rep", "shard"), None),
            P(("rep", "shard"), None),
            P("shard", None),
            P("shard", None),
            P("shard", None),
        ),
        out_specs=(P(), P("shard", None), P("shard", None)),
        check_vma=False,
    )
```
